128 devices in a mesh: wide: 16 (over z_hi, y, core), narrow: 8 (over z_lo, x).
Axes of the slice: x: 4, y: 4, z: 4 (z_hi: 2, z_lo: 2; z = z_hi * 2 + z_lo), core: 2. Of those that a mesh axis runs over, the one named last changes fastest.
Arguments:
- field: bfloat16 [32, 128, 128, 128], P(None, 'wide', 'narrow'), may hold values from -6 to 6
- spectral_weight: bfloat16 [48, 48, 48, 2048], P('wide', 'narrow'), may hold values from -3 to 3
- pointwise_weight: bfloat16 [32, 32], replicated, may hold values from -1 to 1
- cotangent: bfloat16 [32, 128, 128, 128], P(None, 'wide', 'narrow'), may hold values from -6 to 6
Outputs:
- activation: bfloat16 [32, 128, 128, 128], P(None, 'wide', 'narrow')
- field_grad: bfloat16 [32, 128, 128, 128], P(None, 'wide', 'narrow')
- weight_grad: bfloat16 [48, 48, 48, 2048], P('wide', 'narrow')
The draws below stay inside these ranges and needn't reach their ends.
All inputs are finite; a program needn't handle non-finite values.
Results may differ from the reference program's by a relative error of at most 0.025.
Values may be sent and summed in bfloat16 or wider, within the bound.
A program may use at most 128 MiB of HBM per device.

```python
import jax
import jax.numpy as jnp
from jax import lax

NX = 128
NY = 128
NZ = 128
C = 32
KX = 48
KY = 48
KZ = 48


def levels(rng, dims, shards, least, largest):
    gain, own = 1.0, jax.random.fold_in(rng, 6)
    for position, blocks in shards:
        draws = jnp.exp(jax.random.uniform(jax.random.fold_in(own, position), (blocks,), jnp.float32, least / len(shards), largest / len(shards)))
        gain = gain * jnp.repeat(draws, dims[position] // blocks).reshape([-1 if axis == position else 1 for axis in range(len(dims))])
    return gain


def centred(own_key, shape, width, bound, cuts=(), kind=jnp.bfloat16):
    array = jax.random.normal(own_key, shape, jnp.float32) * width
    if len(cuts) > 0:
        array = levels(own_key, shape, cuts, -0.22, 0.18) * array
    return jnp.clip(array, min=-bound, max=bound).astype(kind)


def setup_inputs(seed: int = 0) -> dict:
    streams_of = jax.random.split(jax.random.key(seed), 5)
    field = centred(streams_of[0], (C, NX, NY, NZ), 1.0, 6.0, ((1, 16), (2, 8)))
    spectral_weight = centred(streams_of[1], (KZ, KX, KY, 2 * C * C), 0.5, 3.0, ((0, 16), (1, 8)))
    pointwise_weight = centred(streams_of[2], (C, C), C ** -0.5, 1.0)
    cotangent = centred(streams_of[3], (C, NX, NY, NZ), 1.0, 6.0, ((1, 16), (2, 8)))
    return {"field": field, "spectral_weight": spectral_weight, "pointwise_weight": pointwise_weight, "cotangent": cotangent}


def twiddles(extent, kept_count, two_sided):
    positions = jnp.arange(kept_count, dtype=jnp.int32)
    if two_sided:
        frequency = jnp.where(positions < kept_count // 2, positions, positions + (extent - kept_count))
    else:
        frequency = positions
    places = jnp.arange(extent, dtype=jnp.int32)
    phases = places[:, None] * frequency[None, :] % extent
    angles = phases.astype(jnp.float32) * (2.0 * jnp.pi / extent)
    return (jnp.cos(angles).astype(jnp.bfloat16), jnp.sin(angles).astype(jnp.bfloat16))

def product(pattern, operand, table_in):
    return jnp.einsum(pattern, operand.astype(jnp.float32), table_in.astype(jnp.float32), precision=lax.Precision.HIGHEST)

def activate(combined):
    return jax.nn.gelu(combined, approximate=True)

def forward_modes(grid_data, tables):
    (cosx, sinx), (cosy, siny), (cosz, sinz) = tables
    depth_real = product('xyz,zk->xyk', grid_data, cosz).astype(jnp.bfloat16)
    depth_imag = (-product('xyz,zk->xyk', grid_data, sinz)).astype(jnp.bfloat16)
    cross_real = product('xyk,xq->qyk', depth_real, cosx) + product('xyk,xq->qyk', depth_imag, sinx)
    cross_imag = product('xyk,xq->qyk', depth_imag, cosx) - product('xyk,xq->qyk', depth_real, sinx)
    mode_real = product('qyk,yp->kqp', cross_real, cosy) + product('qyk,yp->kqp', cross_imag, siny)
    mode_imag = product('qyk,yp->kqp', cross_imag, cosy) - product('qyk,yp->kqp', cross_real, siny)
    return jnp.stack([mode_real, mode_imag]).astype(jnp.bfloat16)

def inverse_field(mode_data, tables):
    (cosx, sinx), (cosy, siny), (cosz, sinz) = tables
    mode_real, mode_imag = (mode_data[0], mode_data[1])
    cross_real = product('kqp,yp->kqy', mode_real, cosy) - product('kqp,yp->kqy', mode_imag, siny)
    cross_imag = product('kqp,yp->kqy', mode_real, siny) + product('kqp,yp->kqy', mode_imag, cosy)
    back_real = (product('kqy,xq->xyk', cross_real, cosx) - product('kqy,xq->xyk', cross_imag, sinx)).astype(jnp.bfloat16)
    back_imag = (product('kqy,xq->xyk', cross_real, sinx) + product('kqy,xq->xyk', cross_imag, cosx)).astype(jnp.bfloat16)
    return product('xyk,zk->xyz', back_real, cosz) - product('xyk,zk->xyz', back_imag, sinz)

def reference(field, spectral_weight, pointwise_weight, cotangent):
    tables = (twiddles(NX, KX, True), twiddles(NY, KY, True), twiddles(NZ, KZ, False))
    kz_index = jnp.arange(KZ, dtype=jnp.int32)
    scale = jnp.where(kz_index == 0, 1.0, 2.0).astype(jnp.float32) / float(NX * NY * NZ)
    weights = spectral_weight.reshape(KZ, KX, KY, 2, C, C)
    spectrum = lax.map(lambda grid_data: forward_modes(grid_data, tables), field)
    spectrum_modes = spectrum.transpose(2, 1, 3, 4, 0)

    def mixing(inputs):
        mode_data, weight_block, factor = inputs
        weight_real, weight_imag = (weight_block[:, :, 0], weight_block[:, :, 1])
        mixed_real = product('qpc,qpco->qpo', mode_data[0], weight_real) - product('qpc,qpco->qpo', mode_data[1], weight_imag)
        mixed_imag = product('qpc,qpco->qpo', mode_data[0], weight_imag) + product('qpc,qpco->qpo', mode_data[1], weight_real)
        return (jnp.stack([mixed_real, mixed_imag]) * factor).astype(jnp.bfloat16)
    mixed_modes = lax.map(mixing, (spectrum_modes, weights, scale)).transpose(4, 1, 0, 2, 3)
    nearby = jnp.dot(pointwise_weight.T, field.reshape(C, -1), preferred_element_type=jnp.float32).reshape(C, NX, NY, NZ)

    def respond(inputs):
        mode_data, near_term, upstream = inputs
        combined = inverse_field(mode_data, tables) + near_term
        output_value, pullback = jax.vjp(activate, combined)
        slope_grad = pullback(upstream.astype(jnp.float32))[0]
        return (output_value.astype(jnp.bfloat16), slope_grad.astype(jnp.bfloat16))
    activation, slope = lax.map(respond, (mixed_modes, nearby, cotangent))
    slope_spectrum = lax.map(lambda grid_data: forward_modes(grid_data, tables), slope).transpose(2, 1, 3, 4, 0)

    def adjoint(inputs):
        mode_data, slope_data, weight_block, factor = inputs
        spec_real = mode_data[0].astype(jnp.float32)
        spec_imag = mode_data[1].astype(jnp.float32)
        grad_real_in = slope_data[0].astype(jnp.float32)
        grad_imag_in = slope_data[1].astype(jnp.float32)
        grad_real = (spec_real[..., :, None] * grad_real_in[..., None, :] + spec_imag[..., :, None] * grad_imag_in[..., None, :]) * factor
        grad_imag = (spec_real[..., :, None] * grad_imag_in[..., None, :] - spec_imag[..., :, None] * grad_real_in[..., None, :]) * factor
        weight_real, weight_imag = (weight_block[:, :, 0], weight_block[:, :, 1])
        back_real = (product('qpco,qpo->qpc', weight_real, slope_data[0]) + product('qpco,qpo->qpc', weight_imag, slope_data[1])) * factor
        back_imag = (product('qpco,qpo->qpc', weight_real, slope_data[1]) - product('qpco,qpo->qpc', weight_imag, slope_data[0])) * factor
        return (jnp.stack([grad_real, grad_imag], axis=2).astype(jnp.bfloat16), jnp.stack([back_real, back_imag]).astype(jnp.bfloat16))
    weight_blocks, adjoint_modes = lax.map(adjoint, (spectrum_modes, slope_spectrum, weights, scale))
    weight_grad = weight_blocks.reshape(KZ, KX, KY, 2 * C * C)
    adjoint_modes = adjoint_modes.transpose(4, 1, 0, 2, 3)
    near_back = jnp.dot(pointwise_weight, slope.reshape(C, -1), preferred_element_type=jnp.float32).reshape(C, NX, NY, NZ)

    def gradient(inputs):
        mode_data, near_term = inputs
        return (inverse_field(mode_data, tables) + near_term).astype(jnp.bfloat16)
    field_grad = lax.map(gradient, (adjoint_modes, near_back))
    return (activation, field_grad, weight_grad)
```

```python
import functools

import jax
import jax.numpy as jnp
import ml_dtypes
import numpy as np
from jax import lax
from jax.experimental import pallas as pl
from jax.experimental.pallas import tpu as pltpu
from jax.sharding import PartitionSpec as P

C = 32
XL = 8
YL = 16
KXL = 6
KL = 3
NZ = 128
MESH = pl.DeviceIdType.MESH
F32 = jnp.float32
BF16 = jnp.bfloat16


def angles(extent, kept, two_sided):
    positions = np.arange(kept)
    frequency = (
        np.where(positions < kept // 2, positions, positions + extent - kept)
        if two_sided
        else positions
    )
    phases = np.arange(extent)[:, None] * frequency[None, :] % extent
    theta = 2.0 * np.pi * phases / extent
    rounded = lambda t: t.astype(np.float32).astype(ml_dtypes.bfloat16).astype(np.float32)
    return rounded(np.cos(theta)), rounded(np.sin(theta))


def tables(wide, narrow, ky):
    nx, ny, kx, kz = XL * wide, YL * narrow, KXL * narrow, KL * wide
    cx, sx = angles(nx, kx, True)
    cy, sy = angles(ny, ky, True)
    cz, sz = angles(NZ, kz, False)
    z_rows = np.stack([cz, -sz], axis=-1).reshape(NZ, wide, KL, 2)
    z_fwd = z_rows.transpose(2, 1, 3, 0).reshape(KL * wide * 2, NZ)
    z_inv = z_fwd
    fwd = lambda c, s: np.stack([np.stack([c, s]), np.stack([-s, c])])
    inv = lambda c, s: np.stack([np.stack([c, -s]), np.stack([s, c])])
    fx = fwd(cx, sx).reshape(2, 2, wide, XL, narrow, KXL)
    x_fwd = fx.transpose(5, 4, 0, 2, 1, 3).reshape(KXL * narrow * 2, wide * 2 * XL)
    ix = inv(cx, sx).reshape(2, 2, wide, XL, narrow, KXL)
    x_inv = ix.transpose(2, 0, 3, 5, 4, 1).reshape(wide * 2 * XL, KXL * narrow * 2)
    fy = fwd(cy, sy).reshape(2, 2, narrow, YL, ky)
    y_fwd = fy.transpose(0, 4, 2, 1, 3).reshape(2 * ky, narrow * 2 * YL)
    iy = inv(cy, sy).reshape(2, 2, narrow, YL, ky)
    y_inv = iy.transpose(2, 0, 3, 1, 4).reshape(narrow * 2 * YL, 2 * ky)
    return [t.astype(ml_dtypes.bfloat16) for t in (z_fwd, z_inv, x_fwd, x_inv, y_fwd, y_inv)]


def dot(a, b, dims=((1,), (0,))):
    return lax.dot_general(a, b, (dims, ((), ())), preferred_element_type=F32)


def ones_where(condition):
    return jnp.where(condition, 1.0, 0.0).astype(BF16)


def kernel(
    wide, narrow, ky, total,
    field, cot_hbm, weight_hbm, pw, z_fwd, z_inv, x_fwd, x_inv, y_fwd, y_inv,
    act_hbm, fgrad_hbm, wgrad_hbm,
    cot, weight, act, fgrad, wgrad,
    zs, zi, near, slope, spec, mix, t1, t2,
    perm, perm_t, pw_fwd, pw_back, repeat, tile, group_sum,
    ws, wr, ns, nr,
    ws_sem, wr_sem, ns_sem, nr_sem, load_sem, store_sem,
):
    w = lax.axis_index("wide")
    n = lax.axis_index("narrow")
    cells = C * YL
    pairs = 2 * narrow
    kk = KL * wide * 2

    load_cot = pltpu.make_async_copy(cot_hbm, cot, load_sem.at[0])
    load_weight = pltpu.make_async_copy(weight_hbm, weight, load_sem.at[1])
    load_cot.start()
    load_weight.start()

    barrier = pltpu.get_barrier_semaphore()

    @pl.loop(1, wide)
    def _(d):
        pl.semaphore_signal(
            barrier, inc=1, device_id={"wide": lax.rem(w + d, wide)}, device_id_type=MESH
        )

    @pl.loop(1, narrow)
    def _(d):
        pl.semaphore_signal(
            barrier, inc=1, device_id={"narrow": lax.rem(n + d, narrow)}, device_id_type=MESH
        )

    row = lax.broadcasted_iota(jnp.int32, (cells, cells), 0)
    col = lax.broadcasted_iota(jnp.int32, (cells, cells), 1)
    perm[...] = ones_where(((row & 15) == (col >> 5)) & ((row >> 4) == (col & 31)))

    lane = lax.broadcasted_iota(jnp.int32, (1, 128), 1) >> 5

    def depth(x, b, block):
        out = dot(z_fwd[...], block, ((1,), (1,)))
        zs[b, pl.ds(x, kk, stride=XL), :] = out

    def send_wide(a, j):
        wr[a, j, w] = ws[a, j, w]

        @pl.loop(1, wide)
        def _(d):
            to = lax.rem(w + d, wide)
            pltpu.make_async_remote_copy(
                src_ref=ws.at[a, j, to],
                dst_ref=wr.at[a, j, w],
                send_sem=ws_sem.at[a, j],
                recv_sem=wr_sem.at[a, j],
                device_id={"wide": to},
                device_id_type=MESH,
            ).start()

    def send_narrow(a, j):
        nr[a, j, n] = ns[a, j, n]

        @pl.loop(1, narrow)
        def _(d):
            to = lax.rem(n + d, narrow)
            pltpu.make_async_remote_copy(
                src_ref=ns.at[a, j, to],
                dst_ref=nr.at[a, j, n],
                send_sem=ns_sem.at[a, j],
                recv_sem=nr_sem.at[a, j],
                device_id={"narrow": to},
                device_id_type=MESH,
            ).start()

    def wait_all(buffer, a, j, sem, count):
        ref = buffer.at[a, j, pl.ds(0, count - 1)]
        pltpu.make_async_copy(ref, ref, sem.at[a, j]).wait()

    def depth_out(a, j):
        rows = pl.ds(j * wide * 16, wide * 16)
        block = jnp.concatenate([zs[b, rows, :].astype(BF16) for b in range(4)], axis=1)
        out = dot(block, perm[...]).astype(BF16)
        ws[a, j] = out.reshape(wide, 16, cells)
        send_wide(a, j)

    def x_forward(a, j):
        wait_all(wr, a, j, wr_sem, wide)
        out = dot(x_fwd[...], wr[a, j].reshape(wide * 16, cells))
        for y in range(YL):
            yb, g = y // 4, y % 4
            for lb in range(2):
                acc = None
                for s in range(4 if lb == 0 else 2):
                    kx = 4 * lb + s
                    piece = out[kx * pairs : (kx + 1) * pairs, yb * 128 : (yb + 1) * 128]
                    if s != g:
                        piece = pltpu.roll(piece, ((s - g) * 32) % 128, 1)
                    acc = piece if acc is None else jnp.where(lane == s, piece, acc)
                t1[lb, pl.ds(y, pairs, stride=YL), :] = acc
        for lb in range(2):
            ns[a, j, :, :, lb * 128 : (lb + 1) * 128] = (
                t1[lb].astype(BF16).reshape(narrow, 2 * YL, 128)
            )
        send_narrow(a, j)

    def y_forward(a, j, which):
        wait_all(nr, a, j, nr_sem, narrow)
        out = dot(y_fwd[...], nr[a, j].reshape(narrow * 2 * YL, 256)).astype(BF16)
        for lb in range(2):
            spec[which, j, lb] = out[:, lb * 128 : (lb + 1) * 128]

    def scale(j):
        return jnp.where(w * KL + j == 0, 1.0, 2.0).astype(F32) / total

    def channels_first(which, j, kx):
        rolled = pltpu.roll(
            spec[which, j, kx // 4].astype(F32), lax.rem(128 - 32 * lax.rem(kx, 4), 128), 1
        )
        return rolled.astype(BF16)

    def place(kx, value):
        lb = kx // 4
        mix[lb] = jnp.where(lane == lax.rem(kx, 4), value, mix[lb])

    def mix_forward(j):
        @pl.loop(0, KXL)
        def _(kx):
            spectrum = channels_first(0, j, kx)
            acc_r = jnp.zeros((ky, 128), F32)
            acc_i = jnp.zeros((ky, 128), F32)
            for b in range(4):
                lanes = slice(b * 256, (b + 1) * 256)
                rep = dot(spectrum, repeat[:, lanes])
                rep_r, rep_i = rep[:ky], rep[ky:]
                w_r = weight[j, kx, :, b * 256 : (b + 1) * 256].astype(F32)
                w_i = weight[j, kx, :, 1024 + b * 256 : 1024 + (b + 1) * 256].astype(F32)
                p_r = rep_r * w_r - rep_i * w_i
                p_i = rep_r * w_i + rep_i * w_r
                acc_r = acc_r + (p_r[:, :128] + p_r[:, 128:])
                acc_i = acc_i + (p_i[:, :128] + p_i[:, 128:])
            acc = jnp.concatenate([acc_r, acc_i], axis=0) * scale(j)
            acc = acc + pltpu.roll(acc, 64, 1)
            acc = acc + pltpu.roll(acc, 32, 1)
            place(kx, acc)

    def mix_back(j):
        @pl.loop(0, KXL)
        def _(kx):
            tiled = dot(channels_first(1, j, kx), tile[...])
            g_r = jnp.concatenate([tiled[:ky]] * 2, axis=1)
            g_i = jnp.concatenate([tiled[ky:]] * 2, axis=1)
            acc = jnp.zeros((2 * ky, 128), F32)
            for b in range(4):
                w_r = weight[j, kx, :, b * 256 : (b + 1) * 256].astype(F32)
                w_i = weight[j, kx, :, 1024 + b * 256 : 1024 + (b + 1) * 256].astype(F32)
                a_r = (w_r * g_r + w_i * g_i).astype(BF16)
                a_i = (w_r * g_i - w_i * g_r).astype(BF16)
                acc = acc + dot(
                    jnp.concatenate([a_r, a_i], axis=0), group_sum[b * 256 : (b + 1) * 256, :]
                )
            place(kx, acc * scale(j))

    def weight_gradient(j):
        @pl.loop(0, KXL)
        def _(kx):
            spectrum = channels_first(0, j, kx)
            tiled = dot(channels_first(1, j, kx), tile[...]) * scale(j)
            g_r = jnp.concatenate([tiled[:ky]] * 2, axis=1)
            g_i = jnp.concatenate([tiled[ky:]] * 2, axis=1)
            for b in range(4):
                rep = dot(spectrum, repeat[:, b * 256 : (b + 1) * 256])
                rep_r, rep_i = rep[:ky], rep[ky:]
                wgrad[j, kx, :, b * 256 : (b + 1) * 256] = (rep_r * g_r + rep_i * g_i).astype(BF16)
                wgrad[j, kx, :, 1024 + b * 256 : 1024 + (b + 1) * 256] = (
                    rep_r * g_i - rep_i * g_r
                ).astype(BF16)

    def y_inverse(a, j):
        modes = jnp.concatenate([mix[0].astype(BF16), mix[1].astype(BF16)], axis=1)
        out = dot(y_inv[...], modes).astype(BF16)
        ns[a, j] = out.reshape(narrow, 2 * YL, 256)
        send_narrow(a, j)

    def x_inverse(a, j, aw):
        wait_all(nr, a, j, nr_sem, narrow)
        for lb in range(2):
            t1[lb] = (
                nr[a, j, :, :, lb * 128 : (lb + 1) * 128]
                .reshape(narrow * 2 * YL, 128)
                .astype(F32)
            )
        for yb in range(4):
            for lb in range(2):
                loaded = [t1[lb, pl.ds(4 * yb + g, pairs, stride=YL), :] for g in range(4)]
                for s in range(4 if lb == 0 else 2):
                    kx = 4 * lb + s
                    acc = None
                    for g in range(4):
                        piece = loaded[g]
                        if s != g:
                            piece = pltpu.roll(piece, ((g - s) * 32) % 128, 1)
                        acc = piece if acc is None else jnp.where(lane == g, piece, acc)
                    t2[kx * pairs : (kx + 1) * pairs, yb * 128 : (yb + 1) * 128] = acc.astype(BF16)
        out = dot(x_inv[...], t2[...]).astype(BF16)
        ws[aw, j] = out.reshape(wide, 16, cells)
        send_wide(aw, j)

    def depth_in(a, j):
        wait_all(wr, a, j, wr_sem, wide)
        out = dot(wr[a, j].reshape(wide * 16, cells), perm_t[...])
        for b in range(4):
            zi[b, pl.ds(j * wide * 16, wide * 16), :] = out[:, b * 128 : (b + 1) * 128]

    def depth_inverse(x, b):
        block = zi[b, pl.ds(x, kk, stride=XL), :].astype(BF16)
        return dot(block, z_inv[...], ((0,), (0,)))

    def pointwise(matrix, source):
        @pl.loop(0, XL)
        def _(x):
            near[x] = dot(matrix[...], source[:, x].reshape(cells, NZ))

    for x in range(XL):
        plane = field[:, x].reshape(cells, NZ)
        for b in range(4):
            depth(x, b, plane[b * 128 : (b + 1) * 128])

    pl.semaphore_wait(barrier, wide + narrow - 2)

    for j in range(KL):
        depth_out(0, j)

    perm_t[...] = ones_where(((row >> 5) == (col & 15)) & ((row & 31) == (col >> 4)))
    spread_row = lax.broadcasted_iota(jnp.int32, (cells, C), 0)
    spread_col = lax.broadcasted_iota(jnp.int32, (cells, C), 1)
    spread = ones_where((spread_row >> 4) == spread_col)
    same_y = (row & 15) == (col & 15)
    back = dot(dot(spread, pw[...]).astype(BF16), spread, ((1,), (1,)))
    pw_back[...] = jnp.where(same_y, back, 0.0).astype(BF16)
    ahead = dot(dot(spread, pw[...], ((1,), (1,))).astype(BF16), spread, ((1,), (1,)))
    pw_fwd[...] = jnp.where(same_y, ahead, 0.0).astype(BF16)
    r_row = lax.broadcasted_iota(jnp.int32, (128, 1024), 0)
    r_col = lax.broadcasted_iota(jnp.int32, (128, 1024), 1)
    repeat[...] = ones_where(r_row == (r_col >> 5))
    t_row = lax.broadcasted_iota(jnp.int32, (128, 128), 0)
    t_col = lax.broadcasted_iota(jnp.int32, (128, 128), 1)
    tile[...] = ones_where(t_row == (t_col & 31))
    g_row = lax.broadcasted_iota(jnp.int32, (1024, 128), 0)
    g_col = lax.broadcasted_iota(jnp.int32, (1024, 128), 1)
    group_sum[...] = ones_where((g_row >> 5) == (g_col & 31))
    mix[...] = jnp.zeros_like(mix)
    pointwise(pw_fwd, field)
    load_weight.wait()

    for j in range(KL):
        x_forward(0, j)
    for j in range(KL):
        y_forward(0, j, 0)
        mix_forward(j)
        y_inverse(1, j)
    for j in range(KL):
        x_inverse(1, j, 1)
    load_cot.wait()
    for j in range(KL):
        depth_in(1, j)

    root = 0.7978845608028654

    @pl.loop(0, 4)
    def _(b):
        rows = pl.ds(pl.multiple_of(b * 128, 128), 128)
        group = pl.ds(b * 8, 8)
        for x in range(XL):
            t = depth_inverse(x, b) + near[x, rows, :]
            square = t * t
            th = jnp.tanh(root * t * (1.0 + 0.044715 * square))
            half = 0.5 + 0.5 * th
            act[group, x] = (t * half).astype(BF16).reshape(8, YL, NZ)
            grad = half + (0.5 * root) * t * (1.0 - th * th) * (1.0 + 0.134145 * square)
            up = cot[group, x].reshape(128, NZ).astype(F32)
            block = (up * grad).astype(BF16)
            slope[group, x] = block.reshape(8, YL, NZ)
            depth(x, b, block)

    store_act = pltpu.make_async_copy(act, act_hbm, store_sem.at[0])
    store_act.start()

    for j in range(KL):
        depth_out(2, j)
    pointwise(pw_back, slope)
    for j in range(KL):
        x_forward(2, j)
    for j in range(KL):
        y_forward(2, j, 1)
        mix_back(j)
        y_inverse(3, j)
    for j in range(KL):
        x_inverse(3, j, 3)
    for j in range(KL):
        weight_gradient(j)
    store_wgrad = pltpu.make_async_copy(wgrad, wgrad_hbm, store_sem.at[1])
    store_wgrad.start()
    for j in range(KL):
        depth_in(3, j)

    @pl.loop(0, 4)
    def _(b):
        rows = pl.ds(pl.multiple_of(b * 128, 128), 128)
        group = pl.ds(b * 8, 8)
        for x in range(XL):
            t = depth_inverse(x, b) + near[x, rows, :]
            fgrad[group, x] = t.astype(BF16).reshape(8, YL, NZ)

    store_fgrad = pltpu.make_async_copy(fgrad, fgrad_hbm, store_sem.at[2])
    store_fgrad.start()

    for a in range(4):
        for j in range(KL):
            wait_all(ws, a, j, ws_sem, wide)
            wait_all(ns, a, j, ns_sem, narrow)
    store_act.wait()
    store_wgrad.wait()
    store_fgrad.wait()


def on_device(wide, narrow, field, weight, pw, cot):
    ky = weight.shape[2]
    total = float(XL * wide * YL * narrow * NZ)
    consts = tables(wide, narrow, ky)
    cells = C * YL
    kk = KL * wide * 2
    vmem = pl.BlockSpec(memory_space=pltpu.VMEM)
    hbm = pl.BlockSpec(memory_space=pl.ANY)
    act, fgrad, wgrad = pl.pallas_call(
        functools.partial(kernel, wide, narrow, ky, total),
        out_shape=(
            jax.ShapeDtypeStruct(field.shape, BF16),
            jax.ShapeDtypeStruct(field.shape, BF16),
            jax.ShapeDtypeStruct(weight.shape, BF16),
        ),
        in_specs=[vmem, hbm, hbm, vmem] + [vmem] * 6,
        out_specs=(hbm, hbm, hbm),
        scratch_shapes=[
            pltpu.VMEM(cot.shape, BF16),
            pltpu.VMEM(weight.shape, BF16),
            pltpu.VMEM(field.shape, BF16),
            pltpu.VMEM(field.shape, BF16),
            pltpu.VMEM(weight.shape, BF16),
            pltpu.VMEM((4, kk * XL, 128), F32),
            pltpu.VMEM((4, kk * XL, 128), F32),
            pltpu.VMEM((XL, cells, NZ), F32),
            pltpu.VMEM(field.shape, BF16),
            pltpu.VMEM((2, KL, 2, 2 * ky, 128), BF16),
            pltpu.VMEM((2, 2 * ky, 128), F32),
            pltpu.VMEM((2, narrow * 2 * YL, 128), F32),
            pltpu.VMEM((KXL * narrow * 2, cells), BF16),
            pltpu.VMEM((cells, cells), BF16),
            pltpu.VMEM((cells, cells), BF16),
            pltpu.VMEM((cells, cells), BF16),
            pltpu.VMEM((cells, cells), BF16),
            pltpu.VMEM((128, 1024), BF16),
            pltpu.VMEM((128, 128), BF16),
            pltpu.VMEM((1024, 128), BF16),
            pltpu.VMEM((4, KL, wide, 2 * XL, cells), BF16),
            pltpu.VMEM((4, KL, wide, 2 * XL, cells), BF16),
            pltpu.VMEM((4, KL, narrow, 2 * YL, 256), BF16),
            pltpu.VMEM((4, KL, narrow, 2 * YL, 256), BF16),
            pltpu.SemaphoreType.DMA((4, KL)),
            pltpu.SemaphoreType.DMA((4, KL)),
            pltpu.SemaphoreType.DMA((4, KL)),
            pltpu.SemaphoreType.DMA((4, KL)),
            pltpu.SemaphoreType.DMA((2,)),
            pltpu.SemaphoreType.DMA((3,)),
        ],
        compiler_params=pltpu.CompilerParams(
            collective_id=0, has_side_effects=True, vmem_limit_bytes=48 * 1024 * 1024
        ),
        name="spectral_layer",
    )(field, cot, weight, pw, *[jnp.asarray(t) for t in consts])
    return act, fgrad, wgrad


def solution(mesh):
    wide, narrow = mesh.shape["wide"], mesh.shape["narrow"]
    return jax.shard_map(
        functools.partial(on_device, wide, narrow),
        mesh=mesh,
        in_specs=(
            P(None, "wide", "narrow", None),
            P("wide", "narrow", None, None),
            P(),
            P(None, "wide", "narrow", None),
        ),
        out_specs=(
            P(None, "wide", "narrow", None),
            P(None, "wide", "narrow", None),
            P("wide", "narrow", None, None),
        ),
        check_vma=False,
    )
```

```python
import functools

import jax
import jax.numpy as jnp
import ml_dtypes
import numpy as np
from jax import lax
from jax.experimental import pallas as pl
from jax.experimental.pallas import tpu as pltpu
from jax.sharding import PartitionSpec as P

C = 32
XL = 8
YL = 16
KXL = 6
KL = 3
NZ = 128
VMEM_BYTES = 64 * 1024 * 1024
MESH = pl.DeviceIdType.MESH
F32 = jnp.float32
BF16 = jnp.bfloat16


def angles(extent, kept, two_sided):
    positions = np.arange(kept)
    frequency = (
        np.where(positions < kept // 2, positions, positions + extent - kept)
        if two_sided
        else positions
    )
    phases = np.arange(extent)[:, None] * frequency[None, :] % extent
    theta = 2.0 * np.pi * phases / extent
    rounded = lambda t: t.astype(np.float32).astype(ml_dtypes.bfloat16).astype(np.float32)
    return rounded(np.cos(theta)), rounded(np.sin(theta))


def tables(wide, narrow, ky):
    nx, ny, kx, kz = XL * wide, YL * narrow, KXL * narrow, KL * wide
    cx, sx = angles(nx, kx, True)
    cy, sy = angles(ny, ky, True)
    cz, sz = angles(NZ, kz, False)
    z_rows = np.stack([cz, -sz], axis=-1).reshape(NZ, wide, KL, 2)
    z_fwd = z_rows.transpose(2, 1, 3, 0).reshape(KL * wide * 2, NZ)
    fwd = lambda c, s: np.stack([np.stack([c, s]), np.stack([-s, c])])
    inv = lambda c, s: np.stack([np.stack([c, -s]), np.stack([s, c])])
    fx = fwd(cx, sx).reshape(2, 2, wide, XL, narrow, KXL)
    x_fwd = fx.transpose(5, 0, 4, 2, 1, 3).reshape(KXL * 2 * narrow, wide * 2 * XL)
    ix = inv(cx, sx).reshape(2, 2, wide, XL, narrow, KXL)
    x_inv = ix.transpose(2, 0, 3, 5, 1, 4).reshape(wide * 2 * XL, KXL * 2 * narrow)
    fy = fwd(cy, sy).reshape(2, 2, narrow, YL, ky)
    y_fwd = fy.transpose(0, 4, 2, 1, 3).reshape(2 * ky, narrow * 2 * YL)
    y_fwd_split = fy.transpose(1, 0, 4, 2, 3).reshape(4 * ky, narrow * YL)
    iy = inv(cy, sy).reshape(2, 2, narrow, YL, ky)
    y_inv = iy.transpose(2, 0, 3, 1, 4).reshape(narrow * 2 * YL, 2 * ky)
    y_inv_split = iy.transpose(0, 2, 3, 1, 4).reshape(2 * narrow * YL, 2 * ky)
    found = (z_fwd, x_fwd, x_inv, y_fwd, y_fwd_split, y_inv, y_inv_split)
    places, blocks, row = [], [], 0
    for t in found:
        rows, columns = t.shape
        places.append((row, rows, columns))
        for first in range(0, columns, 128):
            block = t[:, first : first + 128]
            blocks.append(np.pad(block, ((0, 0), (0, 128 - block.shape[1]))))
            row += rows
    return places, np.concatenate(blocks).astype(ml_dtypes.bfloat16)


def read_table(table, place):
    row, rows, columns = place
    blocks = [
        table[row + i * rows : row + (i + 1) * rows, : min(128, columns - first)]
        for i, first in enumerate(range(0, columns, 128))
    ]
    return jnp.concatenate(blocks, axis=1) if len(blocks) > 1 else blocks[0]


def dot(a, b, dims=((1,), (0,))):
    return lax.dot_general(a, b, (dims, ((), ())), preferred_element_type=F32)


def ones_where(condition):
    return jnp.where(condition, 1.0, 0.0).astype(BF16)


def kernel(
    wide, narrow, ky, total, places,
    field_hbm, cot_hbm, weight_hbm, pw_hbm, table_hbm,
    act_hbm, wgrad_hbm, back_hbm, near_hbm,
    *scratch,
):
    (
        table, field, cot, weight, pw, act, wgrad, zi, near, back_rows, zs, slope, spec, sums, prods, mix, t1, t1_last, t2,
        perm, perm_t, pw_fwd, pw_back, repeat, tile, group_sum,
        ws, wr, ns, nr,
        ws_sem, wr_sem, ns_sem, nr_sem, load_sem, store_sem,
    ) = scratch
    w = lax.axis_index("wide")
    n = lax.axis_index("narrow")
    cells = C * YL
    kk = KL * wide * 2
    rows_j = wide * 2 * XL
    modes = KXL * 2 * ky

    z_fwd, x_fwd, x_inv, y_fwd, y_fwd_split, y_inv, y_inv_split = [
        functools.partial(read_table, table, place) for place in places
    ]
    z_part = pl.ds(0, kk)
    other = pl.ds(kk, table.shape[0] - kk)
    loads = [
        pltpu.make_async_copy(src, dst, load_sem.at[i])
        for i, (src, dst) in enumerate(
            (
                (field_hbm, field),
                (table_hbm.at[z_part], table.at[z_part]),
                (pw_hbm, pw),
                (table_hbm.at[other], table.at[other]),
                (cot_hbm, cot),
                (weight_hbm, weight),
            )
        )
    ]
    for load in loads:
        load.start()

    barrier = pltpu.get_barrier_semaphore()

    @pl.loop(1, wide)
    def _(d):
        pl.semaphore_signal(
            barrier, inc=1, device_id={"wide": lax.rem(w + d, wide)}, device_id_type=MESH
        )

    @pl.loop(1, narrow)
    def _(d):
        pl.semaphore_signal(
            barrier, inc=1, device_id={"narrow": lax.rem(n + d, narrow)}, device_id_type=MESH
        )

    row = lax.broadcasted_iota(jnp.int32, (cells, cells), 0)
    col = lax.broadcasted_iota(jnp.int32, (cells, cells), 1)
    perm[...] = ones_where(((row & 15) == (col >> 5)) & ((row >> 4) == (col & 31)))

    lane = lax.broadcasted_iota(jnp.int32, (1, 128), 1) >> 5

    def shift(value, groups):
        amount = (groups * 32) % 128
        return value if amount == 0 else pltpu.roll(value, amount, 1)

    def pick(pieces):
        acc = pieces[0]
        for s, piece in enumerate(pieces[1:], 1):
            acc = jnp.where(lane == s, piece, acc)
        return acc

    def depth(x, b, block):
        out = dot(z_fwd(), block, ((1,), (1,)))
        zs[b, pl.ds(x, kk, stride=XL), :] = out

    def send(axis, count, me, src, dst, send_sem, recv_sem, a, j):
        dst[a, j, me] = src[a, j, me]

        @pl.loop(1, count)
        def _(d):
            to = lax.rem(me + d, count)
            pltpu.make_async_remote_copy(
                src_ref=src.at[a, j, to],
                dst_ref=dst.at[a, j, me],
                send_sem=send_sem.at[a, j],
                recv_sem=recv_sem.at[a, j],
                device_id={axis: to},
                device_id_type=MESH,
            ).start()

    def send_wide(a, j):
        send("wide", wide, w, ws, wr, ws_sem, wr_sem, a, j)

    def send_narrow(a, j):
        send("narrow", narrow, n, ns, nr, ns_sem, nr_sem, a, j)

    def wait_all(buffer, a, j, sem, count):
        ref = buffer.at[a, j, pl.ds(0, count - 1)]
        pltpu.make_async_copy(ref, ref, sem.at[a, j]).wait()

    def part(j):
        return pl.ds(pl.multiple_of(j * rows_j, rows_j), rows_j)

    def depth_out(a):
        @pl.loop(0, KL)
        def _(j):
            block = jnp.concatenate([zs[b, part(j), :].astype(BF16) for b in range(4)], axis=1)
            ws[a, j] = dot(block, perm[...]).astype(BF16).reshape(wide, 2 * XL, cells)
            send_wide(a, j)

    def x_forward(a, j):
        wait_all(wr, a, j, wr_sem, wide)
        out = dot(x_fwd(), wr[a, j].reshape(rows_j, cells))
        for y in range(YL):
            yb, g = y // 4, y % 4

            def piece(kx, ri):
                first = (kx * 2 + ri) * narrow
                return out[first : first + narrow, yb * 128 : (yb + 1) * 128]

            for ri in range(2):
                t1[pl.ds(ri * YL + y, narrow, stride=2 * YL), :] = pick(
                    [shift(piece(s, ri), s - g) for s in range(4)]
                )
            t1_last[pl.ds(y, narrow, stride=YL), :] = pick(
                [shift(piece(4 + s % 2, s // 2), s - g) for s in range(4)]
            )
        ns[a, j, :, : 2 * YL, :] = t1[...].astype(BF16).reshape(narrow, 2 * YL, 128)
        ns[a, j, :, 2 * YL :, :] = t1_last[...].astype(BF16).reshape(narrow, YL, 128)
        send_narrow(a, j)

    def y_forward(a, j, which):
        wait_all(nr, a, j, nr_sem, narrow)
        first = dot(y_fwd(), nr[a, j, :, : 2 * YL, :].reshape(narrow * 2 * YL, 128))
        both = dot(y_fwd_split(), nr[a, j, :, 2 * YL :, :].reshape(narrow * YL, 128))
        last = both[: 2 * ky] + shift(both[2 * ky :], 2)
        for kx in range(KXL):
            source = first if kx < 4 else last
            spec[which, j, kx * 2 * ky : (kx + 1) * 2 * ky, :] = shift(source, -(kx % 4)).astype(BF16)

    def scale(j):
        return jnp.where(w * KL + j == 0, 1.0, 2.0).astype(F32) / total

    def weights(j, kx, b):
        return (
            weight[j, kx, :, b * 256 : (b + 1) * 256].astype(F32),
            weight[j, kx, :, 1024 + b * 256 : 1024 + (b + 1) * 256].astype(F32),
        )

    def mode_rows(kx):
        return slice(kx * 2 * ky, kx * 2 * ky + ky), slice(kx * 2 * ky + ky, (kx + 1) * 2 * ky)

    def place(summed):
        for lb in range(2):
            found = [
                summed[kx * 2 * ky : (kx + 1) * 2 * ky] for kx in range(4 * lb, min(4 * lb + 4, KXL))
            ]
            mix[lb] = pick(found).astype(BF16)

    def mix_forward(j):
        for b in range(4):
            rep = dot(spec[0, j], repeat[:, b * 256 : (b + 1) * 256])
            for kx in range(KXL):
                re, im = mode_rows(kx)
                w_r, w_i = weights(j, kx, b)
                p_r = rep[re] * w_r - rep[im] * w_i
                p_i = rep[re] * w_i + rep[im] * w_r
                p_r = p_r[:, :128] + p_r[:, 128:]
                p_i = p_i[:, :128] + p_i[:, 128:]
                sums[re, :] = p_r if b == 0 else sums[re, :] + p_r
                sums[im, :] = p_i if b == 0 else sums[im, :] + p_i
        acc = sums[...] * scale(j)
        acc = acc + shift(acc, 2)
        acc = acc + shift(acc, 1)
        place(acc)

    def mix_back(j):
        sums[...] = dot(spec[1, j], tile[...])
        for kx in range(KXL):
            re, im = mode_rows(kx)
            g_r = jnp.concatenate([sums[re, :]] * 2, axis=1)
            g_i = jnp.concatenate([sums[im, :]] * 2, axis=1)
            for b in range(4):
                w_r, w_i = weights(j, kx, b)
                lanes = slice(b * 256, (b + 1) * 256)
                prods[re, lanes] = (w_r * g_r + w_i * g_i).astype(BF16)
                prods[im, lanes] = (w_r * g_i - w_i * g_r).astype(BF16)
        place(dot(prods[...], group_sum[...]) * scale(j))

    def weight_gradient(j):
        sums[...] = dot(spec[1, j], tile[...]) * scale(j)
        for b in range(4):
            rep = dot(spec[0, j], repeat[:, b * 256 : (b + 1) * 256])
            for kx in range(KXL):
                re, im = mode_rows(kx)
                g_r = jnp.concatenate([sums[re, :]] * 2, axis=1)
                g_i = jnp.concatenate([sums[im, :]] * 2, axis=1)
                wgrad[j, kx, :, b * 256 : (b + 1) * 256] = (rep[re] * g_r + rep[im] * g_i).astype(BF16)
                wgrad[j, kx, :, 1024 + b * 256 : 1024 + (b + 1) * 256] = (
                    rep[re] * g_i - rep[im] * g_r
                ).astype(BF16)

    def y_inverse(a, j):
        first = dot(y_inv(), mix[0]).astype(BF16)
        ns[a, j, :, : 2 * YL, :] = first.reshape(narrow, 2 * YL, 128)
        both = dot(y_inv_split(), mix[1])
        half = narrow * YL
        last = jnp.where(lane < 2, both[:half], shift(both[half:], 2)).astype(BF16)
        ns[a, j, :, 2 * YL :, :] = last.reshape(narrow, YL, 128)
        send_narrow(a, j)

    def x_inverse(a, j):
        wait_all(nr, a, j, nr_sem, narrow)
        t1[...] = nr[a, j, :, : 2 * YL, :].reshape(narrow * 2 * YL, 128).astype(F32)
        t1_last[...] = nr[a, j, :, 2 * YL :, :].reshape(narrow * YL, 128).astype(F32)
        for yb in range(4):
            lanes = slice(yb * 128, (yb + 1) * 128)
            ys = [4 * yb + g for g in range(4)]
            loaded = [
                [t1[pl.ds(ri * YL + y, narrow, stride=2 * YL), :] for y in ys] for ri in range(2)
            ]
            last = [t1_last[pl.ds(y, narrow, stride=YL), :] for y in ys]
            for kx in range(KXL):
                both = []
                for ri in range(2):
                    source = loaded[ri] if kx < 4 else last
                    s = kx if kx < 4 else ri * 2 + kx - 4
                    both.append(pick([shift(source[g], g - s) for g in range(4)]))
                t2[kx * 2 * narrow : (kx + 1) * 2 * narrow, lanes] = jnp.concatenate(
                    both, axis=0
                ).astype(BF16)
        ws[a, j] = dot(x_inv(), t2[...]).astype(BF16).reshape(wide, 2 * XL, cells)
        send_wide(a, j)

    def through_modes(back):
        @pl.loop(0, KL + 2)
        def _(t):
            @pl.when(t < KL)
            def _():
                x_forward(2 * back, t)

            @pl.when((t >= 1) & (t <= KL))
            def _():
                y_forward(2 * back, t - 1, back)
                mix_back(t - 1) if back else mix_forward(t - 1)
                y_inverse(2 * back + 1, t - 1)

            @pl.when(t >= 2)
            def _():
                x_inverse(2 * back + 1, t - 2)

    def depth_in(a):
        @pl.loop(0, KL)
        def _(j):
            wait_all(wr, a, j, wr_sem, wide)
            out = dot(wr[a, j].reshape(rows_j, cells), perm_t[...])
            for b in range(4):
                block = out[:, b * 128 : (b + 1) * 128]
                if a == 1:
                    zi[b, part(j), :] = block
                else:
                    back_rows[b, part(j), :] = block.astype(BF16)

    def pointwise(matrix, source):
        @pl.loop(0, XL)
        def _(x):
            near[x] = dot(matrix[...], source[:, x].reshape(cells, NZ))

    loads[0].wait()
    loads[1].wait()
    for x in range(XL):
        plane = field[:, x].reshape(cells, NZ)
        for b in range(4):
            depth(x, b, plane[b * 128 : (b + 1) * 128])

    pl.semaphore_wait(barrier, wide + narrow - 2)
    depth_out(0)

    loads[2].wait()
    loads[3].wait()
    perm_t[...] = ones_where(((row >> 5) == (col & 15)) & ((row & 31) == (col >> 4)))
    spread_row = lax.broadcasted_iota(jnp.int32, (cells, C), 0)
    spread_col = lax.broadcasted_iota(jnp.int32, (cells, C), 1)
    spread = ones_where((spread_row >> 4) == spread_col)
    same_y = (row & 15) == (col & 15)
    behind = dot(dot(spread, pw[...]).astype(BF16), spread, ((1,), (1,)))
    pw_back[...] = jnp.where(same_y, behind, 0.0).astype(BF16)
    ahead = dot(dot(spread, pw[...], ((1,), (1,))).astype(BF16), spread, ((1,), (1,)))
    pw_fwd[...] = jnp.where(same_y, ahead, 0.0).astype(BF16)
    r_row = lax.broadcasted_iota(jnp.int32, (128, 1024), 0)
    r_col = lax.broadcasted_iota(jnp.int32, (128, 1024), 1)
    repeat[...] = ones_where(r_row == (r_col >> 5))
    t_row = lax.broadcasted_iota(jnp.int32, (128, 128), 0)
    t_col = lax.broadcasted_iota(jnp.int32, (128, 128), 1)
    tile[...] = ones_where(t_row == (t_col & 31))
    g_row = lax.broadcasted_iota(jnp.int32, (1024, 128), 0)
    g_col = lax.broadcasted_iota(jnp.int32, (1024, 128), 1)
    group_sum[...] = ones_where((g_row >> 5) == (g_col & 31))
    pointwise(pw_fwd, field)
    loads[4].wait()
    loads[5].wait()

    through_modes(0)
    depth_in(1)

    root = 0.7978845608028654

    @pl.loop(0, 4)
    def _(b):
        rows = pl.ds(pl.multiple_of(b * 128, 128), 128)
        group = pl.ds(b * 8, 8)
        for x in range(XL):
            block = zi[b, pl.ds(x, kk, stride=XL), :].astype(BF16)
            t = dot(block, z_fwd(), ((0,), (0,))) + near[x, rows, :]
            square = t * t
            th = jnp.tanh(root * t * (1.0 + 0.044715 * square))
            half = 0.5 + 0.5 * th
            act[group, x] = (t * half).astype(BF16).reshape(8, YL, NZ)
            grad = half + (0.5 * root) * t * (1.0 - th * th) * (1.0 + 0.134145 * square)
            up = cot[group, x].reshape(128, NZ).astype(F32)
            block = (up * grad).astype(BF16)
            slope[group, x] = block.reshape(8, YL, NZ)
            depth(x, b, block)

    depth_out(2)
    stores = [
        pltpu.make_async_copy(src, dst, store_sem.at[i])
        for i, (src, dst) in enumerate(
            ((act, act_hbm), (near, near_hbm), (wgrad, wgrad_hbm), (back_rows, back_hbm))
        )
    ]
    stores[0].start()
    pointwise(pw_back, slope)
    stores[1].start()
    through_modes(1)
    pl.loop(0, KL)(weight_gradient)
    stores[2].start()
    depth_in(3)
    stores[3].start()

    @pl.loop(0, 4)
    def _(a):
        @pl.loop(0, KL)
        def _(j):
            wait_all(ws, a, j, ws_sem, wide)
            wait_all(ns, a, j, ns_sem, narrow)

    for store in stores:
        store.wait()


def finish(
    kk, act_in, wgrad_in, back_hbm, near_hbm, table_hbm,
    act_hbm, wgrad_hbm, fgrad_hbm,
    back, near, table, zi, fgrad, sem,
):
    stores = [
        pltpu.make_async_copy(act_in, act_hbm, sem.at[0]),
        pltpu.make_async_copy(wgrad_in, wgrad_hbm, sem.at[1]),
    ]
    load_table = pltpu.make_async_copy(table_hbm.at[pl.ds(0, kk)], table, sem.at[2])
    load_table.start()
    loads = []
    for b in range(4):
        rows = pl.ds(b * 128, 128)
        loads.append(
            (
                pltpu.make_async_copy(back_hbm.at[b], back.at[b], sem.at[3 + b]),
                pltpu.make_async_copy(near_hbm.at[:, rows], near.at[:, rows], sem.at[7 + b]),
            )
        )
        for load in loads[-1]:
            load.start()
    for store in stores:
        store.start()
    load_table.wait()
    for b in range(4):
        for load in loads[b]:
            load.wait()
        zi[b] = back[b].astype(F32)
        for x in range(XL):
            block = zi[b, pl.ds(x, kk, stride=XL), :].astype(BF16)
            t = dot(block, table[...], ((0,), (0,))) + near[x, b * 128 : (b + 1) * 128, :]
            fgrad[b * 8 : (b + 1) * 8, x] = t.astype(BF16).reshape(8, YL, NZ)
        group = pl.ds(b * 8, 8)
        stores.append(pltpu.make_async_copy(fgrad.at[group], fgrad_hbm.at[group], sem.at[11 + b]))
        stores[-1].start()
    for store in stores:
        store.wait()


def on_device(wide, narrow, field, weight, pw, cot):
    ky = weight.shape[2]
    total = float(XL * wide * YL * narrow * NZ)
    places, packed = tables(wide, narrow, ky)
    table = jnp.asarray(packed)
    cells = C * YL
    kk = KL * wide * 2
    modes = KXL * 2 * ky
    hbm = pl.BlockSpec(memory_space=pl.ANY)
    grid_like = jax.ShapeDtypeStruct(field.shape, BF16)
    weight_like = jax.ShapeDtypeStruct(weight.shape, BF16)
    parts = pl.pallas_call(
        functools.partial(kernel, wide, narrow, ky, total, places),
        out_shape=(
            grid_like,
            weight_like,
            jax.ShapeDtypeStruct((4, kk * XL, 128), BF16),
            jax.ShapeDtypeStruct((XL, cells, NZ), F32),
        ),
        in_specs=[hbm] * 5,
        out_specs=(hbm,) * 4,
        scratch_shapes=[
            pltpu.VMEM(table.shape, BF16),
            pltpu.VMEM(field.shape, BF16),
            pltpu.VMEM(cot.shape, BF16),
            pltpu.VMEM(weight.shape, BF16),
            pltpu.VMEM(pw.shape, BF16),
            pltpu.VMEM(field.shape, BF16),
            pltpu.VMEM(weight.shape, BF16),
            pltpu.VMEM((4, kk * XL, 128), F32),
            pltpu.VMEM((XL, cells, NZ), F32),
            pltpu.VMEM((4, kk * XL, 128), BF16),
            pltpu.VMEM((4, kk * XL, 128), F32),
            pltpu.VMEM(field.shape, BF16),
            pltpu.VMEM((2, KL, modes, 128), BF16),
            pltpu.VMEM((modes, 128), F32),
            pltpu.VMEM((modes, 1024), BF16),
            pltpu.VMEM((2, 2 * ky, 128), BF16),
            pltpu.VMEM((narrow * 2 * YL, 128), F32),
            pltpu.VMEM((narrow * YL, 128), F32),
            pltpu.VMEM((KXL * narrow * 2, cells), BF16),
            pltpu.VMEM((cells, cells), BF16),
            pltpu.VMEM((cells, cells), BF16),
            pltpu.VMEM((cells, cells), BF16),
            pltpu.VMEM((cells, cells), BF16),
            pltpu.VMEM((128, 1024), BF16),
            pltpu.VMEM((128, 128), BF16),
            pltpu.VMEM((1024, 128), BF16),
            pltpu.VMEM((4, KL, wide, 2 * XL, cells), BF16),
            pltpu.VMEM((4, KL, wide, 2 * XL, cells), BF16),
            pltpu.VMEM((4, KL, narrow, 3 * YL, 128), BF16),
            pltpu.VMEM((4, KL, narrow, 3 * YL, 128), BF16),
            pltpu.SemaphoreType.DMA((4, KL)),
            pltpu.SemaphoreType.DMA((4, KL)),
            pltpu.SemaphoreType.DMA((4, KL)),
            pltpu.SemaphoreType.DMA((4, KL)),
            pltpu.SemaphoreType.DMA((6,)),
            pltpu.SemaphoreType.DMA((4,)),
        ],
        compiler_params=pltpu.CompilerParams(
            collective_id=0, has_side_effects=True, vmem_limit_bytes=VMEM_BYTES
        ),
        name="spectral_layer",
    )(field, cot, weight, pw, table)
    act, wgrad, fgrad = pl.pallas_call(
        functools.partial(finish, kk),
        out_shape=(grid_like, weight_like, grid_like),
        in_specs=[hbm] * 5,
        out_specs=(hbm,) * 3,
        scratch_shapes=[
            pltpu.VMEM((4, kk * XL, 128), BF16),
            pltpu.VMEM((XL, cells, NZ), F32),
            pltpu.VMEM((kk, NZ), BF16),
            pltpu.VMEM((4, kk * XL, 128), F32),
            pltpu.VMEM(field.shape, BF16),
            pltpu.SemaphoreType.DMA((15,)),
        ],
        compiler_params=pltpu.CompilerParams(vmem_limit_bytes=VMEM_BYTES),
        name="field_gradient",
    )(*parts, table)
    return act, fgrad, wgrad


def solution(mesh):
    wide, narrow = mesh.shape["wide"], mesh.shape["narrow"]
    return jax.shard_map(
        functools.partial(on_device, wide, narrow),
        mesh=mesh,
        in_specs=(
            P(None, "wide", "narrow", None),
            P("wide", "narrow", None, None),
            P(),
            P(None, "wide", "narrow", None),
        ),
        out_specs=(
            P(None, "wide", "narrow", None),
            P(None, "wide", "narrow", None),
            P("wide", "narrow", None, None),
        ),
        check_vma=False,
    )
```

```python
import functools

import jax
import jax.numpy as jnp
import ml_dtypes
import numpy as np
from jax import lax
from jax.experimental import pallas as pl
from jax.experimental.pallas import tpu as pltpu
from jax.sharding import PartitionSpec as P

C = 32
XL = 8
YL = 16
KXL = 6
KL = 3
NZ = 128
VMEM_BYTES = 64 * 1024 * 1024
MESH = pl.DeviceIdType.MESH
F32 = jnp.float32
BF16 = jnp.bfloat16


def angles(extent, kept, two_sided):
    positions = np.arange(kept)
    frequency = (
        np.where(positions < kept // 2, positions, positions + extent - kept)
        if two_sided
        else positions
    )
    phases = np.arange(extent)[:, None] * frequency[None, :] % extent
    theta = 2.0 * np.pi * phases / extent
    rounded = lambda t: t.astype(np.float32).astype(ml_dtypes.bfloat16).astype(np.float32)
    return rounded(np.cos(theta)), rounded(np.sin(theta))


def tables(wide, narrow, ky):
    nx, ny, kx, kz = XL * wide, YL * narrow, KXL * narrow, KL * wide
    cx, sx = angles(nx, kx, True)
    cy, sy = angles(ny, ky, True)
    cz, sz = angles(NZ, kz, False)
    z_rows = np.stack([cz, -sz], axis=-1).reshape(NZ, wide, KL, 2)
    z_fwd = z_rows.transpose(2, 1, 3, 0).reshape(KL * wide * 2, NZ)
    fwd = lambda c, s: np.stack([np.stack([c, s]), np.stack([-s, c])])
    inv = lambda c, s: np.stack([np.stack([c, -s]), np.stack([s, c])])
    fx = fwd(cx, sx).reshape(2, 2, wide, XL, narrow, KXL)
    x_fwd = fx.transpose(5, 0, 4, 2, 1, 3).reshape(KXL * 2 * narrow, wide * 2 * XL)
    ix = inv(cx, sx).reshape(2, 2, wide, XL, narrow, KXL)
    x_inv = ix.transpose(2, 0, 3, 5, 1, 4).reshape(wide * 2 * XL, KXL * 2 * narrow)
    fy = fwd(cy, sy).reshape(2, 2, narrow, YL, ky)
    y_fwd = fy.transpose(0, 4, 2, 1, 3).reshape(2 * ky, narrow * 2 * YL)
    y_fwd_split = fy.transpose(1, 0, 4, 2, 3).reshape(4 * ky, narrow * YL)
    iy = inv(cy, sy).reshape(2, 2, narrow, YL, ky)
    y_inv = iy.transpose(2, 0, 3, 1, 4).reshape(narrow * 2 * YL, 2 * ky)
    y_inv_split = iy.transpose(0, 2, 3, 1, 4).reshape(2 * narrow * YL, 2 * ky)
    found = (z_fwd, x_fwd, x_inv, y_fwd, y_fwd_split, y_inv, y_inv_split)
    places, blocks, row = [], [], 0
    for t in found:
        rows, columns = t.shape
        places.append((row, rows, columns))
        for first in range(0, columns, 128):
            block = t[:, first : first + 128]
            blocks.append(np.pad(block, ((0, 0), (0, 128 - block.shape[1]))))
            row += rows
    return places, np.concatenate(blocks).astype(ml_dtypes.bfloat16)


def read_table(table, place):
    row, rows, columns = place
    blocks = [
        table[row + i * rows : row + (i + 1) * rows, : min(128, columns - first)]
        for i, first in enumerate(range(0, columns, 128))
    ]
    return jnp.concatenate(blocks, axis=1) if len(blocks) > 1 else blocks[0]


def dot(a, b, dims=((1,), (0,))):
    return lax.dot_general(a, b, (dims, ((), ())), preferred_element_type=F32)


def ones_where(condition):
    return jnp.where(condition, 1.0, 0.0).astype(BF16)


def kernel(
    wide, narrow, ky, total, places,
    field_hbm, cot_hbm, weight_hbm, pw_hbm, table_hbm,
    act_hbm, wgrad_hbm, back_hbm, near_hbm,
    *scratch,
):
    (
        table, field, cot, weight, pw, act, wgrad, zi, near, back_rows, zs, slope, spec, sums, prods, mix, t1, t1_last, t2,
        perm, perm_t, pw_fwd, pw_back, repeat, tile, group_sum,
        ws, wr, ns, nr,
        ws_sem, wr_sem, ns_sem, nr_sem, load_sem, store_sem,
    ) = scratch
    w = lax.axis_index("wide")
    n = lax.axis_index("narrow")
    cells = C * YL
    kk = KL * wide * 2
    rows_j = wide * 2 * XL
    modes = KXL * 2 * ky

    z_fwd, x_fwd, x_inv, y_fwd, y_fwd_split, y_inv, y_inv_split = [
        functools.partial(read_table, table, place) for place in places
    ]
    z_part = pl.ds(0, kk)
    other = pl.ds(kk, table.shape[0] - kk)
    loads = [
        pltpu.make_async_copy(src, dst, load_sem.at[i])
        for i, (src, dst) in enumerate(
            (
                (field_hbm, field),
                (table_hbm.at[z_part], table.at[z_part]),
                (pw_hbm, pw),
                (table_hbm.at[other], table.at[other]),
                (cot_hbm, cot),
                (weight_hbm, weight),
            )
        )
    ]
    for load in loads:
        load.start()

    barrier = pltpu.get_barrier_semaphore()

    half = narrow // 2
    flip = lax.rem(n + half, narrow)

    @pl.loop(0, wide)
    def _(d):
        pl.semaphore_signal(
            barrier, inc=1, device_id={"wide": d, "narrow": flip}, device_id_type=MESH
        )

    @pl.loop(1, narrow)
    def _(d):
        pl.semaphore_signal(
            barrier, inc=1, device_id={"narrow": lax.rem(n + d, narrow)}, device_id_type=MESH
        )

    row = lax.broadcasted_iota(jnp.int32, (cells, cells), 0)
    col = lax.broadcasted_iota(jnp.int32, (cells, cells), 1)
    perm[...] = ones_where(((row & 15) == (col >> 5)) & ((row >> 4) == (col & 31)))

    lane = lax.broadcasted_iota(jnp.int32, (1, 128), 1) >> 5

    def shift(value, groups):
        amount = (groups * 32) % 128
        return value if amount == 0 else pltpu.roll(value, amount, 1)

    def pick(pieces):
        acc = pieces[0]
        for s, piece in enumerate(pieces[1:], 1):
            acc = jnp.where(lane == s, piece, acc)
        return acc

    def depth(x, b, block):
        out = dot(z_fwd(), block, ((1,), (1,)))
        zs[b, pl.ds(x, kk, stride=XL), :] = out

    def send_wide(a, j):
        @pl.loop(0, wide)
        def _(d):
            to = lax.rem(w + d, wide)
            pltpu.make_async_remote_copy(
                src_ref=ws.at[a, j, to],
                dst_ref=wr.at[a, j, w],
                send_sem=ws_sem.at[a, j],
                recv_sem=wr_sem.at[a, j],
                device_id={"wide": to, "narrow": flip},
                device_id_type=MESH,
            ).start()

    def send_narrow(a, j, take, slot):
        nr[a, j, slot] = ns[a, j, take(n)]

        @pl.loop(1, narrow)
        def _(d):
            to = lax.rem(n + d, narrow)
            pltpu.make_async_remote_copy(
                src_ref=ns.at[a, j, take(to)],
                dst_ref=nr.at[a, j, slot],
                send_sem=ns_sem.at[a, j],
                recv_sem=nr_sem.at[a, j],
                device_id={"narrow": to},
                device_id_type=MESH,
            ).start()

    def wait_all(buffer, a, j, sem, count):
        ref = buffer.at[a, j, pl.ds(0, count)]
        pltpu.make_async_copy(ref, ref, sem.at[a, j]).wait()

    def part(j):
        return pl.ds(pl.multiple_of(j * rows_j, rows_j), rows_j)

    def depth_out(a):
        @pl.loop(0, KL)
        def _(j):
            block = jnp.concatenate([zs[b, part(j), :].astype(BF16) for b in range(4)], axis=1)
            ws[a, j] = dot(block, perm[...]).astype(BF16).reshape(wide, 2 * XL, cells)
            send_wide(a, j)

    def x_forward(a, j):
        wait_all(wr, a, j, wr_sem, wide)
        out = dot(x_fwd(), wr[a, j].reshape(rows_j, cells))
        for y in range(YL):
            yb, g = y // 4, y % 4

            def piece(kx, ri):
                first = (kx * 2 + ri) * narrow
                return out[first : first + narrow, yb * 128 : (yb + 1) * 128]

            for ri in range(2):
                t1[pl.ds(ri * YL + y, narrow, stride=2 * YL), :] = pick(
                    [shift(piece(s, ri), s - g) for s in range(4)]
                )
            t1_last[pl.ds(y, narrow, stride=YL), :] = pick(
                [shift(piece(4 + s % 2, s // 2), s - g) for s in range(4)]
            )
        ns[a, j, :, : 2 * YL, :] = t1[...].astype(BF16).reshape(narrow, 2 * YL, 128)
        ns[a, j, :, 2 * YL :, :] = t1_last[...].astype(BF16).reshape(narrow, YL, 128)
        send_narrow(a, j, lambda to: to, flip)

    def y_forward(a, j, which):
        wait_all(nr, a, j, nr_sem, narrow - 1)
        first = dot(y_fwd(), nr[a, j, :, : 2 * YL, :].reshape(narrow * 2 * YL, 128))
        both = dot(y_fwd_split(), nr[a, j, :, 2 * YL :, :].reshape(narrow * YL, 128))
        last = both[: 2 * ky] + shift(both[2 * ky :], 2)
        for kx in range(KXL):
            source = first if kx < 4 else last
            spec[which, j, kx * 2 * ky : (kx + 1) * 2 * ky, :] = shift(source, -(kx % 4)).astype(BF16)

    def scale(j):
        return jnp.where(w * KL + j == 0, 1.0, 2.0).astype(F32) / total

    def weights(j, kx, b):
        return (
            weight[j, kx, :, b * 256 : (b + 1) * 256].astype(F32),
            weight[j, kx, :, 1024 + b * 256 : 1024 + (b + 1) * 256].astype(F32),
        )

    def mode_rows(kx):
        return slice(kx * 2 * ky, kx * 2 * ky + ky), slice(kx * 2 * ky + ky, (kx + 1) * 2 * ky)

    def place(summed):
        for lb in range(2):
            found = [
                summed[kx * 2 * ky : (kx + 1) * 2 * ky] for kx in range(4 * lb, min(4 * lb + 4, KXL))
            ]
            mix[lb] = pick(found).astype(BF16)

    def mix_forward(j):
        for b in range(4):
            rep = dot(spec[0, j], repeat[:, b * 256 : (b + 1) * 256])
            for kx in range(KXL):
                re, im = mode_rows(kx)
                w_r, w_i = weights(j, kx, b)
                p_r = rep[re] * w_r - rep[im] * w_i
                p_i = rep[re] * w_i + rep[im] * w_r
                p_r = p_r[:, :128] + p_r[:, 128:]
                p_i = p_i[:, :128] + p_i[:, 128:]
                sums[re, :] = p_r if b == 0 else sums[re, :] + p_r
                sums[im, :] = p_i if b == 0 else sums[im, :] + p_i
        acc = sums[...] * scale(j)
        acc = acc + shift(acc, 2)
        acc = acc + shift(acc, 1)
        place(acc)

    def mix_back(j):
        sums[...] = dot(spec[1, j], tile[...])
        for kx in range(KXL):
            re, im = mode_rows(kx)
            g_r = jnp.concatenate([sums[re, :]] * 2, axis=1)
            g_i = jnp.concatenate([sums[im, :]] * 2, axis=1)
            for b in range(4):
                w_r, w_i = weights(j, kx, b)
                lanes = slice(b * 256, (b + 1) * 256)
                prods[re, lanes] = (w_r * g_r + w_i * g_i).astype(BF16)
                prods[im, lanes] = (w_r * g_i - w_i * g_r).astype(BF16)
        place(dot(prods[...], group_sum[...]) * scale(j))

    def weight_gradient(j):
        sums[...] = dot(spec[1, j], tile[...]) * scale(j)
        for b in range(4):
            rep = dot(spec[0, j], repeat[:, b * 256 : (b + 1) * 256])
            for kx in range(KXL):
                re, im = mode_rows(kx)
                g_r = jnp.concatenate([sums[re, :]] * 2, axis=1)
                g_i = jnp.concatenate([sums[im, :]] * 2, axis=1)
                wgrad[j, kx, :, b * 256 : (b + 1) * 256] = (rep[re] * g_r + rep[im] * g_i).astype(BF16)
                wgrad[j, kx, :, 1024 + b * 256 : 1024 + (b + 1) * 256] = (
                    rep[re] * g_i - rep[im] * g_r
                ).astype(BF16)

    def y_inverse(a, j):
        first = dot(y_inv(), mix[0]).astype(BF16)
        ns[a, j, :, : 2 * YL, :] = first.reshape(narrow, 2 * YL, 128)
        both = dot(y_inv_split(), mix[1])
        split = narrow * YL
        last = jnp.where(lane < 2, both[:split], shift(both[split:], 2)).astype(BF16)
        ns[a, j, :, 2 * YL :, :] = last.reshape(narrow, YL, 128)
        send_narrow(a, j, lambda to: lax.rem(to + half, narrow), n)

    def x_inverse(a, j):
        wait_all(nr, a, j, nr_sem, narrow - 1)
        t1[...] = nr[a, j, :, : 2 * YL, :].reshape(narrow * 2 * YL, 128).astype(F32)
        t1_last[...] = nr[a, j, :, 2 * YL :, :].reshape(narrow * YL, 128).astype(F32)
        for yb in range(4):
            lanes = slice(yb * 128, (yb + 1) * 128)
            ys = [4 * yb + g for g in range(4)]
            loaded = [
                [t1[pl.ds(ri * YL + y, narrow, stride=2 * YL), :] for y in ys] for ri in range(2)
            ]
            last = [t1_last[pl.ds(y, narrow, stride=YL), :] for y in ys]
            for kx in range(KXL):
                both = []
                for ri in range(2):
                    source = loaded[ri] if kx < 4 else last
                    s = kx if kx < 4 else ri * 2 + kx - 4
                    both.append(pick([shift(source[g], g - s) for g in range(4)]))
                t2[kx * 2 * narrow : (kx + 1) * 2 * narrow, lanes] = jnp.concatenate(
                    both, axis=0
                ).astype(BF16)
        ws[a, j] = dot(x_inv(), t2[...]).astype(BF16).reshape(wide, 2 * XL, cells)
        send_wide(a, j)

    def through_modes(back):
        @pl.loop(0, KL + 2)
        def _(t):
            @pl.when(t < KL)
            def _():
                x_forward(2 * back, t)

            @pl.when((t >= 1) & (t <= KL))
            def _():
                y_forward(2 * back, t - 1, back)
                mix_back(t - 1) if back else mix_forward(t - 1)
                y_inverse(2 * back + 1, t - 1)

            @pl.when(t >= 2)
            def _():
                x_inverse(2 * back + 1, t - 2)

    def depth_in(a):
        @pl.loop(0, KL)
        def _(j):
            wait_all(wr, a, j, wr_sem, wide)
            out = dot(wr[a, j].reshape(rows_j, cells), perm_t[...])
            for b in range(4):
                block = out[:, b * 128 : (b + 1) * 128]
                if a == 1:
                    zi[b, part(j), :] = block
                else:
                    back_rows[b, part(j), :] = block.astype(BF16)

    def pointwise(matrix, source):
        @pl.loop(0, XL)
        def _(x):
            near[x] = dot(matrix[...], source[:, x].reshape(cells, NZ))

    loads[0].wait()
    loads[1].wait()
    for x in range(XL):
        plane = field[:, x].reshape(cells, NZ)
        for b in range(4):
            depth(x, b, plane[b * 128 : (b + 1) * 128])

    pl.semaphore_wait(barrier, wide + narrow - 1)
    depth_out(0)

    loads[2].wait()
    loads[3].wait()
    perm_t[...] = ones_where(((row >> 5) == (col & 15)) & ((row & 31) == (col >> 4)))
    spread_row = lax.broadcasted_iota(jnp.int32, (cells, C), 0)
    spread_col = lax.broadcasted_iota(jnp.int32, (cells, C), 1)
    spread = ones_where((spread_row >> 4) == spread_col)
    same_y = (row & 15) == (col & 15)
    behind = dot(dot(spread, pw[...]).astype(BF16), spread, ((1,), (1,)))
    pw_back[...] = jnp.where(same_y, behind, 0.0).astype(BF16)
    ahead = dot(dot(spread, pw[...], ((1,), (1,))).astype(BF16), spread, ((1,), (1,)))
    pw_fwd[...] = jnp.where(same_y, ahead, 0.0).astype(BF16)
    r_row = lax.broadcasted_iota(jnp.int32, (128, 1024), 0)
    r_col = lax.broadcasted_iota(jnp.int32, (128, 1024), 1)
    repeat[...] = ones_where(r_row == (r_col >> 5))
    t_row = lax.broadcasted_iota(jnp.int32, (128, 128), 0)
    t_col = lax.broadcasted_iota(jnp.int32, (128, 128), 1)
    tile[...] = ones_where(t_row == (t_col & 31))
    g_row = lax.broadcasted_iota(jnp.int32, (1024, 128), 0)
    g_col = lax.broadcasted_iota(jnp.int32, (1024, 128), 1)
    group_sum[...] = ones_where((g_row >> 5) == (g_col & 31))
    pointwise(pw_fwd, field)
    loads[4].wait()
    loads[5].wait()

    through_modes(0)
    depth_in(1)

    root = 0.7978845608028654

    @pl.loop(0, 4)
    def _(b):
        rows = pl.ds(pl.multiple_of(b * 128, 128), 128)
        group = pl.ds(b * 8, 8)
        for x in range(XL):
            block = zi[b, pl.ds(x, kk, stride=XL), :].astype(BF16)
            t = dot(block, z_fwd(), ((0,), (0,))) + near[x, rows, :]
            square = t * t
            th = jnp.tanh(root * t * (1.0 + 0.044715 * square))
            gate = 0.5 + 0.5 * th
            act[group, x] = (t * gate).astype(BF16).reshape(8, YL, NZ)
            grad = gate + (0.5 * root) * t * (1.0 - th * th) * (1.0 + 0.134145 * square)
            up = cot[group, x].reshape(128, NZ).astype(F32)
            block = (up * grad).astype(BF16)
            slope[group, x] = block.reshape(8, YL, NZ)
            depth(x, b, block)

    depth_out(2)
    stores = [
        pltpu.make_async_copy(src, dst, store_sem.at[i])
        for i, (src, dst) in enumerate(
            ((act, act_hbm), (near, near_hbm), (wgrad, wgrad_hbm), (back_rows, back_hbm))
        )
    ]
    stores[0].start()
    pointwise(pw_back, slope)
    stores[1].start()
    through_modes(1)
    pl.loop(0, KL)(weight_gradient)
    stores[2].start()
    depth_in(3)
    stores[3].start()

    @pl.loop(0, 4)
    def _(a):
        @pl.loop(0, KL)
        def _(j):
            wait_all(ws, a, j, ws_sem, wide)
            wait_all(ns, a, j, ns_sem, narrow - 1)

    for store in stores:
        store.wait()


def finish(
    kk, act_in, wgrad_in, back_hbm, near_hbm, table_hbm,
    act_hbm, wgrad_hbm, fgrad_hbm,
    back, near, table, zi, fgrad, act, wgrad, sem,
):
    load_table = pltpu.make_async_copy(table_hbm.at[pl.ds(0, kk)], table, sem.at[0])
    load_table.start()
    loads, passed, stores = [], [], []
    for b in range(4):
        rows = pl.ds(b * 128, 128)
        loads.append(
            (
                pltpu.make_async_copy(back_hbm.at[b], back.at[b], sem.at[1 + b]),
                pltpu.make_async_copy(near_hbm.at[:, rows], near.at[:, rows], sem.at[5 + b]),
            )
        )
        for load in loads[-1]:
            load.start()
    whole = [(act_in, act, act_hbm)] + [
        (wgrad_in.at[j], wgrad.at[j], wgrad_hbm.at[j]) for j in range(KL)
    ]
    for i, (src, held, dst) in enumerate(whole):
        passed.append(
            (
                pltpu.make_async_copy(src, held, sem.at[9 + i]),
                pltpu.make_async_copy(held, dst, sem.at[13 + i]),
            )
        )
        passed[-1][0].start()
    load_table.wait()
    for b in range(4):
        for load in loads[b]:
            load.wait()
        zi[b] = back[b].astype(F32)
        for x in range(XL):
            block = zi[b, pl.ds(x, kk, stride=XL), :].astype(BF16)
            t = dot(block, table[...], ((0,), (0,))) + near[x, b * 128 : (b + 1) * 128, :]
            fgrad[b * 8 : (b + 1) * 8, x] = t.astype(BF16).reshape(8, YL, NZ)
        group = pl.ds(b * 8, 8)
        stores.append(pltpu.make_async_copy(fgrad.at[group], fgrad_hbm.at[group], sem.at[17 + b]))
        stores[-1].start()
        passed[b][0].wait()
        passed[b][1].start()
        stores.append(passed[b][1])
    for store in stores:
        store.wait()


def on_device(wide, narrow, field, weight, pw, cot):
    ky = weight.shape[2]
    total = float(XL * wide * YL * narrow * NZ)
    places, packed = tables(wide, narrow, ky)
    table = jnp.asarray(packed)
    cells = C * YL
    kk = KL * wide * 2
    modes = KXL * 2 * ky
    hbm = pl.BlockSpec(memory_space=pl.ANY)
    grid_like = jax.ShapeDtypeStruct(field.shape, BF16)
    weight_like = jax.ShapeDtypeStruct(weight.shape, BF16)
    parts = pl.pallas_call(
        functools.partial(kernel, wide, narrow, ky, total, places),
        out_shape=(
            grid_like,
            weight_like,
            jax.ShapeDtypeStruct((4, kk * XL, 128), BF16),
            jax.ShapeDtypeStruct((XL, cells, NZ), F32),
        ),
        in_specs=[hbm] * 5,
        out_specs=(hbm,) * 4,
        scratch_shapes=[
            pltpu.VMEM(table.shape, BF16),
            pltpu.VMEM(field.shape, BF16),
            pltpu.VMEM(cot.shape, BF16),
            pltpu.VMEM(weight.shape, BF16),
            pltpu.VMEM(pw.shape, BF16),
            pltpu.VMEM(field.shape, BF16),
            pltpu.VMEM(weight.shape, BF16),
            pltpu.VMEM((4, kk * XL, 128), F32),
            pltpu.VMEM((XL, cells, NZ), F32),
            pltpu.VMEM((4, kk * XL, 128), BF16),
            pltpu.VMEM((4, kk * XL, 128), F32),
            pltpu.VMEM(field.shape, BF16),
            pltpu.VMEM((2, KL, modes, 128), BF16),
            pltpu.VMEM((modes, 128), F32),
            pltpu.VMEM((modes, 1024), BF16),
            pltpu.VMEM((2, 2 * ky, 128), BF16),
            pltpu.VMEM((narrow * 2 * YL, 128), F32),
            pltpu.VMEM((narrow * YL, 128), F32),
            pltpu.VMEM((KXL * narrow * 2, cells), BF16),
            pltpu.VMEM((cells, cells), BF16),
            pltpu.VMEM((cells, cells), BF16),
            pltpu.VMEM((cells, cells), BF16),
            pltpu.VMEM((cells, cells), BF16),
            pltpu.VMEM((128, 1024), BF16),
            pltpu.VMEM((128, 128), BF16),
            pltpu.VMEM((1024, 128), BF16),
            pltpu.VMEM((4, KL, wide, 2 * XL, cells), BF16),
            pltpu.VMEM((4, KL, wide, 2 * XL, cells), BF16),
            pltpu.VMEM((4, KL, narrow, 3 * YL, 128), BF16),
            pltpu.VMEM((4, KL, narrow, 3 * YL, 128), BF16),
            pltpu.SemaphoreType.DMA((4, KL)),
            pltpu.SemaphoreType.DMA((4, KL)),
            pltpu.SemaphoreType.DMA((4, KL)),
            pltpu.SemaphoreType.DMA((4, KL)),
            pltpu.SemaphoreType.DMA((6,)),
            pltpu.SemaphoreType.DMA((4,)),
        ],
        compiler_params=pltpu.CompilerParams(
            collective_id=0, has_side_effects=True, vmem_limit_bytes=VMEM_BYTES
        ),
        name="spectral_layer",
    )(field, cot, weight, pw, table)
    act, wgrad, fgrad = pl.pallas_call(
        functools.partial(finish, kk),
        out_shape=(grid_like, weight_like, grid_like),
        in_specs=[hbm] * 5,
        out_specs=(hbm,) * 3,
        scratch_shapes=[
            pltpu.VMEM((4, kk * XL, 128), BF16),
            pltpu.VMEM((XL, cells, NZ), F32),
            pltpu.VMEM((kk, NZ), BF16),
            pltpu.VMEM((4, kk * XL, 128), F32),
            pltpu.VMEM(field.shape, BF16),
            pltpu.VMEM(field.shape, BF16),
            pltpu.VMEM(weight.shape, BF16),
            pltpu.SemaphoreType.DMA((21,)),
        ],
        compiler_params=pltpu.CompilerParams(vmem_limit_bytes=VMEM_BYTES),
        name="field_gradient",
    )(*parts, table)
    return act, fgrad, wgrad


def solution(mesh):
    wide, narrow = mesh.shape["wide"], mesh.shape["narrow"]
    return jax.shard_map(
        functools.partial(on_device, wide, narrow),
        mesh=mesh,
        in_specs=(
            P(None, "wide", "narrow", None),
            P("wide", "narrow", None, None),
            P(),
            P(None, "wide", "narrow", None),
        ),
        out_specs=(
            P(None, "wide", "narrow", None),
            P(None, "wide", "narrow", None),
            P("wide", "narrow", None, None),
        ),
        check_vma=False,
    )
```

```python
import functools

import jax
import jax.numpy as jnp
import ml_dtypes
import numpy as np
from jax import lax
from jax.experimental import pallas as pl
from jax.experimental.pallas import tpu as pltpu
from jax.sharding import PartitionSpec as P

C = 32
XL = 8
YL = 16
KXL = 6
KL = 3
HALVES = 2
NZ = 128
VMEM_BYTES = 64 * 1024 * 1024
MESH = pl.DeviceIdType.MESH
F32 = jnp.float32
BF16 = jnp.bfloat16


def angles(extent, kept, two_sided):
    positions = np.arange(kept)
    frequency = (
        np.where(positions < kept // 2, positions, positions + extent - kept)
        if two_sided
        else positions
    )
    phases = np.arange(extent)[:, None] * frequency[None, :] % extent
    theta = 2.0 * np.pi * phases / extent
    rounded = lambda t: t.astype(np.float32).astype(ml_dtypes.bfloat16).astype(np.float32)
    return rounded(np.cos(theta)), rounded(np.sin(theta))


def tables(wide, narrow, ky):
    nx, ny, kx, kz = XL * wide, YL * narrow, KXL * narrow, KL * wide
    cx, sx = angles(nx, kx, True)
    cy, sy = angles(ny, ky, True)
    cz, sz = angles(NZ, kz, False)
    v = wide // HALVES
    z_rows = np.stack([cz, -sz], axis=-1).reshape(NZ, HALVES, v, KL, 2)
    z_fwd = z_rows.transpose(3, 2, 1, 4, 0).reshape(KL * wide * 2, NZ)
    fwd = lambda c, s: np.stack([np.stack([c, s]), np.stack([-s, c])])
    inv = lambda c, s: np.stack([np.stack([c, -s]), np.stack([s, c])])
    fx = fwd(cx, sx).reshape(2, 2, HALVES, v, XL, narrow, KXL)
    x_fwd = fx.transpose(2, 6, 0, 5, 3, 1, 4).reshape(HALVES * KXL * 2 * narrow, v * 2 * XL)
    ix = inv(cx, sx).reshape(2, 2, wide, XL, narrow, KXL)
    x_inv = ix.transpose(2, 0, 3, 5, 1, 4).reshape(wide * 2 * XL, KXL * 2 * narrow)
    fy = fwd(cy, sy).reshape(2, 2, narrow, YL, ky)
    y_fwd = fy.transpose(0, 4, 2, 1, 3).reshape(2 * ky, narrow * 2 * YL)
    y_fwd_split = fy.transpose(1, 0, 4, 2, 3).reshape(4 * ky, narrow * YL)
    iy = inv(cy, sy).reshape(2, 2, narrow, YL, ky)
    y_inv = iy.transpose(2, 0, 3, 1, 4).reshape(narrow * 2 * YL, 2 * ky)
    y_inv_split = iy.transpose(0, 2, 3, 1, 4).reshape(2 * narrow * YL, 2 * ky)
    found = (z_fwd, x_fwd, x_inv, y_fwd, y_fwd_split, y_inv, y_inv_split)
    places, blocks, row = [], [], 0
    for t in found:
        rows, columns = t.shape
        places.append((row, rows, columns))
        for first in range(0, columns, 128):
            block = t[:, first : first + 128]
            blocks.append(np.pad(block, ((0, 0), (0, 128 - block.shape[1]))))
            row += rows
    return places, np.concatenate(blocks).astype(ml_dtypes.bfloat16)


def read_table(table, place):
    row, rows, columns = place
    blocks = [
        table[row + i * rows : row + (i + 1) * rows, : min(128, columns - first)]
        for i, first in enumerate(range(0, columns, 128))
    ]
    return jnp.concatenate(blocks, axis=1) if len(blocks) > 1 else blocks[0]


def dot(a, b, dims=((1,), (0,))):
    return lax.dot_general(a, b, (dims, ((), ())), preferred_element_type=F32)


def ones_where(condition):
    return jnp.where(condition, 1.0, 0.0).astype(BF16)


def kernel(
    wide, narrow, ky, total, places,
    field_hbm, cot_hbm, weight_hbm, pw_hbm, table_hbm,
    act_hbm, wgrad_hbm, back_hbm, near_hbm,
    *scratch,
):
    (
        table, field, cot, weight, pw, act, wgrad, zi, near, back_rows, zs, slope, spec, sums, prods, mix, t1, t1_last, t2,
        perm, perm_t, pw_fwd, pw_back, repeat, tile, group_sum,
        ws, wr, ns, nr,
        ws_sem, wr_sem, ns_sem, nr_sem, load_sem, store_sem,
    ) = scratch
    w = lax.axis_index("wide")
    n = lax.axis_index("narrow")
    cells = C * YL
    kk = KL * wide * 2
    rows_j = wide * 2 * XL
    modes = KXL * 2 * ky

    z_fwd, x_fwd, x_inv, y_fwd, y_fwd_split, y_inv, y_inv_split = [
        functools.partial(read_table, table, place) for place in places
    ]
    z_part = pl.ds(0, kk)
    other = pl.ds(kk, table.shape[0] - kk)
    loads = [
        pltpu.make_async_copy(src, dst, load_sem.at[i])
        for i, (src, dst) in enumerate(
            (
                (field_hbm, field),
                (table_hbm.at[z_part], table.at[z_part]),
                (pw_hbm, pw),
                (table_hbm.at[other], table.at[other]),
                (cot_hbm, cot),
                (weight_hbm, weight),
            )
        )
    ]
    for load in loads:
        load.start()

    side = wide // HALVES
    h, v = w // side, lax.rem(w, side)
    plane = HALVES * narrow
    here = h * narrow + n

    barrier = pltpu.get_barrier_semaphore()

    def along(d):
        to = lax.rem(v + d, side)
        return to, {"wide": h * side + to}

    def across(d):
        to = lax.rem(here + d, plane)
        return to, {"wide": to // narrow * side + v, "narrow": lax.rem(to, narrow)}

    for count, peer in ((side, along), (plane, across)):
        for d in range(1, count):
            pl.semaphore_signal(barrier, inc=1, device_id=peer(d)[1], device_id_type=MESH)

    row = lax.broadcasted_iota(jnp.int32, (cells, cells), 0)
    col = lax.broadcasted_iota(jnp.int32, (cells, cells), 1)
    perm[...] = ones_where(((row & 15) == (col >> 5)) & ((row >> 4) == (col & 31)))

    lane = lax.broadcasted_iota(jnp.int32, (1, 128), 1) >> 5

    def shift(value, groups):
        amount = (groups * 32) % 128
        return value if amount == 0 else pltpu.roll(value, amount, 1)

    def pick(pieces):
        acc = pieces[0]
        for s, piece in enumerate(pieces[1:], 1):
            acc = jnp.where(lane == s, piece, acc)
        return acc

    def depth(x, b, block):
        out = dot(z_fwd(), block, ((1,), (1,)))
        zs[b, pl.ds(x, kk, stride=XL), :] = out

    def send(peer, count, src, dst, slot, send_sem, recv_sem, take=lambda to: to):
        for d in range(1, count):
            to, device = peer(d)
            pltpu.make_async_remote_copy(
                src_ref=src.at[take(to)],
                dst_ref=dst.at[slot],
                send_sem=send_sem,
                recv_sem=recv_sem,
                device_id=device,
                device_id_type=MESH,
            ).start()

    def send_wide(a, j):
        wr[a, j, v] = ws[a, j, v]
        send(along, side, ws.at[a, j], wr.at[a, j], v, ws_sem.at[a, j], wr_sem.at[a, j])

    def send_narrow(a, j, take):
        nr[a, j, here] = ns[a, j, take(here)]
        send(across, plane, ns.at[a, j], nr.at[a, j], here, ns_sem.at[a, j], nr_sem.at[a, j], take)

    def wait_all(buffer, a, j, sem, count):
        ref = buffer.at[a, j, pl.ds(0, count)]
        pltpu.make_async_copy(ref, ref, sem.at[a, j]).wait()

    def part(j):
        return pl.ds(pl.multiple_of(j * rows_j, rows_j), rows_j)

    def depth_out(a):
        @pl.loop(0, KL)
        def _(j):
            block = jnp.concatenate([zs[b, part(j), :].astype(BF16) for b in range(4)], axis=1)
            ws[a, j] = dot(block, perm[...]).astype(BF16).reshape(side, HALVES * 2 * XL, cells)
            send_wide(a, j)

    def x_forward(a, j):
        wait_all(wr, a, j, wr_sem, side - 1)
        first, rows, columns = places[1]
        rows = rows // HALVES
        matrix = table[pl.ds(first + h * rows, rows), :columns]
        for to_h in range(HALVES):
            part_rows = slice(to_h * 2 * XL, (to_h + 1) * 2 * XL)
            out = dot(matrix, wr[a, j, :, part_rows, :].reshape(side * 2 * XL, cells))
            for y in range(YL):
                yb, g = y // 4, y % 4

                def piece(kx, ri):
                    first = (kx * 2 + ri) * narrow
                    return out[first : first + narrow, yb * 128 : (yb + 1) * 128]

                for ri in range(2):
                    t1[pl.ds(ri * YL + y, narrow, stride=2 * YL), :] = pick(
                        [shift(piece(s, ri), s - g) for s in range(4)]
                    )
                t1_last[pl.ds(y, narrow, stride=YL), :] = pick(
                    [shift(piece(4 + s % 2, s // 2), s - g) for s in range(4)]
                )
            owners = slice(to_h * narrow, (to_h + 1) * narrow)
            ns[a, j, owners, : 2 * YL, :] = t1[...].astype(BF16).reshape(narrow, 2 * YL, 128)
            ns[a, j, owners, 2 * YL :, :] = t1_last[...].astype(BF16).reshape(narrow, YL, 128)
        send_narrow(a, j, lambda to: to)

    def y_forward(a, j, which):
        wait_all(nr, a, j, nr_sem, plane - 1)
        halves = [slice(i * narrow, (i + 1) * narrow) for i in range(HALVES)]
        first, both = (
            sum(dot(matrix, nr[a, j, i, lines, :].reshape(-1, 128)) for i in halves)
            for matrix, lines in ((y_fwd(), slice(0, 2 * YL)), (y_fwd_split(), slice(2 * YL, None)))
        )
        last = both[: 2 * ky] + shift(both[2 * ky :], 2)
        for kx in range(KXL):
            source = first if kx < 4 else last
            spec[which, j, kx * 2 * ky : (kx + 1) * 2 * ky, :] = shift(source, -(kx % 4)).astype(BF16)

    def scale(j):
        return jnp.where(w * KL + j == 0, 1.0, 2.0).astype(F32) / total

    def weights(j, kx, b):
        return (
            weight[j, kx, :, b * 256 : (b + 1) * 256].astype(F32),
            weight[j, kx, :, 1024 + b * 256 : 1024 + (b + 1) * 256].astype(F32),
        )

    def mode_rows(kx):
        return slice(kx * 2 * ky, kx * 2 * ky + ky), slice(kx * 2 * ky + ky, (kx + 1) * 2 * ky)

    def place(summed):
        for lb in range(2):
            found = [
                summed[kx * 2 * ky : (kx + 1) * 2 * ky] for kx in range(4 * lb, min(4 * lb + 4, KXL))
            ]
            mix[lb] = pick(found).astype(BF16)

    def mix_forward(j):
        for b in range(4):
            rep = dot(spec[0, j], repeat[:, b * 256 : (b + 1) * 256])
            for kx in range(KXL):
                re, im = mode_rows(kx)
                w_r, w_i = weights(j, kx, b)
                p_r = rep[re] * w_r - rep[im] * w_i
                p_i = rep[re] * w_i + rep[im] * w_r
                p_r = p_r[:, :128] + p_r[:, 128:]
                p_i = p_i[:, :128] + p_i[:, 128:]
                sums[re, :] = p_r if b == 0 else sums[re, :] + p_r
                sums[im, :] = p_i if b == 0 else sums[im, :] + p_i
        acc = sums[...] * scale(j)
        acc = acc + shift(acc, 2)
        acc = acc + shift(acc, 1)
        place(acc)

    def mix_back(j):
        sums[...] = dot(spec[1, j], tile[...])
        for kx in range(KXL):
            re, im = mode_rows(kx)
            g_r = jnp.concatenate([sums[re, :]] * 2, axis=1)
            g_i = jnp.concatenate([sums[im, :]] * 2, axis=1)
            for b in range(4):
                w_r, w_i = weights(j, kx, b)
                lanes = slice(b * 256, (b + 1) * 256)
                prods[re, lanes] = (w_r * g_r + w_i * g_i).astype(BF16)
                prods[im, lanes] = (w_r * g_i - w_i * g_r).astype(BF16)
        place(dot(prods[...], group_sum[...]) * scale(j))

    def weight_gradient(j):
        sums[...] = dot(spec[1, j], tile[...]) * scale(j)
        for b in range(4):
            rep = dot(spec[0, j], repeat[:, b * 256 : (b + 1) * 256])
            for kx in range(KXL):
                re, im = mode_rows(kx)
                g_r = jnp.concatenate([sums[re, :]] * 2, axis=1)
                g_i = jnp.concatenate([sums[im, :]] * 2, axis=1)
                wgrad[j, kx, :, b * 256 : (b + 1) * 256] = (rep[re] * g_r + rep[im] * g_i).astype(BF16)
                wgrad[j, kx, :, 1024 + b * 256 : 1024 + (b + 1) * 256] = (
                    rep[re] * g_i - rep[im] * g_r
                ).astype(BF16)

    def y_inverse(a, j):
        first = dot(y_inv(), mix[0]).astype(BF16)
        ns[a, j, :narrow, : 2 * YL, :] = first.reshape(narrow, 2 * YL, 128)
        both = dot(y_inv_split(), mix[1])
        split = narrow * YL
        last = jnp.where(lane < 2, both[:split], shift(both[split:], 2)).astype(BF16)
        ns[a, j, :narrow, 2 * YL :, :] = last.reshape(narrow, YL, 128)
        send_narrow(a, j, lambda to: lax.rem(to, narrow))

    def x_inverse(a, j):
        wait_all(nr, a, j, nr_sem, plane - 1)
        first, rows, columns = places[2]
        rows = rows // HALVES
        matrix = table[pl.ds(first + h * rows, rows), :columns]
        for from_h in range(HALVES):
            owners = slice(from_h * narrow, (from_h + 1) * narrow)
            t1[...] = nr[a, j, owners, : 2 * YL, :].reshape(narrow * 2 * YL, 128).astype(F32)
            t1_last[...] = nr[a, j, owners, 2 * YL :, :].reshape(narrow * YL, 128).astype(F32)
            for yb in range(4):
                lanes = slice(yb * 128, (yb + 1) * 128)
                ys = [4 * yb + g for g in range(4)]
                loaded = [
                    [t1[pl.ds(ri * YL + y, narrow, stride=2 * YL), :] for y in ys] for ri in range(2)
                ]
                last = [t1_last[pl.ds(y, narrow, stride=YL), :] for y in ys]
                for kx in range(KXL):
                    both = []
                    for ri in range(2):
                        source = loaded[ri] if kx < 4 else last
                        s = kx if kx < 4 else ri * 2 + kx - 4
                        both.append(pick([shift(source[g], g - s) for g in range(4)]))
                    t2[kx * 2 * narrow : (kx + 1) * 2 * narrow, lanes] = jnp.concatenate(
                        both, axis=0
                    ).astype(BF16)
            out = dot(matrix, t2[...]).astype(BF16)
            part_rows = slice(from_h * 2 * XL, (from_h + 1) * 2 * XL)
            ws[a, j, :, part_rows, :] = out.reshape(side, 2 * XL, cells)
        send_wide(a, j)

    def through_modes(back):
        @pl.loop(0, KL + 2)
        def _(t):
            @pl.when(t < KL)
            def _():
                x_forward(2 * back, t)

            @pl.when((t >= 1) & (t <= KL))
            def _():
                y_forward(2 * back, t - 1, back)
                mix_back(t - 1) if back else mix_forward(t - 1)
                y_inverse(2 * back + 1, t - 1)

            @pl.when(t >= 2)
            def _():
                x_inverse(2 * back + 1, t - 2)

    def depth_in(a):
        @pl.loop(0, KL)
        def _(j):
            wait_all(wr, a, j, wr_sem, side - 1)
            out = dot(wr[a, j].reshape(rows_j, cells), perm_t[...])
            for b in range(4):
                block = out[:, b * 128 : (b + 1) * 128]
                if a == 1:
                    zi[b, part(j), :] = block
                else:
                    back_rows[b, part(j), :] = block.astype(BF16)

    def pointwise(matrix, source):
        @pl.loop(0, XL)
        def _(x):
            near[x] = dot(matrix[...], source[:, x].reshape(cells, NZ))

    loads[0].wait()
    loads[1].wait()
    for x in range(XL):
        slab = field[:, x].reshape(cells, NZ)
        for b in range(4):
            depth(x, b, slab[b * 128 : (b + 1) * 128])

    pl.semaphore_wait(barrier, side + plane - 2)
    depth_out(0)

    loads[2].wait()
    loads[3].wait()
    perm_t[...] = ones_where(((row >> 5) == (col & 15)) & ((row & 31) == (col >> 4)))
    spread_row = lax.broadcasted_iota(jnp.int32, (cells, C), 0)
    spread_col = lax.broadcasted_iota(jnp.int32, (cells, C), 1)
    spread = ones_where((spread_row >> 4) == spread_col)
    same_y = (row & 15) == (col & 15)
    behind = dot(dot(spread, pw[...]).astype(BF16), spread, ((1,), (1,)))
    pw_back[...] = jnp.where(same_y, behind, 0.0).astype(BF16)
    ahead = dot(dot(spread, pw[...], ((1,), (1,))).astype(BF16), spread, ((1,), (1,)))
    pw_fwd[...] = jnp.where(same_y, ahead, 0.0).astype(BF16)
    r_row = lax.broadcasted_iota(jnp.int32, (128, 1024), 0)
    r_col = lax.broadcasted_iota(jnp.int32, (128, 1024), 1)
    repeat[...] = ones_where(r_row == (r_col >> 5))
    t_row = lax.broadcasted_iota(jnp.int32, (128, 128), 0)
    t_col = lax.broadcasted_iota(jnp.int32, (128, 128), 1)
    tile[...] = ones_where(t_row == (t_col & 31))
    g_row = lax.broadcasted_iota(jnp.int32, (1024, 128), 0)
    g_col = lax.broadcasted_iota(jnp.int32, (1024, 128), 1)
    group_sum[...] = ones_where((g_row >> 5) == (g_col & 31))
    pointwise(pw_fwd, field)
    loads[4].wait()
    loads[5].wait()

    through_modes(0)
    depth_in(1)

    root = 0.7978845608028654

    @pl.loop(0, 4)
    def _(b):
        rows = pl.ds(pl.multiple_of(b * 128, 128), 128)
        group = pl.ds(b * 8, 8)
        for x in range(XL):
            block = zi[b, pl.ds(x, kk, stride=XL), :].astype(BF16)
            t = dot(block, z_fwd(), ((0,), (0,))) + near[x, rows, :]
            square = t * t
            th = jnp.tanh(root * t * (1.0 + 0.044715 * square))
            gate = 0.5 + 0.5 * th
            act[group, x] = (t * gate).astype(BF16).reshape(8, YL, NZ)
            grad = gate + (0.5 * root) * t * (1.0 - th * th) * (1.0 + 0.134145 * square)
            up = cot[group, x].reshape(128, NZ).astype(F32)
            block = (up * grad).astype(BF16)
            slope[group, x] = block.reshape(8, YL, NZ)
            depth(x, b, block)

    depth_out(2)
    stores = [
        pltpu.make_async_copy(src, dst, store_sem.at[i])
        for i, (src, dst) in enumerate(
            ((act, act_hbm), (near, near_hbm), (wgrad, wgrad_hbm), (back_rows, back_hbm))
        )
    ]
    stores[0].start()
    pointwise(pw_back, slope)
    stores[1].start()
    through_modes(1)
    pl.loop(0, KL)(weight_gradient)
    stores[2].start()
    depth_in(3)
    stores[3].start()

    @pl.loop(0, 4)
    def _(a):
        @pl.loop(0, KL)
        def _(j):
            wait_all(ws, a, j, ws_sem, side - 1)
            wait_all(ns, a, j, ns_sem, plane - 1)

    for store in stores:
        store.wait()


def finish(
    kk, act_in, wgrad_in, back_hbm, near_hbm, table_hbm,
    act_hbm, wgrad_hbm, fgrad_hbm,
    back, near, table, zi, fgrad, act, wgrad, sem,
):
    load_table = pltpu.make_async_copy(table_hbm.at[pl.ds(0, kk)], table, sem.at[0])
    load_table.start()
    loads, passed, stores = [], [], []
    for b in range(4):
        rows = pl.ds(b * 128, 128)
        loads.append(
            (
                pltpu.make_async_copy(back_hbm.at[b], back.at[b], sem.at[1 + b]),
                pltpu.make_async_copy(near_hbm.at[:, rows], near.at[:, rows], sem.at[5 + b]),
            )
        )
        for load in loads[-1]:
            load.start()
    whole = [(act_in, act, act_hbm)] + [
        (wgrad_in.at[j], wgrad.at[j], wgrad_hbm.at[j]) for j in range(KL)
    ]
    for i, (src, held, dst) in enumerate(whole):
        passed.append(
            (
                pltpu.make_async_copy(src, held, sem.at[9 + i]),
                pltpu.make_async_copy(held, dst, sem.at[13 + i]),
            )
        )
        passed[-1][0].start()
    load_table.wait()
    for b in range(4):
        for load in loads[b]:
            load.wait()
        zi[b] = back[b].astype(F32)
        for x in range(XL):
            block = zi[b, pl.ds(x, kk, stride=XL), :].astype(BF16)
            t = dot(block, table[...], ((0,), (0,))) + near[x, b * 128 : (b + 1) * 128, :]
            fgrad[b * 8 : (b + 1) * 8, x] = t.astype(BF16).reshape(8, YL, NZ)
        group = pl.ds(b * 8, 8)
        stores.append(pltpu.make_async_copy(fgrad.at[group], fgrad_hbm.at[group], sem.at[17 + b]))
        stores[-1].start()
        passed[b][0].wait()
        passed[b][1].start()
        stores.append(passed[b][1])
    for store in stores:
        store.wait()


def on_device(wide, narrow, field, weight, pw, cot):
    ky = weight.shape[2]
    total = float(XL * wide * YL * narrow * NZ)
    places, packed = tables(wide, narrow, ky)
    table = jnp.asarray(packed)
    cells = C * YL
    kk = KL * wide * 2
    modes = KXL * 2 * ky
    side, plane = wide // HALVES, narrow * HALVES
    hbm = pl.BlockSpec(memory_space=pl.ANY)
    grid_like = jax.ShapeDtypeStruct(field.shape, BF16)
    weight_like = jax.ShapeDtypeStruct(weight.shape, BF16)
    parts = pl.pallas_call(
        functools.partial(kernel, wide, narrow, ky, total, places),
        out_shape=(
            grid_like,
            weight_like,
            jax.ShapeDtypeStruct((4, kk * XL, 128), BF16),
            jax.ShapeDtypeStruct((XL, cells, NZ), F32),
        ),
        in_specs=[hbm] * 5,
        out_specs=(hbm,) * 4,
        scratch_shapes=[
            pltpu.VMEM(table.shape, BF16),
            pltpu.VMEM(field.shape, BF16),
            pltpu.VMEM(cot.shape, BF16),
            pltpu.VMEM(weight.shape, BF16),
            pltpu.VMEM(pw.shape, BF16),
            pltpu.VMEM(field.shape, BF16),
            pltpu.VMEM(weight.shape, BF16),
            pltpu.VMEM((4, kk * XL, 128), F32),
            pltpu.VMEM((XL, cells, NZ), F32),
            pltpu.VMEM((4, kk * XL, 128), BF16),
            pltpu.VMEM((4, kk * XL, 128), F32),
            pltpu.VMEM(field.shape, BF16),
            pltpu.VMEM((2, KL, modes, 128), BF16),
            pltpu.VMEM((modes, 128), F32),
            pltpu.VMEM((modes, 1024), BF16),
            pltpu.VMEM((2, 2 * ky, 128), BF16),
            pltpu.VMEM((narrow * 2 * YL, 128), F32),
            pltpu.VMEM((narrow * YL, 128), F32),
            pltpu.VMEM((KXL * narrow * 2, cells), BF16),
            pltpu.VMEM((cells, cells), BF16),
            pltpu.VMEM((cells, cells), BF16),
            pltpu.VMEM((cells, cells), BF16),
            pltpu.VMEM((cells, cells), BF16),
            pltpu.VMEM((128, 1024), BF16),
            pltpu.VMEM((128, 128), BF16),
            pltpu.VMEM((1024, 128), BF16),
            pltpu.VMEM((4, KL, side, HALVES * 2 * XL, cells), BF16),
            pltpu.VMEM((4, KL, side, HALVES * 2 * XL, cells), BF16),
            pltpu.VMEM((4, KL, plane, 3 * YL, 128), BF16),
            pltpu.VMEM((4, KL, plane, 3 * YL, 128), BF16),
            pltpu.SemaphoreType.DMA((4, KL)),
            pltpu.SemaphoreType.DMA((4, KL)),
            pltpu.SemaphoreType.DMA((4, KL)),
            pltpu.SemaphoreType.DMA((4, KL)),
            pltpu.SemaphoreType.DMA((6,)),
            pltpu.SemaphoreType.DMA((4,)),
        ],
        compiler_params=pltpu.CompilerParams(
            collective_id=0, has_side_effects=True, vmem_limit_bytes=VMEM_BYTES
        ),
        name="spectral_layer",
    )(field, cot, weight, pw, table)
    act, wgrad, fgrad = pl.pallas_call(
        functools.partial(finish, kk),
        out_shape=(grid_like, weight_like, grid_like),
        in_specs=[hbm] * 5,
        out_specs=(hbm,) * 3,
        scratch_shapes=[
            pltpu.VMEM((4, kk * XL, 128), BF16),
            pltpu.VMEM((XL, cells, NZ), F32),
            pltpu.VMEM((kk, NZ), BF16),
            pltpu.VMEM((4, kk * XL, 128), F32),
            pltpu.VMEM(field.shape, BF16),
            pltpu.VMEM(field.shape, BF16),
            pltpu.VMEM(weight.shape, BF16),
            pltpu.SemaphoreType.DMA((21,)),
        ],
        compiler_params=pltpu.CompilerParams(vmem_limit_bytes=VMEM_BYTES),
        name="field_gradient",
    )(*parts, table)
    return act, fgrad, wgrad


def solution(mesh):
    wide, narrow = mesh.shape["wide"], mesh.shape["narrow"]
    return jax.shard_map(
        functools.partial(on_device, wide, narrow),
        mesh=mesh,
        in_specs=(
            P(None, "wide", "narrow", None),
            P("wide", "narrow", None, None),
            P(),
            P(None, "wide", "narrow", None),
        ),
        out_specs=(
            P(None, "wide", "narrow", None),
            P(None, "wide", "narrow", None),
            P("wide", "narrow", None, None),
        ),
        check_vma=False,
    )
```

```python
import functools

import jax
import jax.numpy as jnp
import ml_dtypes
import numpy as np
from jax import lax
from jax.experimental import pallas as pl
from jax.experimental.pallas import tpu as pltpu
from jax.sharding import PartitionSpec as P

C = 32
XL = 8
YL = 16
KXL = 6
KL = 3
NZ = 128
VMEM_BYTES = 64 * 1024 * 1024
MESH = pl.DeviceIdType.MESH
F32 = jnp.float32
BF16 = jnp.bfloat16


def angles(extent, kept, two_sided):
    positions = np.arange(kept)
    frequency = (
        np.where(positions < kept // 2, positions, positions + extent - kept)
        if two_sided
        else positions
    )
    phases = np.arange(extent)[:, None] * frequency[None, :] % extent
    theta = 2.0 * np.pi * phases / extent
    rounded = lambda t: t.astype(np.float32).astype(ml_dtypes.bfloat16).astype(np.float32)
    return rounded(np.cos(theta)), rounded(np.sin(theta))


def tables(wide, narrow, ky):
    nx, ny, kx, kz = XL * wide, YL * narrow, KXL * narrow, KL * wide
    cx, sx = angles(nx, kx, True)
    cy, sy = angles(ny, ky, True)
    cz, sz = angles(NZ, kz, False)
    z_rows = np.stack([cz, -sz], axis=-1).reshape(NZ, wide, KL, 2)
    z_fwd = z_rows.transpose(2, 1, 3, 0).reshape(KL * wide * 2, NZ)
    fwd = lambda c, s: np.stack([np.stack([c, s]), np.stack([-s, c])])
    inv = lambda c, s: np.stack([np.stack([c, -s]), np.stack([s, c])])
    fx = fwd(cx, sx).reshape(2, 2, wide, XL, narrow, KXL)
    x_fwd = fx.transpose(5, 0, 4, 2, 1, 3).reshape(KXL * 2 * narrow, wide * 2 * XL)
    ix = inv(cx, sx).reshape(2, 2, wide, XL, narrow, KXL)
    x_inv = ix.transpose(2, 0, 3, 5, 1, 4).reshape(wide * 2 * XL, KXL * 2 * narrow)
    fy = fwd(cy, sy).reshape(2, 2, narrow, YL, ky)
    y_fwd = fy.transpose(0, 4, 2, 1, 3).reshape(2 * ky, narrow * 2 * YL)
    y_fwd_split = fy.transpose(1, 0, 4, 2, 3).reshape(4 * ky, narrow * YL)
    iy = inv(cy, sy).reshape(2, 2, narrow, YL, ky)
    y_inv = iy.transpose(2, 0, 3, 1, 4).reshape(narrow * 2 * YL, 2 * ky)
    y_inv_split = iy.transpose(0, 2, 3, 1, 4).reshape(2 * narrow * YL, 2 * ky)
    found = (z_fwd, x_fwd, x_inv, y_fwd, y_fwd_split, y_inv, y_inv_split)
    places, blocks, row = [], [], 0
    for t in found:
        rows, columns = t.shape
        places.append((row, rows, columns))
        for first in range(0, columns, 128):
            block = t[:, first : first + 128]
            blocks.append(np.pad(block, ((0, 0), (0, 128 - block.shape[1]))))
            row += rows
    return places, np.concatenate(blocks).astype(ml_dtypes.bfloat16)


def read_table(table, place):
    row, rows, columns = place
    blocks = [
        table[row + i * rows : row + (i + 1) * rows, : min(128, columns - first)]
        for i, first in enumerate(range(0, columns, 128))
    ]
    return jnp.concatenate(blocks, axis=1) if len(blocks) > 1 else blocks[0]


def dot(a, b, dims=((1,), (0,))):
    return lax.dot_general(a, b, (dims, ((), ())), preferred_element_type=F32)


def ones_where(condition):
    return jnp.where(condition, 1.0, 0.0).astype(BF16)


def kernel(
    wide, narrow, ky, total, places,
    field_hbm, cot_hbm, weight_hbm, pw_hbm, table_hbm,
    act_hbm, wgrad_hbm, back_hbm, near_hbm,
    *scratch,
):
    (
        table, field, cot, weight, pw, act, wgrad, zi, near, back_rows, zs, slope, spec, sums, prods, mix, t1, t1_last, t2,
        perm, perm_t, pw_fwd, pw_back, repeat, tile, group_sum,
        ws, wr, ns, nr,
        ws_sem, wr_sem, ns_sem, nr_sem, early_sem, load_sem, store_sem,
    ) = scratch
    w = lax.axis_index("wide")
    n = lax.axis_index("narrow")
    cells = C * YL
    kk = KL * wide * 2
    rows_j = wide * 2 * XL
    modes = KXL * 2 * ky

    z_fwd, x_fwd, x_inv, y_fwd, y_fwd_split, y_inv, y_inv_split = [
        functools.partial(read_table, table, place) for place in places
    ]
    z_part = pl.ds(0, kk)
    other = pl.ds(kk, table.shape[0] - kk)
    loads = [
        pltpu.make_async_copy(src, dst, load_sem.at[i])
        for i, (src, dst) in enumerate(
            (
                (field_hbm.at[pl.ds(0, C // 2)], field.at[pl.ds(0, C // 2)]),
                (table_hbm.at[z_part], table.at[z_part]),
                (field_hbm.at[pl.ds(C // 2, C // 2)], field.at[pl.ds(C // 2, C // 2)]),
                (pw_hbm, pw),
                (table_hbm.at[other], table.at[other]),
                (cot_hbm, cot),
                (weight_hbm, weight),
            )
        )
    ]
    for load in loads:
        load.start()

    barrier = pltpu.get_barrier_semaphore()

    half = narrow // 2
    flip = lax.rem(n + half, narrow)

    @pl.loop(0, wide)
    def _(d):
        pl.semaphore_signal(
            barrier, inc=1, device_id={"wide": d, "narrow": flip}, device_id_type=MESH
        )

    @pl.loop(1, narrow)
    def _(d):
        pl.semaphore_signal(
            barrier, inc=1, device_id={"narrow": lax.rem(n + d, narrow)}, device_id_type=MESH
        )

    row = lax.broadcasted_iota(jnp.int32, (cells, cells), 0)
    col = lax.broadcasted_iota(jnp.int32, (cells, cells), 1)
    lane = lax.broadcasted_iota(jnp.int32, (1, 128), 1) >> 5

    def shift(value, groups):
        amount = (groups * 32) % 128
        return value if amount == 0 else pltpu.roll(value, amount, 1)

    def pick(pieces):
        acc = pieces[0]
        for s, piece in enumerate(pieces[1:], 1):
            acc = jnp.where(lane == s, piece, acc)
        return acc

    def exchange(low, high, groups, first):
        return (
            jnp.where(first, low, shift(high, groups)),
            jnp.where(first, shift(low, -groups), high),
        )

    def transpose_groups(p):
        p0, p2 = exchange(p[0], p[2], 2, lane < 2)
        p1, p3 = exchange(p[1], p[3], 2, lane < 2)
        p0, p1 = exchange(p0, p1, 1, (lane & 1) == 0)
        p2, p3 = exchange(p2, p3, 1, (lane & 1) == 0)
        return [p0, p1, p2, p3]

    def depth(x, hb, block):
        out = dot(z_fwd(), block, ((1,), (1,)))
        for i in range(2):
            zs[2 * hb + i, pl.ds(x, kk, stride=XL), :] = out[:, i * 128 : (i + 1) * 128]

    def wide_copy(src, dst, to, send_sem, recv_sem):
        pltpu.make_async_remote_copy(
            src_ref=src,
            dst_ref=dst,
            send_sem=send_sem,
            recv_sem=recv_sem,
            device_id={"wide": to, "narrow": flip},
            device_id_type=MESH,
        ).start()

    def send_wide(a, j, first=0, lanes=C * YL):
        @pl.loop(0, wide)
        def _(d):
            to = lax.rem(w + d, wide)
            window = (pl.ds(0, 2 * XL), pl.ds(first, lanes))
            wide_copy(
                ws.at[(a, j, to) + window], wr.at[(a, j, w) + window], to,
                ws_sem.at[a, j], wr_sem.at[a, j],
            )

    early = (pl.ds(0, KL), pl.ds(0, wide), pl.ds(0, 2 * XL), pl.ds(0, 256))

    def send_early(a):
        @pl.loop(0, wide)
        def _(d):
            to = lax.rem(w + d, wide)
            window = (pl.ds(0, 2 * XL), pl.ds(0, 256))
            wide_copy(
                ws.at[(a, pl.ds(0, KL), to) + window], wr.at[(a, pl.ds(0, KL), w) + window], to,
                early_sem.at[0, a // 2], early_sem.at[1, a // 2],
            )

    def wait_early(buffer, a, which):
        ref = buffer.at[(a,) + early]
        pltpu.make_async_copy(ref, ref, early_sem.at[which, a // 2]).wait()

    def wait_late(buffer, a, j, sem):
        ref = buffer.at[a, j, pl.ds(0, wide), pl.ds(0, 2 * XL), pl.ds(256, 256)]
        pltpu.make_async_copy(ref, ref, sem.at[a, j]).wait()

    def send_narrow(a, j, take, slot):
        nr[a, j, slot] = ns[a, j, take(n)]

        @pl.loop(1, narrow)
        def _(d):
            to = lax.rem(n + d, narrow)
            pltpu.make_async_remote_copy(
                src_ref=ns.at[a, j, take(to)],
                dst_ref=nr.at[a, j, slot],
                send_sem=ns_sem.at[a, j],
                recv_sem=nr_sem.at[a, j],
                device_id={"narrow": to},
                device_id_type=MESH,
            ).start()

    def wait_all(buffer, a, j, sem, count):
        ref = buffer.at[a, j, pl.ds(0, count)]
        pltpu.make_async_copy(ref, ref, sem.at[a, j]).wait()

    def part(j):
        return pl.ds(pl.multiple_of(j * rows_j, rows_j), rows_j)

    def pack(a, j, b):
        block = zs[b, part(j), :].astype(BF16).reshape(wide, 2 * XL, 128)
        ws[a, j, :, :, b * 128 : (b + 1) * 128] = block

    def depth_out_early(a):
        @pl.loop(0, KL)
        def _(j):
            pack(a, j, 0)
            pack(a, j, 1)

        send_early(a)

    def depth_out_late(a):
        @pl.loop(0, KL)
        def _(j):
            pack(a, j, 2)
            pack(a, j, 3)
            send_wide(a, j, 256, 256)

    def x_forward(a, j):
        wait_late(wr, a, j, wr_sem)
        out = dot(x_fwd(), wr[a, j].reshape(rows_j, cells))
        out = dot(out.astype(BF16), perm[...])
        for yb in range(4):

            def piece(kx, ri):
                first = (kx * 2 + ri) * narrow
                return out[first : first + narrow, yb * 128 : (yb + 1) * 128]

            for ri in range(2):
                for g, value in enumerate(transpose_groups([piece(s, ri) for s in range(4)])):
                    t1[pl.ds(ri * YL + 4 * yb + g, narrow, stride=2 * YL), :] = value
            last = transpose_groups([piece(4 + s % 2, s // 2) for s in range(4)])
            for g, value in enumerate(last):
                t1_last[pl.ds(4 * yb + g, narrow, stride=YL), :] = value
        ns[a, j, :, : 2 * YL, :] = t1[...].astype(BF16).reshape(narrow, 2 * YL, 128)
        ns[a, j, :, 2 * YL :, :] = t1_last[...].astype(BF16).reshape(narrow, YL, 128)
        send_narrow(a, j, lambda to: to, flip)

    def y_forward(a, j, which):
        wait_all(nr, a, j, nr_sem, narrow - 1)
        first = dot(y_fwd(), nr[a, j, :, : 2 * YL, :].reshape(narrow * 2 * YL, 128))
        both = dot(y_fwd_split(), nr[a, j, :, 2 * YL :, :].reshape(narrow * YL, 128))
        last = both[: 2 * ky] + shift(both[2 * ky :], 2)
        for kx in range(KXL):
            source = first if kx < 4 else last
            spec[which, j, kx * 2 * ky : (kx + 1) * 2 * ky, :] = shift(source, -(kx % 4)).astype(BF16)

    def scale(j):
        return jnp.where(w * KL + j == 0, 1.0, 2.0).astype(F32) / total

    def weights(j, kx, b):
        return (
            weight[j, kx, :, b * 256 : (b + 1) * 256].astype(F32),
            weight[j, kx, :, 1024 + b * 256 : 1024 + (b + 1) * 256].astype(F32),
        )

    def mode_rows(kx):
        return slice(kx * 2 * ky, kx * 2 * ky + ky), slice(kx * 2 * ky + ky, (kx + 1) * 2 * ky)

    def place(summed):
        for lb in range(2):
            found = [
                summed[kx * 2 * ky : (kx + 1) * 2 * ky] for kx in range(4 * lb, min(4 * lb + 4, KXL))
            ]
            mix[lb] = pick(found).astype(BF16)

    def mix_forward(j):
        for b in range(4):
            rep = dot(spec[0, j], repeat[:, b * 256 : (b + 1) * 256])
            for kx in range(KXL):
                re, im = mode_rows(kx)
                w_r, w_i = weights(j, kx, b)
                p_r = rep[re] * w_r - rep[im] * w_i
                p_i = rep[re] * w_i + rep[im] * w_r
                p_r = p_r[:, :128] + p_r[:, 128:]
                p_i = p_i[:, :128] + p_i[:, 128:]
                sums[re, :] = p_r if b == 0 else sums[re, :] + p_r
                sums[im, :] = p_i if b == 0 else sums[im, :] + p_i
        acc = sums[...] * scale(j)
        acc = acc + shift(acc, 2)
        acc = acc + shift(acc, 1)
        place(acc)

    def mix_back(j):
        sums[...] = dot(spec[1, j], tile[...])
        for kx in range(KXL):
            re, im = mode_rows(kx)
            g_r = jnp.concatenate([sums[re, :]] * 2, axis=1)
            g_i = jnp.concatenate([sums[im, :]] * 2, axis=1)
            for b in range(4):
                w_r, w_i = weights(j, kx, b)
                lanes = slice(b * 256, (b + 1) * 256)
                prods[re, lanes] = (w_r * g_r + w_i * g_i).astype(BF16)
                prods[im, lanes] = (w_r * g_i - w_i * g_r).astype(BF16)
        place(dot(prods[...], group_sum[...]) * scale(j))

    def weight_gradient(j):
        sums[...] = dot(spec[1, j], tile[...]) * scale(j)
        for b in range(4):
            rep = dot(spec[0, j], repeat[:, b * 256 : (b + 1) * 256])
            for kx in range(KXL):
                re, im = mode_rows(kx)
                g_r = jnp.concatenate([sums[re, :]] * 2, axis=1)
                g_i = jnp.concatenate([sums[im, :]] * 2, axis=1)
                wgrad[j, kx, :, b * 256 : (b + 1) * 256] = (rep[re] * g_r + rep[im] * g_i).astype(BF16)
                wgrad[j, kx, :, 1024 + b * 256 : 1024 + (b + 1) * 256] = (
                    rep[re] * g_i - rep[im] * g_r
                ).astype(BF16)

    def y_inverse(a, j):
        first = dot(y_inv(), mix[0]).astype(BF16)
        ns[a, j, :, : 2 * YL, :] = first.reshape(narrow, 2 * YL, 128)
        both = dot(y_inv_split(), mix[1])
        split = narrow * YL
        last = jnp.where(lane < 2, both[:split], shift(both[split:], 2)).astype(BF16)
        ns[a, j, :, 2 * YL :, :] = last.reshape(narrow, YL, 128)
        send_narrow(a, j, lambda to: lax.rem(to + half, narrow), n)

    def x_inverse(a, j):
        wait_all(nr, a, j, nr_sem, narrow - 1)
        t1[...] = nr[a, j, :, : 2 * YL, :].reshape(narrow * 2 * YL, 128).astype(F32)
        t1_last[...] = nr[a, j, :, 2 * YL :, :].reshape(narrow * YL, 128).astype(F32)
        for yb in range(4):
            lanes = slice(yb * 128, (yb + 1) * 128)
            ys = [4 * yb + g for g in range(4)]
            loaded = [
                [t1[pl.ds(ri * YL + y, narrow, stride=2 * YL), :] for y in ys] for ri in range(2)
            ]
            last = [t1_last[pl.ds(y, narrow, stride=YL), :] for y in ys]
            real, imag, last = [transpose_groups(p) for p in loaded + [last]]
            pairs = list(zip(real, imag)) + [(last[0], last[2]), (last[1], last[3])]
            for kx, pair in enumerate(pairs):
                t2[kx * 2 * narrow : (kx + 1) * 2 * narrow, lanes] = jnp.concatenate(
                    pair, axis=0
                ).astype(BF16)
        modes_cy = dot(t2[...], perm_t[...]).astype(BF16)
        ws[a, j] = dot(x_inv(), modes_cy).astype(BF16).reshape(wide, 2 * XL, cells)
        send_wide(a, j)

    def through_modes(back):
        wait_early(wr, 2 * back, 1)

        @pl.loop(0, KL + 2)
        def _(t):
            @pl.when(t < KL)
            def _():
                x_forward(2 * back, t)

            @pl.when((t >= 1) & (t <= KL))
            def _():
                y_forward(2 * back, t - 1, back)
                mix_back(t - 1) if back else mix_forward(t - 1)
                y_inverse(2 * back + 1, t - 1)

            @pl.when(t >= 2)
            def _():
                x_inverse(2 * back + 1, t - 2)

    def depth_in(a):
        @pl.loop(0, KL)
        def _(j):
            wait_all(wr, a, j, wr_sem, wide)
            for b in range(4):
                block = wr[a, j, :, :, b * 128 : (b + 1) * 128].reshape(rows_j, 128)
                if a == 1:
                    zi[b, part(j), :] = block.astype(F32)
                else:
                    back_rows[b, part(j), :] = block

    def pointwise(matrix, source):
        @pl.loop(0, XL // 2)
        def _(x):
            both = [source[:, 2 * x + i].reshape(cells, NZ) for i in range(2)]
            out = dot(matrix[...], jnp.concatenate(both, axis=1))
            for i in range(2):
                near[2 * x + i] = out[:, i * NZ : (i + 1) * NZ]

    loads[1].wait()
    for hb in range(2):
        loads[2 * hb].wait()
        for x in range(XL):
            depth(x, hb, field[hb * 16 : (hb + 1) * 16, x].reshape(256, NZ))
        if hb == 0:
            pl.semaphore_wait(barrier, wide + narrow - 1)
            depth_out_early(0)
    depth_out_late(0)

    loads[3].wait()
    loads[4].wait()
    perm[...] = ones_where(((row & 15) == (col >> 5)) & ((row >> 4) == (col & 31)))
    perm_t[...] = ones_where(((row >> 5) == (col & 15)) & ((row & 31) == (col >> 4)))
    spread_row = lax.broadcasted_iota(jnp.int32, (cells, C), 0)
    spread_col = lax.broadcasted_iota(jnp.int32, (cells, C), 1)
    spread = ones_where((spread_row >> 4) == spread_col)
    same_y = (row & 15) == (col & 15)
    behind = dot(dot(spread, pw[...]).astype(BF16), spread, ((1,), (1,)))
    pw_back[...] = jnp.where(same_y, behind, 0.0).astype(BF16)
    ahead = dot(dot(spread, pw[...], ((1,), (1,))).astype(BF16), spread, ((1,), (1,)))
    pw_fwd[...] = jnp.where(same_y, ahead, 0.0).astype(BF16)
    r_row = lax.broadcasted_iota(jnp.int32, (128, 1024), 0)
    r_col = lax.broadcasted_iota(jnp.int32, (128, 1024), 1)
    repeat[...] = ones_where(r_row == (r_col >> 5))
    t_row = lax.broadcasted_iota(jnp.int32, (128, 128), 0)
    t_col = lax.broadcasted_iota(jnp.int32, (128, 128), 1)
    tile[...] = ones_where(t_row == (t_col & 31))
    g_row = lax.broadcasted_iota(jnp.int32, (1024, 128), 0)
    g_col = lax.broadcasted_iota(jnp.int32, (1024, 128), 1)
    group_sum[...] = ones_where((g_row >> 5) == (g_col & 31))
    pointwise(pw_fwd, field)
    loads[5].wait()
    loads[6].wait()

    through_modes(0)
    depth_in(1)

    root = 0.7978845608028654

    @pl.loop(0, 2)
    def _(hb):
        rows = pl.ds(pl.multiple_of(hb * 256, 256), 256)
        group = pl.ds(hb * 16, 16)
        for x in range(XL):
            block = jnp.concatenate(
                [zi[2 * hb + i, pl.ds(x, kk, stride=XL), :].astype(BF16) for i in range(2)], axis=1
            )
            t = dot(block, z_fwd(), ((0,), (0,))) + near[x, rows, :]
            square = t * t
            gate = 0.5 + 0.5 * jnp.tanh(t * (root + (root * 0.044715) * square))
            out = t * gate
            act[group, x] = out.astype(BF16).reshape(16, YL, NZ)
            grad = gate + out * (1.0 - gate) * (2.0 * root + (6.0 * root * 0.044715) * square)
            up = cot[group, x].reshape(256, NZ).astype(F32)
            block = (up * grad).astype(BF16)
            slope[group, x] = block.reshape(16, YL, NZ)
            depth(x, hb, block)

        @pl.when(hb == 0)
        def _():
            depth_out_early(2)

    depth_out_late(2)
    stores = [
        pltpu.make_async_copy(src, dst, store_sem.at[i])
        for i, (src, dst) in enumerate(
            ((act, act_hbm), (near, near_hbm), (wgrad, wgrad_hbm), (back_rows, back_hbm))
        )
    ]
    stores[0].start()
    pointwise(pw_back, slope)
    stores[1].start()
    through_modes(1)
    pl.loop(0, KL)(weight_gradient)
    stores[2].start()
    depth_in(3)
    stores[3].start()

    @pl.loop(0, 4)
    def _(a):
        @pl.loop(0, KL)
        def _(j):
            wait_all(ns, a, j, ns_sem, narrow - 1)

    for a in (0, 2):
        wait_early(ws, a, 0)

        @pl.loop(0, KL)
        def _(j):
            wait_late(ws, a, j, ws_sem)
            wait_all(ws, a + 1, j, ws_sem, wide)

    for store in stores:
        store.wait()


def finish(
    kk, act_in, wgrad_in, back_hbm, near_hbm, table_hbm,
    act_hbm, wgrad_hbm, fgrad_hbm,
    back, near, table, zi, fgrad, act, wgrad, sem,
):
    load_table = pltpu.make_async_copy(table_hbm.at[pl.ds(0, kk)], table, sem.at[0])
    load_table.start()
    loads, passed, stores = [], [], []
    for b in range(4):
        rows = pl.ds(b * 128, 128)
        loads.append(
            (
                pltpu.make_async_copy(back_hbm.at[b], back.at[b], sem.at[1 + b]),
                pltpu.make_async_copy(near_hbm.at[:, rows], near.at[:, rows], sem.at[5 + b]),
            )
        )
        for load in loads[-1]:
            load.start()
    whole = [(act_in, act, act_hbm)] + [
        (wgrad_in.at[j], wgrad.at[j], wgrad_hbm.at[j]) for j in range(KL)
    ]
    for i, (src, held, dst) in enumerate(whole):
        passed.append(
            (
                pltpu.make_async_copy(src, held, sem.at[9 + i]),
                pltpu.make_async_copy(held, dst, sem.at[13 + i]),
            )
        )
        passed[-1][0].start()
    load_table.wait()
    for hb in range(2):
        for b in (2 * hb, 2 * hb + 1):
            for load in loads[b]:
                load.wait()
            zi[b] = back[b].astype(F32)
        for x in range(XL):
            block = jnp.concatenate(
                [zi[2 * hb + i, pl.ds(x, kk, stride=XL), :].astype(BF16) for i in range(2)], axis=1
            )
            rows = slice(hb * 256, (hb + 1) * 256)
            t = dot(block, table[...], ((0,), (0,))) + near[x, rows, :]
            fgrad[hb * 16 : (hb + 1) * 16, x] = t.astype(BF16).reshape(16, YL, NZ)
        group = pl.ds(hb * 16, 16)
        stores.append(pltpu.make_async_copy(fgrad.at[group], fgrad_hbm.at[group], sem.at[17 + hb]))
        stores[-1].start()
        for i in (2 * hb, 2 * hb + 1):
            passed[i][0].wait()
            passed[i][1].start()
            stores.append(passed[i][1])
    for store in stores:
        store.wait()


def on_device(wide, narrow, field, weight, pw, cot):
    ky = weight.shape[2]
    total = float(XL * wide * YL * narrow * NZ)
    places, packed = tables(wide, narrow, ky)
    table = jnp.asarray(packed)
    cells = C * YL
    kk = KL * wide * 2
    modes = KXL * 2 * ky
    hbm = pl.BlockSpec(memory_space=pl.ANY)
    grid_like = jax.ShapeDtypeStruct(field.shape, BF16)
    weight_like = jax.ShapeDtypeStruct(weight.shape, BF16)
    parts = pl.pallas_call(
        functools.partial(kernel, wide, narrow, ky, total, places),
        out_shape=(
            grid_like,
            weight_like,
            jax.ShapeDtypeStruct((4, kk * XL, 128), BF16),
            jax.ShapeDtypeStruct((XL, cells, NZ), F32),
        ),
        in_specs=[hbm] * 5,
        out_specs=(hbm,) * 4,
        scratch_shapes=[
            pltpu.VMEM(table.shape, BF16),
            pltpu.VMEM(field.shape, BF16),
            pltpu.VMEM(cot.shape, BF16),
            pltpu.VMEM(weight.shape, BF16),
            pltpu.VMEM(pw.shape, BF16),
            pltpu.VMEM(field.shape, BF16),
            pltpu.VMEM(weight.shape, BF16),
            pltpu.VMEM((4, kk * XL, 128), F32),
            pltpu.VMEM((XL, cells, NZ), F32),
            pltpu.VMEM((4, kk * XL, 128), BF16),
            pltpu.VMEM((4, kk * XL, 128), F32),
            pltpu.VMEM(field.shape, BF16),
            pltpu.VMEM((2, KL, modes, 128), BF16),
            pltpu.VMEM((modes, 128), F32),
            pltpu.VMEM((modes, 1024), BF16),
            pltpu.VMEM((2, 2 * ky, 128), BF16),
            pltpu.VMEM((narrow * 2 * YL, 128), F32),
            pltpu.VMEM((narrow * YL, 128), F32),
            pltpu.VMEM((KXL * narrow * 2, cells), BF16),
            pltpu.VMEM((cells, cells), BF16),
            pltpu.VMEM((cells, cells), BF16),
            pltpu.VMEM((cells, cells), BF16),
            pltpu.VMEM((cells, cells), BF16),
            pltpu.VMEM((128, 1024), BF16),
            pltpu.VMEM((128, 128), BF16),
            pltpu.VMEM((1024, 128), BF16),
            pltpu.VMEM((4, KL, wide, 2 * XL, cells), BF16),
            pltpu.VMEM((4, KL, wide, 2 * XL, cells), BF16),
            pltpu.VMEM((4, KL, narrow, 3 * YL, 128), BF16),
            pltpu.VMEM((4, KL, narrow, 3 * YL, 128), BF16),
            pltpu.SemaphoreType.DMA((4, KL)),
            pltpu.SemaphoreType.DMA((4, KL)),
            pltpu.SemaphoreType.DMA((4, KL)),
            pltpu.SemaphoreType.DMA((4, KL)),
            pltpu.SemaphoreType.DMA((2, 2)),
            pltpu.SemaphoreType.DMA((7,)),
            pltpu.SemaphoreType.DMA((4,)),
        ],
        compiler_params=pltpu.CompilerParams(
            collective_id=0, has_side_effects=True, vmem_limit_bytes=VMEM_BYTES
        ),
        name="spectral_layer",
    )(field, cot, weight, pw, table)
    act, wgrad, fgrad = pl.pallas_call(
        functools.partial(finish, kk),
        out_shape=(grid_like, weight_like, grid_like),
        in_specs=[hbm] * 5,
        out_specs=(hbm,) * 3,
        scratch_shapes=[
            pltpu.VMEM((4, kk * XL, 128), BF16),
            pltpu.VMEM((XL, cells, NZ), F32),
            pltpu.VMEM((kk, NZ), BF16),
            pltpu.VMEM((4, kk * XL, 128), F32),
            pltpu.VMEM(field.shape, BF16),
            pltpu.VMEM(field.shape, BF16),
            pltpu.VMEM(weight.shape, BF16),
            pltpu.SemaphoreType.DMA((21,)),
        ],
        compiler_params=pltpu.CompilerParams(vmem_limit_bytes=VMEM_BYTES),
        name="field_gradient",
    )(*parts, table)
    return act, fgrad, wgrad


def solution(mesh):
    wide, narrow = mesh.shape["wide"], mesh.shape["narrow"]
    return jax.shard_map(
        functools.partial(on_device, wide, narrow),
        mesh=mesh,
        in_specs=(
            P(None, "wide", "narrow", None),
            P("wide", "narrow", None, None),
            P(),
            P(None, "wide", "narrow", None),
        ),
        out_specs=(
            P(None, "wide", "narrow", None),
            P(None, "wide", "narrow", None),
            P("wide", "narrow", None, None),
        ),
        check_vma=False,
    )
```

```python
import functools

import jax
import jax.numpy as jnp
import ml_dtypes
import numpy as np
from jax import lax
from jax.experimental import pallas as pl
from jax.experimental.pallas import tpu as pltpu
from jax.sharding import PartitionSpec as P

C = 32
XL = 8
YL = 16
KXL = 6
KL = 3
NZ = 128
VMEM_BYTES = 64 * 1024 * 1024
MESH = pl.DeviceIdType.MESH
F32 = jnp.float32
BF16 = jnp.bfloat16


def angles(extent, kept, two_sided):
    positions = np.arange(kept)
    frequency = (
        np.where(positions < kept // 2, positions, positions + extent - kept)
        if two_sided
        else positions
    )
    phases = np.arange(extent)[:, None] * frequency[None, :] % extent
    theta = 2.0 * np.pi * phases / extent
    rounded = lambda t: t.astype(np.float32).astype(ml_dtypes.bfloat16).astype(np.float32)
    return rounded(np.cos(theta)), rounded(np.sin(theta))


def tables(wide, narrow, ky):
    nx, ny, kx, kz = XL * wide, YL * narrow, KXL * narrow, KL * wide
    cx, sx = angles(nx, kx, True)
    cy, sy = angles(ny, ky, True)
    cz, sz = angles(NZ, kz, False)
    z_rows = np.stack([cz, -sz], axis=-1).reshape(NZ, wide, KL, 2)
    z_fwd = z_rows.transpose(2, 1, 3, 0).reshape(KL * wide * 2, NZ)
    fwd = lambda c, s: np.stack([np.stack([c, s]), np.stack([-s, c])])
    inv = lambda c, s: np.stack([np.stack([c, -s]), np.stack([s, c])])
    fx = fwd(cx, sx).reshape(2, 2, wide, XL, narrow, KXL)
    x_fwd = fx.transpose(5, 0, 4, 2, 1, 3).reshape(KXL * 2 * narrow, wide * 2 * XL)
    ix = inv(cx, sx).reshape(2, 2, wide, XL, narrow, KXL)
    x_inv = ix.transpose(2, 0, 3, 5, 1, 4).reshape(wide * 2 * XL, KXL * 2 * narrow)
    fy = fwd(cy, sy).reshape(2, 2, narrow, YL, ky)
    y_fwd = fy.transpose(0, 4, 2, 1, 3).reshape(2 * ky, narrow * 2 * YL)
    y_fwd_split = fy.transpose(1, 0, 4, 2, 3).reshape(4 * ky, narrow * YL)
    iy = inv(cy, sy).reshape(2, 2, narrow, YL, ky)
    y_inv = iy.transpose(2, 0, 3, 1, 4).reshape(narrow * 2 * YL, 2 * ky)
    y_inv_split = iy.transpose(0, 2, 3, 1, 4).reshape(2 * narrow * YL, 2 * ky)
    found = (z_fwd, x_fwd, x_inv, y_fwd, y_fwd_split, y_inv, y_inv_split)
    places, blocks, row = [], [], 0
    for t in found:
        rows, columns = t.shape
        places.append((row, rows, columns))
        for first in range(0, columns, 128):
            block = t[:, first : first + 128]
            blocks.append(np.pad(block, ((0, 0), (0, 128 - block.shape[1]))))
            row += rows
    return places, np.concatenate(blocks).astype(ml_dtypes.bfloat16)


def read_table(table, place):
    row, rows, columns = place
    blocks = [
        table[row + i * rows : row + (i + 1) * rows, : min(128, columns - first)]
        for i, first in enumerate(range(0, columns, 128))
    ]
    return jnp.concatenate(blocks, axis=1) if len(blocks) > 1 else blocks[0]


def dot(a, b, dims=((1,), (0,))):
    return lax.dot_general(a, b, (dims, ((), ())), preferred_element_type=F32)


def ones_where(condition):
    return jnp.where(condition, 1.0, 0.0).astype(BF16)


def kernel(
    wide, narrow, ky, total, places,
    field_hbm, cot_hbm, weight_hbm, pw_hbm, table_hbm,
    act_hbm, wgrad_hbm, back_hbm, near_hbm,
    *scratch,
):
    (
        table, field, cot, weight, pw, act, wgrad, zi, near, back_rows, zs, slope, spec, sums, prods, mix, t1, t1_last, t2,
        perm, perm_t, pw_fwd, pw_back, repeat, tile, group_sum,
        ws, wr, ns, nr,
        ws_sem, wr_sem, ns_sem, nr_sem, load_sem, store_sem,
    ) = scratch
    w = lax.axis_index("wide")
    n = lax.axis_index("narrow")
    cells = C * YL
    kk = KL * wide * 2
    rows_j = wide * 2 * XL
    modes = KXL * 2 * ky

    z_fwd, x_fwd, x_inv, y_fwd, y_fwd_split, y_inv, y_inv_split = [
        functools.partial(read_table, table, place) for place in places
    ]
    z_part = pl.ds(0, kk)
    other = pl.ds(kk, table.shape[0] - kk)
    loads = [
        pltpu.make_async_copy(src, dst, load_sem.at[i])
        for i, (src, dst) in enumerate(
            (
                (field_hbm.at[pl.ds(0, C // 2)], field.at[pl.ds(0, C // 2)]),
                (table_hbm.at[z_part], table.at[z_part]),
                (field_hbm.at[pl.ds(C // 2, C // 2)], field.at[pl.ds(C // 2, C // 2)]),
                (pw_hbm, pw),
                (table_hbm.at[other], table.at[other]),
                (cot_hbm, cot),
                (weight_hbm, weight),
            )
        )
    ]
    for load in loads:
        load.start()

    barrier = pltpu.get_barrier_semaphore()

    half = narrow // 2
    flip = lax.rem(n + half, narrow)

    @pl.loop(0, wide)
    def _(d):
        pl.semaphore_signal(
            barrier, inc=1, device_id={"wide": d, "narrow": flip}, device_id_type=MESH
        )

    @pl.loop(1, narrow)
    def _(d):
        pl.semaphore_signal(
            barrier, inc=1, device_id={"narrow": lax.rem(n + d, narrow)}, device_id_type=MESH
        )

    row = lax.broadcasted_iota(jnp.int32, (cells, cells), 0)
    col = lax.broadcasted_iota(jnp.int32, (cells, cells), 1)
    lane = lax.broadcasted_iota(jnp.int32, (1, 128), 1) >> 5

    def shift(value, groups):
        amount = (groups * 32) % 128
        return value if amount == 0 else pltpu.roll(value, amount, 1)

    def pick(pieces):
        acc = pieces[0]
        for s, piece in enumerate(pieces[1:], 1):
            acc = jnp.where(lane == s, piece, acc)
        return acc

    def exchange(low, high, groups, first):
        return (
            jnp.where(first, low, shift(high, groups)),
            jnp.where(first, shift(low, -groups), high),
        )

    def transpose_groups(p):
        p0, p2 = exchange(p[0], p[2], 2, lane < 2)
        p1, p3 = exchange(p[1], p[3], 2, lane < 2)
        p0, p1 = exchange(p0, p1, 1, (lane & 1) == 0)
        p2, p3 = exchange(p2, p3, 1, (lane & 1) == 0)
        return [p0, p1, p2, p3]

    def depth(x, hb, block):
        out = dot(z_fwd(), block, ((1,), (1,)))
        for i in range(2):
            zs[2 * hb + i, pl.ds(x, kk, stride=XL), :] = out[:, i * 128 : (i + 1) * 128]

    def send_wide(a, hb=None):
        at = lambda ref, i: ref.at[a, i] if hb is None else ref.at[a, i, hb]

        @pl.loop(0, wide)
        def _(d):
            to = lax.rem(w + d, wide)
            pltpu.make_async_remote_copy(
                src_ref=at(ws, to),
                dst_ref=at(wr, w),
                send_sem=ws_sem.at[a, hb or 0],
                recv_sem=wr_sem.at[a, hb or 0],
                device_id={"wide": to, "narrow": flip},
                device_id_type=MESH,
            ).start()

    def wait_wide(buffer, sem, a, hb=None):
        ref = buffer.at[a] if hb is None else buffer.at[a, pl.ds(0, wide), hb]
        pltpu.make_async_copy(ref, ref, sem.at[a, hb or 0]).wait()

    def send_narrow(a, take, slot):
        nr[a, slot] = ns[a, take(n)]

        @pl.loop(1, narrow)
        def _(d):
            to = lax.rem(n + d, narrow)
            pltpu.make_async_remote_copy(
                src_ref=ns.at[a, take(to)],
                dst_ref=nr.at[a, slot],
                send_sem=ns_sem.at[a],
                recv_sem=nr_sem.at[a],
                device_id={"narrow": to},
                device_id_type=MESH,
            ).start()

    def wait_narrow(buffer, sem, a):
        ref = buffer.at[a, pl.ds(0, narrow - 1)]
        pltpu.make_async_copy(ref, ref, sem.at[a]).wait()

    def part(j):
        return pl.ds(pl.multiple_of(j * rows_j, rows_j), rows_j)

    def depth_out(a, hb):
        @pl.loop(0, KL)
        def _(j):
            for i in range(2):
                block = zs[2 * hb + i, part(j), :].astype(BF16).reshape(wide, 2 * XL, 128)
                ws[a, :, hb, j, :, i * 128 : (i + 1) * 128] = block

        send_wide(a, hb)

    def x_forward(a, j):
        block = [wr[a, :, hb, j].reshape(rows_j, 256) for hb in range(2)]
        out = dot(x_fwd(), jnp.concatenate(block, axis=1))
        out = dot(out.astype(BF16), perm[...])
        for yb in range(4):

            def piece(kx, ri):
                first = (kx * 2 + ri) * narrow
                return out[first : first + narrow, yb * 128 : (yb + 1) * 128]

            for ri in range(2):
                for g, value in enumerate(transpose_groups([piece(s, ri) for s in range(4)])):
                    t1[pl.ds(ri * YL + 4 * yb + g, narrow, stride=2 * YL), :] = value
            last = transpose_groups([piece(4 + s % 2, s // 2) for s in range(4)])
            for g, value in enumerate(last):
                t1_last[pl.ds(4 * yb + g, narrow, stride=YL), :] = value
        ns[a, :, j, : 2 * YL, :] = t1[...].astype(BF16).reshape(narrow, 2 * YL, 128)
        ns[a, :, j, 2 * YL :, :] = t1_last[...].astype(BF16).reshape(narrow, YL, 128)

    def y_forward(a, j, which):
        first = dot(y_fwd(), nr[a, :, j, : 2 * YL, :].reshape(narrow * 2 * YL, 128))
        both = dot(y_fwd_split(), nr[a, :, j, 2 * YL :, :].reshape(narrow * YL, 128))
        last = both[: 2 * ky] + shift(both[2 * ky :], 2)
        for kx in range(KXL):
            source = first if kx < 4 else last
            spec[which, j, kx * 2 * ky : (kx + 1) * 2 * ky, :] = shift(source, -(kx % 4)).astype(BF16)

    def scale(j):
        return jnp.where(w * KL + j == 0, 1.0, 2.0).astype(F32) / total

    def weights(j, kx, b):
        return (
            weight[j, kx, :, b * 256 : (b + 1) * 256].astype(F32),
            weight[j, kx, :, 1024 + b * 256 : 1024 + (b + 1) * 256].astype(F32),
        )

    def mode_rows(kx):
        return slice(kx * 2 * ky, kx * 2 * ky + ky), slice(kx * 2 * ky + ky, (kx + 1) * 2 * ky)

    def place(summed):
        for lb in range(2):
            found = [
                summed[kx * 2 * ky : (kx + 1) * 2 * ky] for kx in range(4 * lb, min(4 * lb + 4, KXL))
            ]
            mix[lb] = pick(found).astype(BF16)

    def mix_forward(j):
        for b in range(4):
            rep = dot(spec[0, j], repeat[:, b * 256 : (b + 1) * 256])
            for kx in range(KXL):
                re, im = mode_rows(kx)
                w_r, w_i = weights(j, kx, b)
                p_r = rep[re] * w_r - rep[im] * w_i
                p_i = rep[re] * w_i + rep[im] * w_r
                p_r = p_r[:, :128] + p_r[:, 128:]
                p_i = p_i[:, :128] + p_i[:, 128:]
                sums[re, :] = p_r if b == 0 else sums[re, :] + p_r
                sums[im, :] = p_i if b == 0 else sums[im, :] + p_i
        acc = sums[...] * scale(j)
        acc = acc + shift(acc, 2)
        acc = acc + shift(acc, 1)
        place(acc)

    def mix_back(j):
        sums[...] = dot(spec[1, j], tile[...])
        for kx in range(KXL):
            re, im = mode_rows(kx)
            g_r = jnp.concatenate([sums[re, :]] * 2, axis=1)
            g_i = jnp.concatenate([sums[im, :]] * 2, axis=1)
            for b in range(4):
                w_r, w_i = weights(j, kx, b)
                lanes = slice(b * 256, (b + 1) * 256)
                prods[re, lanes] = (w_r * g_r + w_i * g_i).astype(BF16)
                prods[im, lanes] = (w_r * g_i - w_i * g_r).astype(BF16)
        place(dot(prods[...], group_sum[...]) * scale(j))

    def weight_gradient(j):
        sums[...] = dot(spec[1, j], tile[...]) * scale(j)
        for b in range(4):
            rep = dot(spec[0, j], repeat[:, b * 256 : (b + 1) * 256])
            for kx in range(KXL):
                re, im = mode_rows(kx)
                g_r = jnp.concatenate([sums[re, :]] * 2, axis=1)
                g_i = jnp.concatenate([sums[im, :]] * 2, axis=1)
                wgrad[j, kx, :, b * 256 : (b + 1) * 256] = (rep[re] * g_r + rep[im] * g_i).astype(BF16)
                wgrad[j, kx, :, 1024 + b * 256 : 1024 + (b + 1) * 256] = (
                    rep[re] * g_i - rep[im] * g_r
                ).astype(BF16)

    def y_inverse(a, j):
        first = dot(y_inv(), mix[0]).astype(BF16)
        ns[a, :, j, : 2 * YL, :] = first.reshape(narrow, 2 * YL, 128)
        both = dot(y_inv_split(), mix[1])
        split = narrow * YL
        last = jnp.where(lane < 2, both[:split], shift(both[split:], 2)).astype(BF16)
        ns[a, :, j, 2 * YL :, :] = last.reshape(narrow, YL, 128)

    def x_inverse(a, j):
        t1[...] = nr[a, :, j, : 2 * YL, :].reshape(narrow * 2 * YL, 128).astype(F32)
        t1_last[...] = nr[a, :, j, 2 * YL :, :].reshape(narrow * YL, 128).astype(F32)
        for yb in range(4):
            lanes = slice(yb * 128, (yb + 1) * 128)
            ys = [4 * yb + g for g in range(4)]
            loaded = [
                [t1[pl.ds(ri * YL + y, narrow, stride=2 * YL), :] for y in ys] for ri in range(2)
            ]
            last = [t1_last[pl.ds(y, narrow, stride=YL), :] for y in ys]
            real, imag, last = [transpose_groups(p) for p in loaded + [last]]
            pairs = list(zip(real, imag)) + [(last[0], last[2]), (last[1], last[3])]
            for kx, pair in enumerate(pairs):
                t2[kx * 2 * narrow : (kx + 1) * 2 * narrow, lanes] = jnp.concatenate(
                    pair, axis=0
                ).astype(BF16)
        modes_cy = dot(t2[...], perm_t[...]).astype(BF16)
        out = dot(x_inv(), modes_cy).astype(BF16)
        for hb in range(2):
            ws[a, :, hb, j] = out[:, hb * 256 : (hb + 1) * 256].reshape(wide, 2 * XL, 256)

    def each(step):
        @pl.loop(0, KL)
        def _(j):
            step(j)

    def through_modes(back):
        first, second = 2 * back, 2 * back + 1

        def mode_step(j):
            y_forward(first, j, back)
            mix_back(j) if back else mix_forward(j)
            y_inverse(second, j)

        for hb in range(2):
            wait_wide(wr, wr_sem, first, hb)
        each(lambda j: x_forward(first, j))
        send_narrow(first, lambda to: to, flip)
        wait_narrow(nr, nr_sem, first)
        each(mode_step)
        send_narrow(second, lambda to: lax.rem(to + half, narrow), n)
        if back:
            weight_gradient(0)
        wait_narrow(nr, nr_sem, second)
        each(lambda j: x_inverse(second, j))
        send_wide(second)
        if back:
            pl.loop(1, KL)(weight_gradient)

    def depth_in(a):
        wait_wide(wr, wr_sem, a)

        @pl.loop(0, KL)
        def _(j):
            for b in range(4):
                hb, i = b // 2, b % 2
                block = wr[a, :, hb, j, :, i * 128 : (i + 1) * 128].reshape(rows_j, 128)
                if a == 1:
                    zi[b, part(j), :] = block.astype(F32)
                else:
                    back_rows[b, part(j), :] = block

    def pointwise(matrix, source):
        @pl.loop(0, XL // 2)
        def _(x):
            both = [source[:, 2 * x + i].reshape(cells, NZ) for i in range(2)]
            out = dot(matrix[...], jnp.concatenate(both, axis=1))
            for i in range(2):
                near[2 * x + i] = out[:, i * NZ : (i + 1) * NZ]

    loads[1].wait()
    for hb in range(2):
        loads[2 * hb].wait()
        for x in range(XL):
            depth(x, hb, field[hb * 16 : (hb + 1) * 16, x].reshape(256, NZ))
        if hb == 0:
            pl.semaphore_wait(barrier, wide + narrow - 1)
        depth_out(0, hb)

    loads[3].wait()
    loads[4].wait()
    perm[...] = ones_where(((row & 15) == (col >> 5)) & ((row >> 4) == (col & 31)))
    perm_t[...] = ones_where(((row >> 5) == (col & 15)) & ((row & 31) == (col >> 4)))
    spread_row = lax.broadcasted_iota(jnp.int32, (cells, C), 0)
    spread_col = lax.broadcasted_iota(jnp.int32, (cells, C), 1)
    spread = ones_where((spread_row >> 4) == spread_col)
    same_y = (row & 15) == (col & 15)
    behind = dot(dot(spread, pw[...]).astype(BF16), spread, ((1,), (1,)))
    pw_back[...] = jnp.where(same_y, behind, 0.0).astype(BF16)
    ahead = dot(dot(spread, pw[...], ((1,), (1,))).astype(BF16), spread, ((1,), (1,)))
    pw_fwd[...] = jnp.where(same_y, ahead, 0.0).astype(BF16)
    r_row = lax.broadcasted_iota(jnp.int32, (128, 1024), 0)
    r_col = lax.broadcasted_iota(jnp.int32, (128, 1024), 1)
    repeat[...] = ones_where(r_row == (r_col >> 5))
    t_row = lax.broadcasted_iota(jnp.int32, (128, 128), 0)
    t_col = lax.broadcasted_iota(jnp.int32, (128, 128), 1)
    tile[...] = ones_where(t_row == (t_col & 31))
    g_row = lax.broadcasted_iota(jnp.int32, (1024, 128), 0)
    g_col = lax.broadcasted_iota(jnp.int32, (1024, 128), 1)
    group_sum[...] = ones_where((g_row >> 5) == (g_col & 31))
    pointwise(pw_fwd, field)
    loads[5].wait()
    loads[6].wait()

    through_modes(0)
    depth_in(1)

    root = 0.7978845608028654

    @pl.loop(0, 2)
    def _(hb):
        rows = pl.ds(pl.multiple_of(hb * 256, 256), 256)
        group = pl.ds(hb * 16, 16)
        for x in range(XL):
            block = jnp.concatenate(
                [zi[2 * hb + i, pl.ds(x, kk, stride=XL), :].astype(BF16) for i in range(2)], axis=1
            )
            t = dot(block, z_fwd(), ((0,), (0,))) + near[x, rows, :]
            square = t * t
            gate = 0.5 + 0.5 * jnp.tanh(t * (root + (root * 0.044715) * square))
            out = t * gate
            act[group, x] = out.astype(BF16).reshape(16, YL, NZ)
            grad = gate + out * (1.0 - gate) * (2.0 * root + (6.0 * root * 0.044715) * square)
            up = cot[group, x].reshape(256, NZ).astype(F32)
            block = (up * grad).astype(BF16)
            slope[group, x] = block.reshape(16, YL, NZ)
            depth(x, hb, block)

        for i in range(2):

            @pl.when(hb == i)
            def _():
                depth_out(2, i)

    stores = [
        pltpu.make_async_copy(src, dst, store_sem.at[i])
        for i, (src, dst) in enumerate(
            ((act, act_hbm), (near, near_hbm), (wgrad, wgrad_hbm), (back_rows, back_hbm))
        )
    ]
    stores[0].start()
    pointwise(pw_back, slope)
    stores[1].start()
    through_modes(1)
    stores[2].start()
    depth_in(3)
    stores[3].start()

    for a in range(4):
        wait_narrow(ns, ns_sem, a)
        for hb in (0, 1) if a % 2 == 0 else (None,):
            wait_wide(ws, ws_sem, a, hb)

    for store in stores:
        store.wait()


def finish(
    kk, act_in, wgrad_in, back_hbm, near_hbm, table_hbm,
    act_hbm, wgrad_hbm, fgrad_hbm,
    back, near, table, zi, fgrad, act, wgrad, sem,
):
    load_table = pltpu.make_async_copy(table_hbm.at[pl.ds(0, kk)], table, sem.at[0])
    load_table.start()
    loads, passed, stores = [], [], []
    for b in range(4):
        rows = pl.ds(b * 128, 128)
        loads.append(
            (
                pltpu.make_async_copy(back_hbm.at[b], back.at[b], sem.at[1 + b]),
                pltpu.make_async_copy(near_hbm.at[:, rows], near.at[:, rows], sem.at[5 + b]),
            )
        )
        for load in loads[-1]:
            load.start()
    whole = [(act_in, act, act_hbm)] + [
        (wgrad_in.at[j], wgrad.at[j], wgrad_hbm.at[j]) for j in range(KL)
    ]
    for i, (src, held, dst) in enumerate(whole):
        passed.append(
            (
                pltpu.make_async_copy(src, held, sem.at[9 + i]),
                pltpu.make_async_copy(held, dst, sem.at[13 + i]),
            )
        )
        passed[-1][0].start()
    load_table.wait()
    for hb in range(2):
        for b in (2 * hb, 2 * hb + 1):
            for load in loads[b]:
                load.wait()
            zi[b] = back[b].astype(F32)
        for x in range(XL):
            block = jnp.concatenate(
                [zi[2 * hb + i, pl.ds(x, kk, stride=XL), :].astype(BF16) for i in range(2)], axis=1
            )
            rows = slice(hb * 256, (hb + 1) * 256)
            t = dot(block, table[...], ((0,), (0,))) + near[x, rows, :]
            fgrad[hb * 16 : (hb + 1) * 16, x] = t.astype(BF16).reshape(16, YL, NZ)
        group = pl.ds(hb * 16, 16)
        stores.append(pltpu.make_async_copy(fgrad.at[group], fgrad_hbm.at[group], sem.at[17 + hb]))
        stores[-1].start()
        for i in (2 * hb, 2 * hb + 1):
            passed[i][0].wait()
            passed[i][1].start()
            stores.append(passed[i][1])
    for store in stores:
        store.wait()


def on_device(wide, narrow, field, weight, pw, cot):
    ky = weight.shape[2]
    total = float(XL * wide * YL * narrow * NZ)
    places, packed = tables(wide, narrow, ky)
    table = jnp.asarray(packed)
    cells = C * YL
    kk = KL * wide * 2
    modes = KXL * 2 * ky
    hbm = pl.BlockSpec(memory_space=pl.ANY)
    grid_like = jax.ShapeDtypeStruct(field.shape, BF16)
    weight_like = jax.ShapeDtypeStruct(weight.shape, BF16)
    parts = pl.pallas_call(
        functools.partial(kernel, wide, narrow, ky, total, places),
        out_shape=(
            grid_like,
            weight_like,
            jax.ShapeDtypeStruct((4, kk * XL, 128), BF16),
            jax.ShapeDtypeStruct((XL, cells, NZ), F32),
        ),
        in_specs=[hbm] * 5,
        out_specs=(hbm,) * 4,
        scratch_shapes=[
            pltpu.VMEM(table.shape, BF16),
            pltpu.VMEM(field.shape, BF16),
            pltpu.VMEM(cot.shape, BF16),
            pltpu.VMEM(weight.shape, BF16),
            pltpu.VMEM(pw.shape, BF16),
            pltpu.VMEM(field.shape, BF16),
            pltpu.VMEM(weight.shape, BF16),
            pltpu.VMEM((4, kk * XL, 128), F32),
            pltpu.VMEM((XL, cells, NZ), F32),
            pltpu.VMEM((4, kk * XL, 128), BF16),
            pltpu.VMEM((4, kk * XL, 128), F32),
            pltpu.VMEM(field.shape, BF16),
            pltpu.VMEM((2, KL, modes, 128), BF16),
            pltpu.VMEM((modes, 128), F32),
            pltpu.VMEM((modes, 1024), BF16),
            pltpu.VMEM((2, 2 * ky, 128), BF16),
            pltpu.VMEM((narrow * 2 * YL, 128), F32),
            pltpu.VMEM((narrow * YL, 128), F32),
            pltpu.VMEM((KXL * narrow * 2, cells), BF16),
            pltpu.VMEM((cells, cells), BF16),
            pltpu.VMEM((cells, cells), BF16),
            pltpu.VMEM((cells, cells), BF16),
            pltpu.VMEM((cells, cells), BF16),
            pltpu.VMEM((128, 1024), BF16),
            pltpu.VMEM((128, 128), BF16),
            pltpu.VMEM((1024, 128), BF16),
            pltpu.VMEM((4, wide, 2, KL, 2 * XL, 256), BF16),
            pltpu.VMEM((4, wide, 2, KL, 2 * XL, 256), BF16),
            pltpu.VMEM((4, narrow, KL, 3 * YL, 128), BF16),
            pltpu.VMEM((4, narrow, KL, 3 * YL, 128), BF16),
            pltpu.SemaphoreType.DMA((4, 2)),
            pltpu.SemaphoreType.DMA((4, 2)),
            pltpu.SemaphoreType.DMA((4,)),
            pltpu.SemaphoreType.DMA((4,)),
            pltpu.SemaphoreType.DMA((7,)),
            pltpu.SemaphoreType.DMA((4,)),
        ],
        compiler_params=pltpu.CompilerParams(
            collective_id=0, has_side_effects=True, vmem_limit_bytes=VMEM_BYTES
        ),
        name="spectral_layer",
    )(field, cot, weight, pw, table)
    act, wgrad, fgrad = pl.pallas_call(
        functools.partial(finish, kk),
        out_shape=(grid_like, weight_like, grid_like),
        in_specs=[hbm] * 5,
        out_specs=(hbm,) * 3,
        scratch_shapes=[
            pltpu.VMEM((4, kk * XL, 128), BF16),
            pltpu.VMEM((XL, cells, NZ), F32),
            pltpu.VMEM((kk, NZ), BF16),
            pltpu.VMEM((4, kk * XL, 128), F32),
            pltpu.VMEM(field.shape, BF16),
            pltpu.VMEM(field.shape, BF16),
            pltpu.VMEM(weight.shape, BF16),
            pltpu.SemaphoreType.DMA((21,)),
        ],
        compiler_params=pltpu.CompilerParams(vmem_limit_bytes=VMEM_BYTES),
        name="field_gradient",
    )(*parts, table)
    return act, fgrad, wgrad


def solution(mesh):
    wide, narrow = mesh.shape["wide"], mesh.shape["narrow"]
    return jax.shard_map(
        functools.partial(on_device, wide, narrow),
        mesh=mesh,
        in_specs=(
            P(None, "wide", "narrow", None),
            P("wide", "narrow", None, None),
            P(),
            P(None, "wide", "narrow", None),
        ),
        out_specs=(
            P(None, "wide", "narrow", None),
            P(None, "wide", "narrow", None),
            P("wide", "narrow", None, None),
        ),
        check_vma=False,
    )
```

```python
import functools

import jax
import jax.numpy as jnp
import ml_dtypes
import numpy as np
from jax import lax
from jax.experimental import pallas as pl
from jax.experimental.pallas import tpu as pltpu
from jax.sharding import PartitionSpec as P

C = 32
XL = 8
YL = 16
KXL = 6
KL = 3
NZ = 128
VMEM_BYTES = 64 * 1024 * 1024
MESH = pl.DeviceIdType.MESH
F32 = jnp.float32
BF16 = jnp.bfloat16


def angles(extent, kept, two_sided):
    positions = np.arange(kept)
    frequency = (
        np.where(positions < kept // 2, positions, positions + extent - kept)
        if two_sided
        else positions
    )
    phases = np.arange(extent)[:, None] * frequency[None, :] % extent
    theta = 2.0 * np.pi * phases / extent
    rounded = lambda t: t.astype(np.float32).astype(ml_dtypes.bfloat16).astype(np.float32)
    return rounded(np.cos(theta)), rounded(np.sin(theta))


def tables(wide, narrow, ky):
    nx, ny, kx, kz = XL * wide, YL * narrow, KXL * narrow, KL * wide
    cx, sx = angles(nx, kx, True)
    cy, sy = angles(ny, ky, True)
    cz, sz = angles(NZ, kz, False)
    z_rows = np.stack([cz, -sz], axis=-1).reshape(NZ, wide, KL, 2)
    z_fwd = z_rows.transpose(2, 1, 3, 0).reshape(KL * wide * 2, NZ)
    fwd = lambda c, s: np.stack([np.stack([c, s]), np.stack([-s, c])])
    inv = lambda c, s: np.stack([np.stack([c, -s]), np.stack([s, c])])
    fx = fwd(cx, sx).reshape(2, 2, wide, XL, narrow, KXL)
    x_fwd = fx.transpose(5, 0, 4, 2, 1, 3).reshape(KXL * 2 * narrow, wide * 2 * XL)
    ix = inv(cx, sx).reshape(2, 2, wide, XL, narrow, KXL)
    x_inv = ix.transpose(2, 0, 3, 5, 1, 4).reshape(wide * 2 * XL, KXL * 2 * narrow)
    fy = fwd(cy, sy).reshape(2, 2, narrow, YL, ky)
    y_fwd = fy.transpose(0, 4, 2, 1, 3).reshape(2 * ky, narrow * 2 * YL)
    y_fwd_split = fy.transpose(1, 0, 4, 2, 3).reshape(4 * ky, narrow * YL)
    iy = inv(cy, sy).reshape(2, 2, narrow, YL, ky)
    y_inv = iy.transpose(2, 0, 3, 1, 4).reshape(narrow * 2 * YL, 2 * ky)
    y_inv_split = iy.transpose(0, 2, 3, 1, 4).reshape(2 * narrow * YL, 2 * ky)
    found = (z_fwd, x_fwd, x_inv, y_fwd, y_fwd_split, y_inv, y_inv_split)
    places, blocks, row = [], [], 0
    for t in found:
        rows, columns = t.shape
        places.append((row, rows, columns))
        for first in range(0, columns, 128):
            block = t[:, first : first + 128]
            blocks.append(np.pad(block, ((0, 0), (0, 128 - block.shape[1]))))
            row += rows
    return places, np.concatenate(blocks).astype(ml_dtypes.bfloat16)


def read_table(table, place):
    row, rows, columns = place
    blocks = [
        table[row + i * rows : row + (i + 1) * rows, : min(128, columns - first)]
        for i, first in enumerate(range(0, columns, 128))
    ]
    return jnp.concatenate(blocks, axis=1) if len(blocks) > 1 else blocks[0]


def dot(a, b, dims=((1,), (0,))):
    return lax.dot_general(a, b, (dims, ((), ())), preferred_element_type=F32)


def ones_where(condition):
    return jnp.where(condition, 1.0, 0.0).astype(BF16)


def kernel(
    wide, narrow, ky, total, places,
    field_hbm, cot_hbm, weight_hbm, pw_hbm, table_hbm,
    act_hbm, wgrad_hbm, back_hbm, near_hbm,
    *scratch,
):
    (
        table, field, cot, weight, pw, act, wgrad, zi, near, zs, slope, spec, sums, prods, mix, t1, t1_last, t2,
        perm, perm_t, pw_fwd, pw_back, repeat, tile, group_sum,
        fs, fr, ls, lr, ns, nr,
        fs_sem, fr_sem, ls_sem, lr_sem, ns_sem, nr_sem, load_sem, store_sem,
    ) = scratch
    w = lax.axis_index("wide")
    n = lax.axis_index("narrow")
    cells = C * YL
    kk = KL * wide * 2
    rows_j = wide * 2 * XL
    modes = KXL * 2 * ky

    z_fwd, x_fwd, x_inv, y_fwd, y_fwd_split, y_inv, y_inv_split = [
        functools.partial(read_table, table, place) for place in places
    ]
    z_part = pl.ds(0, kk)
    other = pl.ds(kk, table.shape[0] - kk)
    loads = [
        pltpu.make_async_copy(src, dst, load_sem.at[i])
        for i, (src, dst) in enumerate(
            (
                (field_hbm.at[pl.ds(0, C // 2)], field.at[pl.ds(0, C // 2)]),
                (table_hbm.at[z_part], table.at[z_part]),
                (field_hbm.at[pl.ds(C // 2, C // 2)], field.at[pl.ds(C // 2, C // 2)]),
                (pw_hbm, pw),
                (table_hbm.at[other], table.at[other]),
                (cot_hbm, cot),
                (weight_hbm, weight),
            )
        )
    ]
    for load in loads:
        load.start()

    barrier = pltpu.get_barrier_semaphore()

    half = narrow // 2
    flip = lax.rem(n + half, narrow)

    @pl.loop(0, wide)
    def _(d):
        pl.semaphore_signal(
            barrier, inc=1, device_id={"wide": d, "narrow": flip}, device_id_type=MESH
        )

    @pl.loop(1, narrow)
    def _(d):
        pl.semaphore_signal(
            barrier, inc=1, device_id={"narrow": lax.rem(n + d, narrow)}, device_id_type=MESH
        )

    row = lax.broadcasted_iota(jnp.int32, (cells, cells), 0)
    col = lax.broadcasted_iota(jnp.int32, (cells, cells), 1)
    lane = lax.broadcasted_iota(jnp.int32, (1, 128), 1) >> 5

    def shift(value, groups):
        amount = (groups * 32) % 128
        return value if amount == 0 else pltpu.roll(value, amount, 1)

    def pick(pieces):
        acc = pieces[0]
        for s, piece in enumerate(pieces[1:], 1):
            acc = jnp.where(lane == s, piece, acc)
        return acc

    def exchange(low, high, groups, first):
        return (
            jnp.where(first, low, shift(high, groups)),
            jnp.where(first, shift(low, -groups), high),
        )

    def transpose_groups(p):
        p0, p2 = exchange(p[0], p[2], 2, lane < 2)
        p1, p3 = exchange(p[1], p[3], 2, lane < 2)
        p0, p1 = exchange(p0, p1, 1, (lane & 1) == 0)
        p2, p3 = exchange(p2, p3, 1, (lane & 1) == 0)
        return [p0, p1, p2, p3]

    def depth(x, hb, block):
        out = dot(z_fwd(), block, ((1,), (1,)))
        for i in range(2):
            zs[2 * hb + i, pl.ds(x, kk, stride=XL), :] = out[:, i * 128 : (i + 1) * 128]

    def send_wide(src, dst, send_sem, recv_sem):
        @pl.loop(0, wide)
        def _(d):
            to = lax.rem(w + d, wide)
            pltpu.make_async_remote_copy(
                src_ref=src(to),
                dst_ref=dst(w),
                send_sem=send_sem,
                recv_sem=recv_sem,
                device_id={"wide": to, "narrow": flip},
                device_id_type=MESH,
            ).start()

    def wait(ref, sem):
        pltpu.make_async_copy(ref, ref, sem).wait()

    def send_first(a, hb):
        send_wide(
            lambda to: fs.at[a, to, hb], lambda me: fr.at[a, me, hb],
            fs_sem.at[a, hb], fr_sem.at[a, hb],
        )

    def wait_first(buffer, sem, a, hb):
        wait(buffer.at[a, pl.ds(0, wide), hb], sem.at[a, hb])

    chunks = (pl.ds(0, KL - 1), pl.ds(KL - 1, 1))

    def send_last(a, c):
        send_wide(
            lambda to: ls.at[a, to, chunks[c]], lambda me: lr.at[a, me, chunks[c]],
            ls_sem.at[a, c], lr_sem.at[a, c],
        )

    def wait_last(buffer, sem, a, c):
        wait(buffer.at[a, pl.ds(0, wide), chunks[c]], sem.at[a, c])

    def send_narrow(a, i, j, take, slot):
        nr[a, i, j, slot] = ns[a, i, j, take(n)]

        @pl.loop(1, narrow)
        def _(d):
            to = lax.rem(n + d, narrow)
            pltpu.make_async_remote_copy(
                src_ref=ns.at[a, i, j, take(to)],
                dst_ref=nr.at[a, i, j, slot],
                send_sem=ns_sem.at[a, i, j],
                recv_sem=nr_sem.at[a, i, j],
                device_id={"narrow": to},
                device_id_type=MESH,
            ).start()

    def wait_narrow(buffer, sem, a, i, j):
        wait(buffer.at[a, i, j, pl.ds(0, narrow - 1)], sem.at[a, i, j])

    def part(j):
        return pl.ds(pl.multiple_of(j * rows_j, rows_j), rows_j)

    def depth_out(a, hb):
        @pl.loop(0, KL)
        def _(j):
            for i in range(2):
                block = zs[2 * hb + i, part(j), :].astype(BF16).reshape(wide, 2 * XL, 128)
                fs[a, :, hb, j, :, i * 128 : (i + 1) * 128] = block

        send_first(a, hb)

    def x_forward(a, j):
        block = [fr[a, :, hb, j].reshape(rows_j, 256) for hb in range(2)]
        out = dot(x_fwd(), jnp.concatenate(block, axis=1))
        out = dot(out.astype(BF16), perm[...])
        for yb in range(4):

            def piece(kx, ri):
                first = (kx * 2 + ri) * narrow
                return out[first : first + narrow, yb * 128 : (yb + 1) * 128]

            for ri in range(2):
                for g, value in enumerate(transpose_groups([piece(s, ri) for s in range(4)])):
                    t1[pl.ds(ri * YL + 4 * yb + g, narrow, stride=2 * YL), :] = value
            last = transpose_groups([piece(4 + s % 2, s // 2) for s in range(4)])
            for g, value in enumerate(last):
                t1_last[pl.ds(4 * yb + g, narrow, stride=YL), :] = value
        ns[a, 0, j, :, : 2 * YL, :] = t1[...].astype(BF16).reshape(narrow, 2 * YL, 128)
        ns[a, 0, j, :, 2 * YL :, :] = t1_last[...].astype(BF16).reshape(narrow, YL, 128)
        send_narrow(a, 0, j, lambda to: to, flip)

    def y_forward(a, j):
        wait_narrow(nr, nr_sem, a, 0, j)
        first = dot(y_fwd(), nr[a, 0, j, :, : 2 * YL, :].reshape(narrow * 2 * YL, 128))
        both = dot(y_fwd_split(), nr[a, 0, j, :, 2 * YL :, :].reshape(narrow * YL, 128))
        last = both[: 2 * ky] + shift(both[2 * ky :], 2)
        for kx in range(KXL):
            source = first if kx < 4 else last
            spec[a, j, kx * 2 * ky : (kx + 1) * 2 * ky, :] = shift(source, -(kx % 4)).astype(BF16)

    def scale(j):
        return jnp.where(w * KL + j == 0, 1.0, 2.0).astype(F32) / total

    def weights(j, kx, b):
        return (
            weight[j, kx, :, b * 256 : (b + 1) * 256].astype(F32),
            weight[j, kx, :, 1024 + b * 256 : 1024 + (b + 1) * 256].astype(F32),
        )

    def mode_rows(kx):
        return slice(kx * 2 * ky, kx * 2 * ky + ky), slice(kx * 2 * ky + ky, (kx + 1) * 2 * ky)

    def place(summed):
        for lb in range(2):
            found = [
                summed[kx * 2 * ky : (kx + 1) * 2 * ky] for kx in range(4 * lb, min(4 * lb + 4, KXL))
            ]
            mix[lb] = pick(found).astype(BF16)

    def mix_forward(j):
        for b in range(4):
            rep = dot(spec[0, j], repeat[:, b * 256 : (b + 1) * 256])
            for kx in range(KXL):
                re, im = mode_rows(kx)
                w_r, w_i = weights(j, kx, b)
                p_r = rep[re] * w_r - rep[im] * w_i
                p_i = rep[re] * w_i + rep[im] * w_r
                p_r = p_r[:, :128] + p_r[:, 128:]
                p_i = p_i[:, :128] + p_i[:, 128:]
                sums[re, :] = p_r if b == 0 else sums[re, :] + p_r
                sums[im, :] = p_i if b == 0 else sums[im, :] + p_i
        acc = sums[...] * scale(j)
        acc = acc + shift(acc, 2)
        acc = acc + shift(acc, 1)
        place(acc)

    def mix_back(j):
        sums[...] = dot(spec[1, j], tile[...])
        for kx in range(KXL):
            re, im = mode_rows(kx)
            g_r = jnp.concatenate([sums[re, :]] * 2, axis=1)
            g_i = jnp.concatenate([sums[im, :]] * 2, axis=1)
            for b in range(4):
                w_r, w_i = weights(j, kx, b)
                lanes = slice(b * 256, (b + 1) * 256)
                prods[re, lanes] = (w_r * g_r + w_i * g_i).astype(BF16)
                prods[im, lanes] = (w_r * g_i - w_i * g_r).astype(BF16)
        place(dot(prods[...], group_sum[...]) * scale(j))

    def weight_gradient(j):
        sums[...] = dot(spec[1, j], tile[...]) * scale(j)
        for b in range(4):
            rep = dot(spec[0, j], repeat[:, b * 256 : (b + 1) * 256])
            for kx in range(KXL):
                re, im = mode_rows(kx)
                g_r = jnp.concatenate([sums[re, :]] * 2, axis=1)
                g_i = jnp.concatenate([sums[im, :]] * 2, axis=1)
                wgrad[j, kx, :, b * 256 : (b + 1) * 256] = (rep[re] * g_r + rep[im] * g_i).astype(BF16)
                wgrad[j, kx, :, 1024 + b * 256 : 1024 + (b + 1) * 256] = (
                    rep[re] * g_i - rep[im] * g_r
                ).astype(BF16)

    def y_inverse(a, j):
        first = dot(y_inv(), mix[0]).astype(BF16)
        ns[a, 1, j, :, : 2 * YL, :] = first.reshape(narrow, 2 * YL, 128)
        both = dot(y_inv_split(), mix[1])
        split = narrow * YL
        last = jnp.where(lane < 2, both[:split], shift(both[split:], 2)).astype(BF16)
        ns[a, 1, j, :, 2 * YL :, :] = last.reshape(narrow, YL, 128)
        send_narrow(a, 1, j, lambda to: lax.rem(to + half, narrow), n)

    def x_inverse(a, j):
        wait_narrow(nr, nr_sem, a, 1, j)
        t1[...] = nr[a, 1, j, :, : 2 * YL, :].reshape(narrow * 2 * YL, 128).astype(F32)
        t1_last[...] = nr[a, 1, j, :, 2 * YL :, :].reshape(narrow * YL, 128).astype(F32)
        for yb in range(4):
            lanes = slice(yb * 128, (yb + 1) * 128)
            ys = [4 * yb + g for g in range(4)]
            loaded = [
                [t1[pl.ds(ri * YL + y, narrow, stride=2 * YL), :] for y in ys] for ri in range(2)
            ]
            last = [t1_last[pl.ds(y, narrow, stride=YL), :] for y in ys]
            real, imag, last = [transpose_groups(p) for p in loaded + [last]]
            pairs = list(zip(real, imag)) + [(last[0], last[2]), (last[1], last[3])]
            for kx, pair in enumerate(pairs):
                t2[kx * 2 * narrow : (kx + 1) * 2 * narrow, lanes] = jnp.concatenate(
                    pair, axis=0
                ).astype(BF16)
        modes_cy = dot(t2[...], perm_t[...]).astype(BF16)
        out = dot(x_inv(), modes_cy).astype(BF16)
        ls[a, :, j] = out.reshape(wide, 2 * XL, cells)

    def each(step):
        @pl.loop(0, KL)
        def _(j):
            step(j)

    def through_modes(a):
        def mode_step(j):
            y_forward(a, j)
            mix_back(j) if a else mix_forward(j)
            y_inverse(a, j)

        for hb in range(2):
            wait_first(fr, fr_sem, a, hb)
        each(lambda j: x_forward(a, j))
        each(mode_step)

        @pl.loop(0, KL)
        def _(j):
            if a:

                @pl.when(j == KL - 1)
                def _():
                    weight_gradient(0)

            x_inverse(a, j)

            for c, j_last in enumerate((KL - 2, KL - 1)):

                @pl.when(j == j_last)
                def _():
                    send_last(a, c)

        if a:
            pl.loop(1, KL)(weight_gradient)

    def depth_in():
        for c in range(2):
            wait_last(lr, lr_sem, 0, c)
        for b in range(4):

            @pl.loop(0, KL)
            def _(j):
                block = lr[0, :, j, :, b * 128 : (b + 1) * 128].reshape(rows_j, 128)
                zi[b, part(j), :] = block.astype(F32)

    def pointwise(matrix, source):
        @pl.loop(0, XL // 2)
        def _(x):
            both = [source[:, 2 * x + i].reshape(cells, NZ) for i in range(2)]
            out = dot(matrix[...], jnp.concatenate(both, axis=1))
            for i in range(2):
                near[2 * x + i] = out[:, i * NZ : (i + 1) * NZ]

    loads[1].wait()
    for hb in range(2):
        loads[2 * hb].wait()
        for x in range(XL):
            depth(x, hb, field[hb * 16 : (hb + 1) * 16, x].reshape(256, NZ))
        if hb == 0:
            pl.semaphore_wait(barrier, wide + narrow - 1)
        depth_out(0, hb)

    loads[3].wait()
    loads[4].wait()
    perm[...] = ones_where(((row & 15) == (col >> 5)) & ((row >> 4) == (col & 31)))
    perm_t[...] = ones_where(((row >> 5) == (col & 15)) & ((row & 31) == (col >> 4)))
    spread_row = lax.broadcasted_iota(jnp.int32, (cells, C), 0)
    spread_col = lax.broadcasted_iota(jnp.int32, (cells, C), 1)
    spread = ones_where((spread_row >> 4) == spread_col)
    same_y = (row & 15) == (col & 15)
    behind = dot(dot(spread, pw[...]).astype(BF16), spread, ((1,), (1,)))
    pw_back[...] = jnp.where(same_y, behind, 0.0).astype(BF16)
    ahead = dot(dot(spread, pw[...], ((1,), (1,))).astype(BF16), spread, ((1,), (1,)))
    pw_fwd[...] = jnp.where(same_y, ahead, 0.0).astype(BF16)
    r_row = lax.broadcasted_iota(jnp.int32, (128, 1024), 0)
    r_col = lax.broadcasted_iota(jnp.int32, (128, 1024), 1)
    repeat[...] = ones_where(r_row == (r_col >> 5))
    t_row = lax.broadcasted_iota(jnp.int32, (128, 128), 0)
    t_col = lax.broadcasted_iota(jnp.int32, (128, 128), 1)
    tile[...] = ones_where(t_row == (t_col & 31))
    g_row = lax.broadcasted_iota(jnp.int32, (1024, 128), 0)
    g_col = lax.broadcasted_iota(jnp.int32, (1024, 128), 1)
    group_sum[...] = ones_where((g_row >> 5) == (g_col & 31))
    pointwise(pw_fwd, field)
    loads[5].wait()
    loads[6].wait()

    through_modes(0)
    depth_in()

    root = 0.7978845608028654

    @pl.loop(0, 2)
    def _(hb):
        rows = pl.ds(pl.multiple_of(hb * 256, 256), 256)
        group = pl.ds(hb * 16, 16)
        for x in range(XL):
            block = jnp.concatenate(
                [zi[2 * hb + i, pl.ds(x, kk, stride=XL), :].astype(BF16) for i in range(2)], axis=1
            )
            t = dot(block, z_fwd(), ((0,), (0,))) + near[x, rows, :]
            square = t * t
            gate = 0.5 + 0.5 * jnp.tanh(t * (root + (root * 0.044715) * square))
            out = t * gate
            act[group, x] = out.astype(BF16).reshape(16, YL, NZ)
            grad = gate + out * (1.0 - gate) * (2.0 * root + (6.0 * root * 0.044715) * square)
            up = cot[group, x].reshape(256, NZ).astype(F32)
            block = (up * grad).astype(BF16)
            slope[group, x] = block.reshape(16, YL, NZ)
            depth(x, hb, block)

        for i in range(2):

            @pl.when(hb == i)
            def _():
                depth_out(1, i)

    stores = [
        pltpu.make_async_copy(src, dst, store_sem.at[i])
        for i, (src, dst) in enumerate(
            (
                (act, act_hbm),
                (near, near_hbm),
                (wgrad, wgrad_hbm),
                (lr.at[1, :, chunks[0]], back_hbm.at[:, chunks[0]]),
                (lr.at[1, :, chunks[1]], back_hbm.at[:, chunks[1]]),
            )
        )
    ]
    stores[0].start()
    pointwise(pw_back, slope)
    stores[1].start()
    through_modes(1)
    stores[2].start()
    for c in range(2):
        wait_last(lr, lr_sem, 1, c)
        stores[3 + c].start()

    for a in range(2):
        for i in range(2):
            wait_first(fs, fs_sem, a, i)
            wait_last(ls, ls_sem, a, i)
            for j in range(KL):
                wait_narrow(ns, ns_sem, a, i, j)

    for store in stores:
        store.wait()


def finish(
    kk, act_in, wgrad_in, back_hbm, near_hbm, table_hbm,
    act_hbm, wgrad_hbm, fgrad_hbm,
    back, near, table, zi, fgrad, act, wgrad, sem,
):
    load_table = pltpu.make_async_copy(table_hbm.at[pl.ds(0, kk)], table, sem.at[0])
    load_table.start()
    loads, passed, stores = [], [], []
    for hb in range(2):
        part = pl.ds(hb * 256, 256)
        loads.append(
            (
                pltpu.make_async_copy(
                    back_hbm.at[:, :, :, part], back.at[:, :, :, part], sem.at[1 + hb]
                ),
                pltpu.make_async_copy(near_hbm.at[:, part], near.at[:, part], sem.at[5 + hb]),
            )
        )
        for load in loads[-1]:
            load.start()
    whole = [(act_in, act, act_hbm)] + [
        (wgrad_in.at[j], wgrad.at[j], wgrad_hbm.at[j]) for j in range(KL)
    ]
    for i, (src, held, dst) in enumerate(whole):
        passed.append(
            (
                pltpu.make_async_copy(src, held, sem.at[9 + i]),
                pltpu.make_async_copy(held, dst, sem.at[13 + i]),
            )
        )
        passed[-1][0].start()
    load_table.wait()
    for hb in range(2):
        for load in loads[hb]:
            load.wait()
        for b in (2 * hb, 2 * hb + 1):
            for j in range(KL):
                rows = back.shape[0] * 2 * XL
                block = back[:, j, :, b * 128 : (b + 1) * 128].reshape(rows, 128)
                zi[b, j * rows : (j + 1) * rows, :] = block.astype(F32)
        for x in range(XL):
            block = jnp.concatenate(
                [zi[2 * hb + i, pl.ds(x, kk, stride=XL), :].astype(BF16) for i in range(2)], axis=1
            )
            rows = slice(hb * 256, (hb + 1) * 256)
            t = dot(block, table[...], ((0,), (0,))) + near[x, rows, :]
            fgrad[hb * 16 : (hb + 1) * 16, x] = t.astype(BF16).reshape(16, YL, NZ)
        group = pl.ds(hb * 16, 16)
        stores.append(pltpu.make_async_copy(fgrad.at[group], fgrad_hbm.at[group], sem.at[17 + hb]))
        stores[-1].start()
        for i in (2 * hb, 2 * hb + 1):
            passed[i][0].wait()
            passed[i][1].start()
            stores.append(passed[i][1])
    for store in stores:
        store.wait()


def on_device(wide, narrow, field, weight, pw, cot):
    ky = weight.shape[2]
    total = float(XL * wide * YL * narrow * NZ)
    places, packed = tables(wide, narrow, ky)
    table = jnp.asarray(packed)
    cells = C * YL
    kk = KL * wide * 2
    modes = KXL * 2 * ky
    hbm = pl.BlockSpec(memory_space=pl.ANY)
    grid_like = jax.ShapeDtypeStruct(field.shape, BF16)
    weight_like = jax.ShapeDtypeStruct(weight.shape, BF16)
    parts = pl.pallas_call(
        functools.partial(kernel, wide, narrow, ky, total, places),
        out_shape=(
            grid_like,
            weight_like,
            jax.ShapeDtypeStruct((wide, KL, 2 * XL, cells), BF16),
            jax.ShapeDtypeStruct((XL, cells, NZ), F32),
        ),
        in_specs=[hbm] * 5,
        out_specs=(hbm,) * 4,
        scratch_shapes=[
            pltpu.VMEM(table.shape, BF16),
            pltpu.VMEM(field.shape, BF16),
            pltpu.VMEM(cot.shape, BF16),
            pltpu.VMEM(weight.shape, BF16),
            pltpu.VMEM(pw.shape, BF16),
            pltpu.VMEM(field.shape, BF16),
            pltpu.VMEM(weight.shape, BF16),
            pltpu.VMEM((4, kk * XL, 128), F32),
            pltpu.VMEM((XL, cells, NZ), F32),
            pltpu.VMEM((4, kk * XL, 128), F32),
            pltpu.VMEM(field.shape, BF16),
            pltpu.VMEM((2, KL, modes, 128), BF16),
            pltpu.VMEM((modes, 128), F32),
            pltpu.VMEM((modes, 1024), BF16),
            pltpu.VMEM((2, 2 * ky, 128), BF16),
            pltpu.VMEM((narrow * 2 * YL, 128), F32),
            pltpu.VMEM((narrow * YL, 128), F32),
            pltpu.VMEM((KXL * narrow * 2, cells), BF16),
            pltpu.VMEM((cells, cells), BF16),
            pltpu.VMEM((cells, cells), BF16),
            pltpu.VMEM((cells, cells), BF16),
            pltpu.VMEM((cells, cells), BF16),
            pltpu.VMEM((128, 1024), BF16),
            pltpu.VMEM((128, 128), BF16),
            pltpu.VMEM((1024, 128), BF16),
            pltpu.VMEM((2, wide, 2, KL, 2 * XL, 256), BF16),
            pltpu.VMEM((2, wide, 2, KL, 2 * XL, 256), BF16),
            pltpu.VMEM((2, wide, KL, 2 * XL, cells), BF16),
            pltpu.VMEM((2, wide, KL, 2 * XL, cells), BF16),
            pltpu.VMEM((2, 2, KL, narrow, 3 * YL, 128), BF16),
            pltpu.VMEM((2, 2, KL, narrow, 3 * YL, 128), BF16),
            pltpu.SemaphoreType.DMA((2, 2)),
            pltpu.SemaphoreType.DMA((2, 2)),
            pltpu.SemaphoreType.DMA((2, 2)),
            pltpu.SemaphoreType.DMA((2, 2)),
            pltpu.SemaphoreType.DMA((2, 2, KL)),
            pltpu.SemaphoreType.DMA((2, 2, KL)),
            pltpu.SemaphoreType.DMA((7,)),
            pltpu.SemaphoreType.DMA((5,)),
        ],
        compiler_params=pltpu.CompilerParams(
            collective_id=0, has_side_effects=True, vmem_limit_bytes=VMEM_BYTES
        ),
        name="spectral_layer",
    )(field, cot, weight, pw, table)
    act, wgrad, fgrad = pl.pallas_call(
        functools.partial(finish, kk),
        out_shape=(grid_like, weight_like, grid_like),
        in_specs=[hbm] * 5,
        out_specs=(hbm,) * 3,
        scratch_shapes=[
            pltpu.VMEM((wide, KL, 2 * XL, cells), BF16),
            pltpu.VMEM((XL, cells, NZ), F32),
            pltpu.VMEM((kk, NZ), BF16),
            pltpu.VMEM((4, kk * XL, 128), F32),
            pltpu.VMEM(field.shape, BF16),
            pltpu.VMEM(field.shape, BF16),
            pltpu.VMEM(weight.shape, BF16),
            pltpu.SemaphoreType.DMA((21,)),
        ],
        compiler_params=pltpu.CompilerParams(vmem_limit_bytes=VMEM_BYTES),
        name="field_gradient",
    )(*parts, table)
    return act, fgrad, wgrad


def solution(mesh):
    wide, narrow = mesh.shape["wide"], mesh.shape["narrow"]
    return jax.shard_map(
        functools.partial(on_device, wide, narrow),
        mesh=mesh,
        in_specs=(
            P(None, "wide", "narrow", None),
            P("wide", "narrow", None, None),
            P(),
            P(None, "wide", "narrow", None),
        ),
        out_specs=(
            P(None, "wide", "narrow", None),
            P(None, "wide", "narrow", None),
            P("wide", "narrow", None, None),
        ),
        check_vma=False,
    )
```

```python
import functools

import jax
import jax.numpy as jnp
import ml_dtypes
import numpy as np
from jax import lax
from jax.experimental import pallas as pl
from jax.experimental.pallas import tpu as pltpu
from jax.sharding import PartitionSpec as P

C = 32
XL = 8
YL = 16
KXL = 6
KL = 3
HALVES = 2
NZ = 128
VMEM_BYTES = 64 * 1024 * 1024
MESH = pl.DeviceIdType.MESH
F32 = jnp.float32
BF16 = jnp.bfloat16


def angles(extent, kept, two_sided):
    positions = np.arange(kept)
    frequency = (
        np.where(positions < kept // 2, positions, positions + extent - kept)
        if two_sided
        else positions
    )
    phases = np.arange(extent)[:, None] * frequency[None, :] % extent
    theta = 2.0 * np.pi * phases / extent
    rounded = lambda t: t.astype(np.float32).astype(ml_dtypes.bfloat16).astype(np.float32)
    return rounded(np.cos(theta)), rounded(np.sin(theta))


def tables(wide, narrow, ky):
    nx, ny, kx, kz = XL * wide, YL * narrow, KXL * narrow, KL * wide
    cx, sx = angles(nx, kx, True)
    cy, sy = angles(ny, ky, True)
    cz, sz = angles(NZ, kz, False)
    v = wide // HALVES
    z_rows = np.stack([cz, -sz], axis=-1).reshape(NZ, HALVES, v, KL, 2)
    z_fwd = z_rows.transpose(3, 2, 1, 4, 0).reshape(KL * wide * 2, NZ)
    fwd = lambda c, s: np.stack([np.stack([c, s]), np.stack([-s, c])])
    inv = lambda c, s: np.stack([np.stack([c, -s]), np.stack([s, c])])
    fx = fwd(cx, sx).reshape(2, 2, HALVES, v, XL, narrow, KXL)
    x_fwd = fx.transpose(2, 6, 0, 5, 3, 1, 4).reshape(HALVES * KXL * 2 * narrow, v * 2 * XL)
    ix = inv(cx, sx).reshape(2, 2, wide, XL, narrow, KXL)
    x_inv = ix.transpose(2, 0, 3, 5, 1, 4).reshape(wide * 2 * XL, KXL * 2 * narrow)
    fy = fwd(cy, sy).reshape(2, 2, narrow, YL, ky)
    y_fwd = fy.transpose(0, 4, 2, 1, 3).reshape(2 * ky, narrow * 2 * YL)
    y_fwd_split = fy.transpose(1, 0, 4, 2, 3).reshape(4 * ky, narrow * YL)
    iy = inv(cy, sy).reshape(2, 2, narrow, YL, ky)
    y_inv = iy.transpose(2, 0, 3, 1, 4).reshape(narrow * 2 * YL, 2 * ky)
    y_inv_split = iy.transpose(0, 2, 3, 1, 4).reshape(2 * narrow * YL, 2 * ky)
    found = (z_fwd, x_fwd, x_inv, y_fwd, y_fwd_split, y_inv, y_inv_split)
    places, blocks, row = [], [], 0
    for t in found:
        rows, columns = t.shape
        places.append((row, rows, columns))
        for first in range(0, columns, 128):
            block = t[:, first : first + 128]
            blocks.append(np.pad(block, ((0, 0), (0, 128 - block.shape[1]))))
            row += rows
    return places, np.concatenate(blocks).astype(ml_dtypes.bfloat16)


def read_table(table, place):
    row, rows, columns = place
    blocks = [
        table[row + i * rows : row + (i + 1) * rows, : min(128, columns - first)]
        for i, first in enumerate(range(0, columns, 128))
    ]
    return jnp.concatenate(blocks, axis=1) if len(blocks) > 1 else blocks[0]


def dot(a, b, dims=((1,), (0,))):
    return lax.dot_general(a, b, (dims, ((), ())), preferred_element_type=F32)


def ones_where(condition):
    return jnp.where(condition, 1.0, 0.0).astype(BF16)


def kernel(
    wide, narrow, ky, total, places,
    field_hbm, cot_hbm, weight_hbm, pw_hbm, table_hbm,
    act_hbm, wgrad_hbm, back_hbm, near_hbm,
    *scratch,
):
    (
        table, field, cot, weight, pw, act, wgrad, zi, near, zs, slope, spec, sums, prods, mix, t1, t1_last, t2,
        perm, perm_t, pw_fwd, pw_back, repeat, tile, group_sum,
        fs, fr, ls, lr, ns, nr,
        fs_sem, fr_sem, ls_sem, lr_sem, ns_sem, nr_sem, load_sem, store_sem,
    ) = scratch
    w = lax.axis_index("wide")
    n = lax.axis_index("narrow")
    cells = C * YL
    kk = KL * wide * 2
    rows_j = wide * 2 * XL
    modes = KXL * 2 * ky

    z_fwd, x_fwd, x_inv, y_fwd, y_fwd_split, y_inv, y_inv_split = [
        functools.partial(read_table, table, place) for place in places
    ]
    z_part = pl.ds(0, kk)
    other = pl.ds(kk, table.shape[0] - kk)
    loads = [
        pltpu.make_async_copy(src, dst, load_sem.at[i])
        for i, (src, dst) in enumerate(
            (
                (field_hbm.at[pl.ds(0, C // 2)], field.at[pl.ds(0, C // 2)]),
                (table_hbm.at[z_part], table.at[z_part]),
                (field_hbm.at[pl.ds(C // 2, C // 2)], field.at[pl.ds(C // 2, C // 2)]),
                (pw_hbm, pw),
                (table_hbm.at[other], table.at[other]),
                (cot_hbm, cot),
                (weight_hbm, weight),
            )
        )
    ]
    for load in loads[:5]:
        load.start()

    side = wide // HALVES
    h, v = w // side, lax.rem(w, side)
    plane = HALVES * narrow
    here = h * narrow + n

    barrier = pltpu.get_barrier_semaphore()

    def along(d):
        to = lax.rem(v + d, side)
        return to, {"wide": h * side + to}

    def across(d):
        to = lax.rem(here + d, plane)
        return to, {"wide": to // narrow * side + v, "narrow": lax.rem(to, narrow)}

    for count, peer in ((side, along), (plane, across)):
        for d in range(1, count):
            pl.semaphore_signal(barrier, inc=1, device_id=peer(d)[1], device_id_type=MESH)

    row = lax.broadcasted_iota(jnp.int32, (cells, cells), 0)
    col = lax.broadcasted_iota(jnp.int32, (cells, cells), 1)
    lane = lax.broadcasted_iota(jnp.int32, (1, 128), 1) >> 5

    def shift(value, groups):
        amount = (groups * 32) % 128
        return value if amount == 0 else pltpu.roll(value, amount, 1)

    def pick(pieces):
        acc = pieces[0]
        for s, piece in enumerate(pieces[1:], 1):
            acc = jnp.where(lane == s, piece, acc)
        return acc

    def exchange(low, high, groups, first):
        return (
            jnp.where(first, low, shift(high, groups)),
            jnp.where(first, shift(low, -groups), high),
        )

    def transpose_groups(p):
        p0, p2 = exchange(p[0], p[2], 2, lane < 2)
        p1, p3 = exchange(p[1], p[3], 2, lane < 2)
        p0, p1 = exchange(p0, p1, 1, (lane & 1) == 0)
        p2, p3 = exchange(p2, p3, 1, (lane & 1) == 0)
        return [p0, p1, p2, p3]

    def depth(x, hb, block):
        out = dot(z_fwd(), block, ((1,), (1,)))
        for i in range(2):
            zs[2 * hb + i, pl.ds(x, kk, stride=XL), :] = out[:, i * 128 : (i + 1) * 128]

    def send(peer, count, src, dst, send_sem, recv_sem):
        for d in range(1, count):
            to, device = peer(d)
            pltpu.make_async_remote_copy(
                src_ref=src(to),
                dst_ref=dst,
                send_sem=send_sem,
                recv_sem=recv_sem,
                device_id=device,
                device_id_type=MESH,
            ).start()

    def wait(ref, sem):
        pltpu.make_async_copy(ref, ref, sem).wait()

    def send_first(a, hb):
        fr[a, v, hb] = fs[a, v, hb]
        send(
            along, side, lambda to: fs.at[a, to, hb], fr.at[a, v, hb],
            fs_sem.at[a, hb], fr_sem.at[a, hb],
        )

    def wait_first(buffer, sem, a, hb):
        wait(buffer.at[a, pl.ds(0, side - 1), hb], sem.at[a, hb])

    chunks = (pl.ds(0, KL - 1), pl.ds(KL - 1, 1))

    def send_last(a, c):
        lr[a, v, chunks[c]] = ls[a, v, chunks[c]]
        send(
            along, side, lambda to: ls.at[a, to, chunks[c]], lr.at[a, v, chunks[c]],
            ls_sem.at[a, c], lr_sem.at[a, c],
        )

    def wait_last(buffer, sem, a, c):
        wait(buffer.at[a, pl.ds(0, side - 1), chunks[c]], sem.at[a, c])

    def send_narrow(a, i, j, take):
        nr[a, i, j, here] = ns[a, i, j, take(here)]
        send(
            across, plane, lambda to: ns.at[a, i, j, take(to)], nr.at[a, i, j, here],
            ns_sem.at[a, i, j], nr_sem.at[a, i, j],
        )

    def wait_narrow(buffer, sem, a, i, j):
        wait(buffer.at[a, i, j, pl.ds(0, plane - 1)], sem.at[a, i, j])

    def part(j):
        return pl.ds(pl.multiple_of(j * rows_j, rows_j), rows_j)

    def depth_out(a, hb):
        @pl.loop(0, KL)
        def _(j):
            for i in range(2):
                block = zs[2 * hb + i, part(j), :].astype(BF16).reshape(side, HALVES * 2 * XL, 128)
                fs[a, :, hb, j, :, i * 128 : (i + 1) * 128] = block

        send_first(a, hb)

    def half_lines(i):
        return slice(i * 2 * XL, (i + 1) * 2 * XL)

    def own_half(place):
        first, rows, columns = place
        rows = rows // HALVES
        return table[pl.ds(first + h * rows, rows), :columns]

    def x_forward(a, j):
        matrix = own_half(places[1])
        outs = []
        for to_h in range(HALVES):
            block = [
                fr[a, :, hb, j, half_lines(to_h), :].reshape(side * 2 * XL, 256) for hb in range(2)
            ]
            outs.append(dot(matrix, jnp.concatenate(block, axis=1)).astype(BF16))
        both = dot(jnp.concatenate(outs, axis=0), perm[...])
        rows = KXL * 2 * narrow
        for to_h in range(HALVES):
            out = both[to_h * rows : (to_h + 1) * rows]
            for yb in range(4):

                def piece(kx, ri):
                    first = (kx * 2 + ri) * narrow
                    return out[first : first + narrow, yb * 128 : (yb + 1) * 128]

                for ri in range(2):
                    for g, value in enumerate(transpose_groups([piece(s, ri) for s in range(4)])):
                        t1[pl.ds(ri * YL + 4 * yb + g, narrow, stride=2 * YL), :] = value
                last = transpose_groups([piece(4 + s % 2, s // 2) for s in range(4)])
                for g, value in enumerate(last):
                    t1_last[pl.ds(4 * yb + g, narrow, stride=YL), :] = value
            owners = slice(to_h * narrow, (to_h + 1) * narrow)
            ns[a, 0, j, owners, : 2 * YL, :] = t1[...].astype(BF16).reshape(narrow, 2 * YL, 128)
            ns[a, 0, j, owners, 2 * YL :, :] = t1_last[...].astype(BF16).reshape(narrow, YL, 128)
        send_narrow(a, 0, j, lambda to: to)

    def y_forward(a, j):
        wait_narrow(nr, nr_sem, a, 0, j)
        halves = [slice(i * narrow, (i + 1) * narrow) for i in range(HALVES)]
        first, both = (
            sum(dot(matrix, nr[a, 0, j, i, lines, :].reshape(-1, 128)) for i in halves)
            for matrix, lines in ((y_fwd(), slice(0, 2 * YL)), (y_fwd_split(), slice(2 * YL, None)))
        )
        last = both[: 2 * ky] + shift(both[2 * ky :], 2)
        for kx in range(KXL):
            source = first if kx < 4 else last
            spec[a, j, kx * 2 * ky : (kx + 1) * 2 * ky, :] = shift(source, -(kx % 4)).astype(BF16)

    def scale(j):
        return jnp.where(w * KL + j == 0, 1.0, 2.0).astype(F32) / total

    def weights(j, kx, b):
        return (
            weight[j, kx, :, b * 256 : (b + 1) * 256].astype(F32),
            weight[j, kx, :, 1024 + b * 256 : 1024 + (b + 1) * 256].astype(F32),
        )

    def mode_rows(kx):
        return slice(kx * 2 * ky, kx * 2 * ky + ky), slice(kx * 2 * ky + ky, (kx + 1) * 2 * ky)

    def place(summed):
        for lb in range(2):
            found = [
                summed[kx * 2 * ky : (kx + 1) * 2 * ky] for kx in range(4 * lb, min(4 * lb + 4, KXL))
            ]
            mix[lb] = pick(found).astype(BF16)

    def mix_forward(j):
        for b in range(4):
            rep = dot(spec[0, j], repeat[:, b * 256 : (b + 1) * 256])
            for kx in range(KXL):
                re, im = mode_rows(kx)
                w_r, w_i = weights(j, kx, b)
                p_r = rep[re] * w_r - rep[im] * w_i
                p_i = rep[re] * w_i + rep[im] * w_r
                p_r = p_r[:, :128] + p_r[:, 128:]
                p_i = p_i[:, :128] + p_i[:, 128:]
                sums[re, :] = p_r if b == 0 else sums[re, :] + p_r
                sums[im, :] = p_i if b == 0 else sums[im, :] + p_i
        acc = sums[...] * scale(j)
        acc = acc + shift(acc, 2)
        acc = acc + shift(acc, 1)
        place(acc)

    def mix_back(j):
        sums[...] = dot(spec[1, j], tile[...])
        for kx in range(KXL):
            re, im = mode_rows(kx)
            g_r = jnp.concatenate([sums[re, :]] * 2, axis=1)
            g_i = jnp.concatenate([sums[im, :]] * 2, axis=1)
            for b in range(4):
                w_r, w_i = weights(j, kx, b)
                lanes = slice(b * 256, (b + 1) * 256)
                prods[re, lanes] = (w_r * g_r + w_i * g_i).astype(BF16)
                prods[im, lanes] = (w_r * g_i - w_i * g_r).astype(BF16)
        place(dot(prods[...], group_sum[...]) * scale(j))

    def weight_gradient(j):
        sums[...] = dot(spec[1, j], tile[...]) * scale(j)
        for b in range(4):
            rep = dot(spec[0, j], repeat[:, b * 256 : (b + 1) * 256])
            for kx in range(KXL):
                re, im = mode_rows(kx)
                g_r = jnp.concatenate([sums[re, :]] * 2, axis=1)
                g_i = jnp.concatenate([sums[im, :]] * 2, axis=1)
                wgrad[j, kx, :, b * 256 : (b + 1) * 256] = (rep[re] * g_r + rep[im] * g_i).astype(BF16)
                wgrad[j, kx, :, 1024 + b * 256 : 1024 + (b + 1) * 256] = (
                    rep[re] * g_i - rep[im] * g_r
                ).astype(BF16)

    def y_inverse(a, j):
        first = dot(y_inv(), mix[0]).astype(BF16)
        ns[a, 1, j, :narrow, : 2 * YL, :] = first.reshape(narrow, 2 * YL, 128)
        both = dot(y_inv_split(), mix[1])
        split = narrow * YL
        last = jnp.where(lane < 2, both[:split], shift(both[split:], 2)).astype(BF16)
        ns[a, 1, j, :narrow, 2 * YL :, :] = last.reshape(narrow, YL, 128)
        send_narrow(a, 1, j, lambda to: lax.rem(to, narrow))

    def x_inverse(a, j):
        wait_narrow(nr, nr_sem, a, 1, j)
        rows = KXL * 2 * narrow
        for from_h in range(HALVES):
            owners = slice(from_h * narrow, (from_h + 1) * narrow)
            t1[...] = nr[a, 1, j, owners, : 2 * YL, :].reshape(narrow * 2 * YL, 128).astype(F32)
            t1_last[...] = nr[a, 1, j, owners, 2 * YL :, :].reshape(narrow * YL, 128).astype(F32)
            for yb in range(4):
                lanes = slice(yb * 128, (yb + 1) * 128)
                ys = [4 * yb + g for g in range(4)]
                loaded = [
                    [t1[pl.ds(ri * YL + y, narrow, stride=2 * YL), :] for y in ys] for ri in range(2)
                ]
                last = [t1_last[pl.ds(y, narrow, stride=YL), :] for y in ys]
                real, imag, last = [transpose_groups(p) for p in loaded + [last]]
                pairs = list(zip(real, imag)) + [(last[0], last[2]), (last[1], last[3])]
                for kx, pair in enumerate(pairs):
                    first = from_h * rows + kx * 2 * narrow
                    t2[first : first + 2 * narrow, lanes] = jnp.concatenate(pair, axis=0).astype(BF16)
        modes_cy = dot(t2[...], perm_t[...]).astype(BF16)
        matrix = own_half(places[2])
        for from_h in range(HALVES):
            out = dot(matrix, modes_cy[from_h * rows : (from_h + 1) * rows]).astype(BF16)
            ls[a, :, j, half_lines(from_h), :] = out.reshape(side, 2 * XL, cells)

    def store_gradient(j):
        return pltpu.make_async_copy(wgrad.at[j], wgrad_hbm.at[j], store_sem.at[4 + j])

    def make_gradient(j):
        weight_gradient(j)
        store_gradient(j).start()

    def each(step):
        @pl.loop(0, KL)
        def _(j):
            step(j)

    def through_modes(a):
        def mode_step(j):
            y_forward(a, j)
            mix_back(j) if a else mix_forward(j)
            y_inverse(a, j)

        for hb in range(2):
            wait_first(fr, fr_sem, a, hb)
        each(lambda j: x_forward(a, j))
        each(mode_step)

        @pl.loop(0, KL)
        def _(j):
            if a:

                @pl.when(j == KL - 1)
                def _():
                    make_gradient(0)

            x_inverse(a, j)

            for c, j_last in enumerate((KL - 2, KL - 1)):

                @pl.when(j == j_last)
                def _():
                    send_last(a, c)

        if a:
            pl.loop(1, KL)(make_gradient)

    def depth_in():
        for c in range(2):
            wait_last(lr, lr_sem, 0, c)
        for b in range(4):

            @pl.loop(0, KL)
            def _(j):
                block = lr[0, :, j, :, b * 128 : (b + 1) * 128].reshape(rows_j, 128)
                zi[b, part(j), :] = block.astype(F32)

    def pointwise(matrix, source):
        @pl.loop(0, XL // 2)
        def _(x):
            both = [source[:, 2 * x + i].reshape(cells, NZ) for i in range(2)]
            out = dot(matrix[...], jnp.concatenate(both, axis=1))
            for i in range(2):
                near[2 * x + i] = out[:, i * NZ : (i + 1) * NZ]

    loads[1].wait()
    for hb in range(2):
        loads[2 * hb].wait()
        for x in range(XL):
            depth(x, hb, field[hb * 16 : (hb + 1) * 16, x].reshape(256, NZ))
        if hb == 0:
            pl.semaphore_wait(barrier, side + plane - 2)
        depth_out(0, hb)

    for load in loads[5:]:
        load.start()
    loads[3].wait()
    loads[4].wait()
    perm[...] = ones_where(((row & 15) == (col >> 5)) & ((row >> 4) == (col & 31)))
    perm_t[...] = ones_where(((row >> 5) == (col & 15)) & ((row & 31) == (col >> 4)))
    spread_row = lax.broadcasted_iota(jnp.int32, (cells, C), 0)
    spread_col = lax.broadcasted_iota(jnp.int32, (cells, C), 1)
    spread = ones_where((spread_row >> 4) == spread_col)
    same_y = (row & 15) == (col & 15)
    behind = dot(dot(spread, pw[...]).astype(BF16), spread, ((1,), (1,)))
    pw_back[...] = jnp.where(same_y, behind, 0.0).astype(BF16)
    ahead = dot(dot(spread, pw[...], ((1,), (1,))).astype(BF16), spread, ((1,), (1,)))
    pw_fwd[...] = jnp.where(same_y, ahead, 0.0).astype(BF16)
    r_row = lax.broadcasted_iota(jnp.int32, (128, 1024), 0)
    r_col = lax.broadcasted_iota(jnp.int32, (128, 1024), 1)
    repeat[...] = ones_where(r_row == (r_col >> 5))
    t_row = lax.broadcasted_iota(jnp.int32, (128, 128), 0)
    t_col = lax.broadcasted_iota(jnp.int32, (128, 128), 1)
    tile[...] = ones_where(t_row == (t_col & 31))
    g_row = lax.broadcasted_iota(jnp.int32, (1024, 128), 0)
    g_col = lax.broadcasted_iota(jnp.int32, (1024, 128), 1)
    group_sum[...] = ones_where((g_row >> 5) == (g_col & 31))
    pointwise(pw_fwd, field)
    loads[5].wait()
    loads[6].wait()

    through_modes(0)
    depth_in()

    root = 0.7978845608028654

    @pl.loop(0, 2)
    def _(hb):
        rows = pl.ds(pl.multiple_of(hb * 256, 256), 256)
        group = pl.ds(hb * 16, 16)
        for x in range(XL):
            block = jnp.concatenate(
                [zi[2 * hb + i, pl.ds(x, kk, stride=XL), :].astype(BF16) for i in range(2)], axis=1
            )
            t = dot(block, z_fwd(), ((0,), (0,))) + near[x, rows, :]
            square = t * t
            gate = 0.5 + 0.5 * jnp.tanh(t * (root + (root * 0.044715) * square))
            out = t * gate
            act[group, x] = out.astype(BF16).reshape(16, YL, NZ)
            grad = gate + out * (1.0 - gate) * (2.0 * root + (6.0 * root * 0.044715) * square)
            up = cot[group, x].reshape(256, NZ).astype(F32)
            block = (up * grad).astype(BF16)
            slope[group, x] = block.reshape(16, YL, NZ)
            depth(x, hb, block)

        for i in range(2):

            @pl.when(hb == i)
            def _():
                depth_out(1, i)

    stores = [
        pltpu.make_async_copy(src, dst, store_sem.at[i])
        for i, (src, dst) in enumerate(
            (
                (act, act_hbm),
                (near, near_hbm),
                (lr.at[1, :, chunks[0]], back_hbm.at[:, chunks[0]]),
                (lr.at[1, :, chunks[1]], back_hbm.at[:, chunks[1]]),
            )
        )
    ]
    stores[0].start()
    pointwise(pw_back, slope)
    stores[1].start()
    through_modes(1)
    for c in range(2):
        wait_last(lr, lr_sem, 1, c)
        stores[2 + c].start()

    for a in range(2):
        for i in range(2):
            wait_first(fs, fs_sem, a, i)
            wait_last(ls, ls_sem, a, i)
            for j in range(KL):
                wait_narrow(ns, ns_sem, a, i, j)

    each(lambda j: store_gradient(j).wait())
    for store in stores:
        store.wait()


def finish(
    kk, act_in, wgrad_in, back_hbm, near_hbm, table_hbm,
    act_hbm, wgrad_hbm, fgrad_hbm,
    back, near, table, zi, fgrad, act, wgrad, sem,
):
    load_table = pltpu.make_async_copy(table_hbm.at[pl.ds(0, kk)], table, sem.at[0])
    load_table.start()
    loads, passed, stores = [], [], []
    for hb in range(2):
        part = pl.ds(hb * 256, 256)
        loads.append(
            (
                pltpu.make_async_copy(
                    back_hbm.at[:, :, :, part], back.at[:, :, :, part], sem.at[1 + hb]
                ),
                pltpu.make_async_copy(near_hbm.at[:, part], near.at[:, part], sem.at[5 + hb]),
            )
        )
        for load in loads[-1]:
            load.start()
    whole = [(act_in, act, act_hbm)] + [
        (wgrad_in.at[j], wgrad.at[j], wgrad_hbm.at[j]) for j in range(KL)
    ]
    for i, (src, held, dst) in enumerate(whole):
        passed.append(
            (
                pltpu.make_async_copy(src, held, sem.at[9 + i]),
                pltpu.make_async_copy(held, dst, sem.at[13 + i]),
            )
        )
        passed[-1][0].start()
    load_table.wait()
    for hb in range(2):
        for load in loads[hb]:
            load.wait()
        for b in (2 * hb, 2 * hb + 1):
            for j in range(KL):
                rows = back.shape[0] * back.shape[2]
                block = back[:, j, :, b * 128 : (b + 1) * 128].reshape(rows, 128)
                zi[b, j * rows : (j + 1) * rows, :] = block.astype(F32)
        for x in range(XL):
            block = jnp.concatenate(
                [zi[2 * hb + i, pl.ds(x, kk, stride=XL), :].astype(BF16) for i in range(2)], axis=1
            )
            rows = slice(hb * 256, (hb + 1) * 256)
            t = dot(block, table[...], ((0,), (0,))) + near[x, rows, :]
            fgrad[hb * 16 : (hb + 1) * 16, x] = t.astype(BF16).reshape(16, YL, NZ)
        group = pl.ds(hb * 16, 16)
        stores.append(pltpu.make_async_copy(fgrad.at[group], fgrad_hbm.at[group], sem.at[17 + hb]))
        stores[-1].start()
        for i in (2 * hb, 2 * hb + 1):
            passed[i][0].wait()
            passed[i][1].start()
            stores.append(passed[i][1])
    for store in stores:
        store.wait()


def on_device(wide, narrow, field, weight, pw, cot):
    ky = weight.shape[2]
    total = float(XL * wide * YL * narrow * NZ)
    places, packed = tables(wide, narrow, ky)
    table = jnp.asarray(packed)
    cells = C * YL
    kk = KL * wide * 2
    modes = KXL * 2 * ky
    side, plane = wide // HALVES, narrow * HALVES
    hbm = pl.BlockSpec(memory_space=pl.ANY)
    grid_like = jax.ShapeDtypeStruct(field.shape, BF16)
    weight_like = jax.ShapeDtypeStruct(weight.shape, BF16)
    parts = pl.pallas_call(
        functools.partial(kernel, wide, narrow, ky, total, places),
        out_shape=(
            grid_like,
            weight_like,
            jax.ShapeDtypeStruct((side, KL, HALVES * 2 * XL, cells), BF16),
            jax.ShapeDtypeStruct((XL, cells, NZ), F32),
        ),
        in_specs=[hbm] * 5,
        out_specs=(hbm,) * 4,
        scratch_shapes=[
            pltpu.VMEM(table.shape, BF16),
            pltpu.VMEM(field.shape, BF16),
            pltpu.VMEM(cot.shape, BF16),
            pltpu.VMEM(weight.shape, BF16),
            pltpu.VMEM(pw.shape, BF16),
            pltpu.VMEM(field.shape, BF16),
            pltpu.VMEM(weight.shape, BF16),
            pltpu.VMEM((4, kk * XL, 128), F32),
            pltpu.VMEM((XL, cells, NZ), F32),
            pltpu.VMEM((4, kk * XL, 128), F32),
            pltpu.VMEM(field.shape, BF16),
            pltpu.VMEM((2, KL, modes, 128), BF16),
            pltpu.VMEM((modes, 128), F32),
            pltpu.VMEM((modes, 1024), BF16),
            pltpu.VMEM((2, 2 * ky, 128), BF16),
            pltpu.VMEM((narrow * 2 * YL, 128), F32),
            pltpu.VMEM((narrow * YL, 128), F32),
            pltpu.VMEM((HALVES * KXL * narrow * 2, cells), BF16),
            pltpu.VMEM((cells, cells), BF16),
            pltpu.VMEM((cells, cells), BF16),
            pltpu.VMEM((cells, cells), BF16),
            pltpu.VMEM((cells, cells), BF16),
            pltpu.VMEM((128, 1024), BF16),
            pltpu.VMEM((128, 128), BF16),
            pltpu.VMEM((1024, 128), BF16),
            pltpu.VMEM((2, side, 2, KL, HALVES * 2 * XL, 256), BF16),
            pltpu.VMEM((2, side, 2, KL, HALVES * 2 * XL, 256), BF16),
            pltpu.VMEM((2, side, KL, HALVES * 2 * XL, cells), BF16),
            pltpu.VMEM((2, side, KL, HALVES * 2 * XL, cells), BF16),
            pltpu.VMEM((2, 2, KL, plane, 3 * YL, 128), BF16),
            pltpu.VMEM((2, 2, KL, plane, 3 * YL, 128), BF16),
            pltpu.SemaphoreType.DMA((2, 2)),
            pltpu.SemaphoreType.DMA((2, 2)),
            pltpu.SemaphoreType.DMA((2, 2)),
            pltpu.SemaphoreType.DMA((2, 2)),
            pltpu.SemaphoreType.DMA((2, 2, KL)),
            pltpu.SemaphoreType.DMA((2, 2, KL)),
            pltpu.SemaphoreType.DMA((7,)),
            pltpu.SemaphoreType.DMA((4 + KL,)),
        ],
        compiler_params=pltpu.CompilerParams(
            collective_id=0, has_side_effects=True, vmem_limit_bytes=VMEM_BYTES
        ),
        name="spectral_layer",
    )(field, cot, weight, pw, table)
    act, wgrad, fgrad = pl.pallas_call(
        functools.partial(finish, kk),
        out_shape=(grid_like, weight_like, grid_like),
        in_specs=[hbm] * 5,
        out_specs=(hbm,) * 3,
        scratch_shapes=[
            pltpu.VMEM((side, KL, HALVES * 2 * XL, cells), BF16),
            pltpu.VMEM((XL, cells, NZ), F32),
            pltpu.VMEM((kk, NZ), BF16),
            pltpu.VMEM((4, kk * XL, 128), F32),
            pltpu.VMEM(field.shape, BF16),
            pltpu.VMEM(field.shape, BF16),
            pltpu.VMEM(weight.shape, BF16),
            pltpu.SemaphoreType.DMA((21,)),
        ],
        compiler_params=pltpu.CompilerParams(vmem_limit_bytes=VMEM_BYTES),
        name="field_gradient",
    )(*parts, table)
    return act, fgrad, wgrad


def solution(mesh):
    wide, narrow = mesh.shape["wide"], mesh.shape["narrow"]
    return jax.shard_map(
        functools.partial(on_device, wide, narrow),
        mesh=mesh,
        in_specs=(
            P(None, "wide", "narrow", None),
            P("wide", "narrow", None, None),
            P(),
            P(None, "wide", "narrow", None),
        ),
        out_specs=(
            P(None, "wide", "narrow", None),
            P(None, "wide", "narrow", None),
            P("wide", "narrow", None, None),
        ),
        check_vma=False,
    )
```

```python
import functools

import jax
import jax.numpy as jnp
import ml_dtypes
import numpy as np
from jax import lax
from jax.experimental import pallas as pl
from jax.experimental.pallas import tpu as pltpu
from jax.sharding import PartitionSpec as P

C = 32
XL = 8
YL = 16
KXL = 6
KL = 3
NZ = 128
VMEM_BYTES = 64 * 1024 * 1024
MESH = pl.DeviceIdType.MESH
F32 = jnp.float32
BF16 = jnp.bfloat16


def angles(extent, kept, two_sided):
    positions = np.arange(kept)
    frequency = (
        np.where(positions < kept // 2, positions, positions + extent - kept)
        if two_sided
        else positions
    )
    phases = np.arange(extent)[:, None] * frequency[None, :] % extent
    theta = 2.0 * np.pi * phases / extent
    rounded = lambda t: t.astype(np.float32).astype(ml_dtypes.bfloat16).astype(np.float32)
    return rounded(np.cos(theta)), rounded(np.sin(theta))


def tables(wide, narrow, ky):
    nx, ny, kx, kz = XL * wide, YL * narrow, KXL * narrow, KL * wide
    cx, sx = angles(nx, kx, True)
    cy, sy = angles(ny, ky, True)
    cz, sz = angles(NZ, kz, False)
    z_rows = np.stack([cz, -sz], axis=-1).reshape(NZ, wide, KL, 2)
    z_fwd = z_rows.transpose(2, 1, 3, 0).reshape(KL * wide * 2, NZ)
    fwd = lambda c, s: np.stack([np.stack([c, s]), np.stack([-s, c])])
    inv = lambda c, s: np.stack([np.stack([c, -s]), np.stack([s, c])])
    fx = fwd(cx, sx).reshape(2, 2, wide, XL, narrow, KXL)
    x_fwd = fx.transpose(5, 0, 4, 2, 1, 3).reshape(KXL * 2 * narrow, wide * 2 * XL)
    ix = inv(cx, sx).reshape(2, 2, wide, XL, narrow, KXL)
    x_inv = ix.transpose(2, 0, 3, 5, 1, 4).reshape(wide * 2 * XL, KXL * 2 * narrow)
    fy = fwd(cy, sy).reshape(2, 2, narrow, YL, ky)
    y_fwd = fy.transpose(0, 4, 2, 1, 3).reshape(2 * ky, narrow * 2 * YL)
    y_fwd_split = fy.transpose(1, 0, 4, 2, 3).reshape(4 * ky, narrow * YL)
    iy = inv(cy, sy).reshape(2, 2, narrow, YL, ky)
    y_inv = iy.transpose(2, 0, 3, 1, 4).reshape(narrow * 2 * YL, 2 * ky)
    y_inv_split = iy.transpose(0, 2, 3, 1, 4).reshape(2 * narrow * YL, 2 * ky)
    found = (z_fwd, x_fwd, x_inv, y_fwd, y_fwd_split, y_inv, y_inv_split)
    places, blocks, row = [], [], 0
    for t in found:
        rows, columns = t.shape
        places.append((row, rows, columns))
        for first in range(0, columns, 128):
            block = t[:, first : first + 128]
            blocks.append(np.pad(block, ((0, 0), (0, 128 - block.shape[1]))))
            row += rows
    return places, np.concatenate(blocks).astype(ml_dtypes.bfloat16)


def read_table(table, place):
    row, rows, columns = place
    blocks = [
        table[row + i * rows : row + (i + 1) * rows, : min(128, columns - first)]
        for i, first in enumerate(range(0, columns, 128))
    ]
    return jnp.concatenate(blocks, axis=1) if len(blocks) > 1 else blocks[0]


def dot(a, b, dims=((1,), (0,))):
    return lax.dot_general(a, b, (dims, ((), ())), preferred_element_type=F32)


def ones_where(condition):
    return jnp.where(condition, 1.0, 0.0).astype(BF16)


def kernel(
    wide, narrow, ky, total, places,
    field_hbm, cot_hbm, weight_hbm, pw_hbm, table_hbm,
    act_hbm, wgrad_hbm, back_hbm, near_hbm,
    *scratch,
):
    (
        table, field, cot, weight, pw, act, wgrad, zi, near, zs, slope, spec, sums, prods, mix, t1, t1_last, t2,
        perm, perm_t, pw_fwd, pw_back, repeat, tile, group_sum,
        fs, fr, ls, lr, ns, nr,
        fs_sem, fr_sem, ls_sem, lr_sem, ns_sem, nr_sem, load_sem, store_sem,
    ) = scratch
    w = lax.axis_index("wide")
    n = lax.axis_index("narrow")
    cells = C * YL
    kk = KL * wide * 2
    rows_j = wide * 2 * XL
    modes = KXL * 2 * ky

    z_fwd, x_fwd, x_inv, y_fwd, y_fwd_split, y_inv, y_inv_split = [
        functools.partial(read_table, table, place) for place in places
    ]
    z_part = pl.ds(0, kk)
    other = pl.ds(kk, table.shape[0] - kk)
    loads = [
        pltpu.make_async_copy(src, dst, load_sem.at[i])
        for i, (src, dst) in enumerate(
            (
                (field_hbm.at[pl.ds(0, C // 2)], field.at[pl.ds(0, C // 2)]),
                (table_hbm.at[z_part], table.at[z_part]),
                (field_hbm.at[pl.ds(C // 2, C // 2)], field.at[pl.ds(C // 2, C // 2)]),
                (pw_hbm, pw),
                (table_hbm.at[other], table.at[other]),
                (cot_hbm, cot),
                (weight_hbm, weight),
            )
        )
    ]
    for load in loads[:5]:
        load.start()

    barrier = pltpu.get_barrier_semaphore()

    half = narrow // 2
    flip = lax.rem(n + half, narrow)

    @pl.loop(0, wide)
    def _(d):
        pl.semaphore_signal(
            barrier, inc=1, device_id={"wide": d, "narrow": flip}, device_id_type=MESH
        )

    @pl.loop(1, narrow)
    def _(d):
        pl.semaphore_signal(
            barrier, inc=1, device_id={"narrow": lax.rem(n + d, narrow)}, device_id_type=MESH
        )

    row = lax.broadcasted_iota(jnp.int32, (cells, cells), 0)
    col = lax.broadcasted_iota(jnp.int32, (cells, cells), 1)
    lane = lax.broadcasted_iota(jnp.int32, (1, 128), 1) >> 5

    def shift(value, groups):
        amount = (groups * 32) % 128
        return value if amount == 0 else pltpu.roll(value, amount, 1)

    def pick(pieces):
        acc = pieces[0]
        for s, piece in enumerate(pieces[1:], 1):
            acc = jnp.where(lane == s, piece, acc)
        return acc

    def exchange(low, high, groups, first):
        return (
            jnp.where(first, low, shift(high, groups)),
            jnp.where(first, shift(low, -groups), high),
        )

    def transpose_groups(p):
        p0, p2 = exchange(p[0], p[2], 2, lane < 2)
        p1, p3 = exchange(p[1], p[3], 2, lane < 2)
        p0, p1 = exchange(p0, p1, 1, (lane & 1) == 0)
        p2, p3 = exchange(p2, p3, 1, (lane & 1) == 0)
        return [p0, p1, p2, p3]

    def depth(x, hb, block):
        out = dot(z_fwd(), block, ((1,), (1,)))
        for i in range(2):
            zs[2 * hb + i, pl.ds(x, kk, stride=XL), :] = out[:, i * 128 : (i + 1) * 128]

    def send_wide(src, dst, send_sem, recv_sem):
        @pl.loop(0, wide)
        def _(d):
            to = lax.rem(w + d, wide)
            pltpu.make_async_remote_copy(
                src_ref=src(to),
                dst_ref=dst(w),
                send_sem=send_sem,
                recv_sem=recv_sem,
                device_id={"wide": to, "narrow": flip},
                device_id_type=MESH,
            ).start()

    def wait(ref, sem):
        pltpu.make_async_copy(ref, ref, sem).wait()

    def send_first(a, hb):
        send_wide(
            lambda to: fs.at[a, to, hb], lambda me: fr.at[a, me, hb],
            fs_sem.at[a, hb], fr_sem.at[a, hb],
        )

    def wait_first(buffer, sem, a, hb):
        wait(buffer.at[a, pl.ds(0, wide), hb], sem.at[a, hb])

    chunks = (pl.ds(0, KL - 1), pl.ds(KL - 1, 1))

    def send_last(a, c):
        send_wide(
            lambda to: ls.at[a, to, chunks[c]], lambda me: lr.at[a, me, chunks[c]],
            ls_sem.at[a, c], lr_sem.at[a, c],
        )

    def wait_last(buffer, sem, a, c):
        wait(buffer.at[a, pl.ds(0, wide), chunks[c]], sem.at[a, c])

    def send_narrow(a, i, j, take, slot):
        nr[a, i, j, slot] = ns[a, i, j, take(n)]

        @pl.loop(1, narrow)
        def _(d):
            to = lax.rem(n + d, narrow)
            pltpu.make_async_remote_copy(
                src_ref=ns.at[a, i, j, take(to)],
                dst_ref=nr.at[a, i, j, slot],
                send_sem=ns_sem.at[a, i, j],
                recv_sem=nr_sem.at[a, i, j],
                device_id={"narrow": to},
                device_id_type=MESH,
            ).start()

    def wait_narrow(buffer, sem, a, i, j):
        wait(buffer.at[a, i, j, pl.ds(0, narrow - 1)], sem.at[a, i, j])

    def part(j):
        return pl.ds(pl.multiple_of(j * rows_j, rows_j), rows_j)

    def depth_out(a, hb):
        @pl.loop(0, KL)
        def _(j):
            for i in range(2):
                block = zs[2 * hb + i, part(j), :].astype(BF16).reshape(wide, 2 * XL, 128)
                fs[a, :, hb, j, :, i * 128 : (i + 1) * 128] = block

        send_first(a, hb)

    def x_forward(a, j):
        block = [fr[a, :, hb, j].reshape(rows_j, 256) for hb in range(2)]
        out = dot(x_fwd(), jnp.concatenate(block, axis=1))
        out = dot(out.astype(BF16), perm[...])
        for yb in range(4):

            def piece(kx, ri):
                first = (kx * 2 + ri) * narrow
                return out[first : first + narrow, yb * 128 : (yb + 1) * 128]

            for ri in range(2):
                for g, value in enumerate(transpose_groups([piece(s, ri) for s in range(4)])):
                    t1[pl.ds(ri * YL + 4 * yb + g, narrow, stride=2 * YL), :] = value
            last = transpose_groups([piece(4 + s % 2, s // 2) for s in range(4)])
            for g, value in enumerate(last):
                t1_last[pl.ds(4 * yb + g, narrow, stride=YL), :] = value
        ns[a, 0, j, :, : 2 * YL, :] = t1[...].astype(BF16).reshape(narrow, 2 * YL, 128)
        ns[a, 0, j, :, 2 * YL :, :] = t1_last[...].astype(BF16).reshape(narrow, YL, 128)
        send_narrow(a, 0, j, lambda to: to, flip)

    def y_forward(a, j):
        wait_narrow(nr, nr_sem, a, 0, j)
        first = dot(y_fwd(), nr[a, 0, j, :, : 2 * YL, :].reshape(narrow * 2 * YL, 128))
        both = dot(y_fwd_split(), nr[a, 0, j, :, 2 * YL :, :].reshape(narrow * YL, 128))
        last = both[: 2 * ky] + shift(both[2 * ky :], 2)
        for kx in range(KXL):
            source = first if kx < 4 else last
            spec[a, j, kx * 2 * ky : (kx + 1) * 2 * ky, :] = shift(source, -(kx % 4)).astype(BF16)

    def scale(j):
        return jnp.where(w * KL + j == 0, 1.0, 2.0).astype(F32) / total

    def weights(j, kx, b):
        return (
            weight[j, kx, :, b * 256 : (b + 1) * 256].astype(F32),
            weight[j, kx, :, 1024 + b * 256 : 1024 + (b + 1) * 256].astype(F32),
        )

    def mode_rows(kx):
        return slice(kx * 2 * ky, kx * 2 * ky + ky), slice(kx * 2 * ky + ky, (kx + 1) * 2 * ky)

    def place(summed):
        for lb in range(2):
            found = [
                summed[kx * 2 * ky : (kx + 1) * 2 * ky] for kx in range(4 * lb, min(4 * lb + 4, KXL))
            ]
            mix[lb] = pick(found).astype(BF16)

    def mix_forward(j):
        for b in range(4):
            rep = dot(spec[0, j], repeat[:, b * 256 : (b + 1) * 256])
            for kx in range(KXL):
                re, im = mode_rows(kx)
                w_r, w_i = weights(j, kx, b)
                p_r = rep[re] * w_r - rep[im] * w_i
                p_i = rep[re] * w_i + rep[im] * w_r
                p_r = p_r[:, :128] + p_r[:, 128:]
                p_i = p_i[:, :128] + p_i[:, 128:]
                sums[re, :] = p_r if b == 0 else sums[re, :] + p_r
                sums[im, :] = p_i if b == 0 else sums[im, :] + p_i
        acc = sums[...] * scale(j)
        acc = acc + shift(acc, 2)
        acc = acc + shift(acc, 1)
        place(acc)

    def mix_back(j):
        sums[...] = dot(spec[1, j], tile[...])
        for kx in range(KXL):
            re, im = mode_rows(kx)
            g_r = jnp.concatenate([sums[re, :]] * 2, axis=1)
            g_i = jnp.concatenate([sums[im, :]] * 2, axis=1)
            for b in range(4):
                w_r, w_i = weights(j, kx, b)
                lanes = slice(b * 256, (b + 1) * 256)
                prods[re, lanes] = (w_r * g_r + w_i * g_i).astype(BF16)
                prods[im, lanes] = (w_r * g_i - w_i * g_r).astype(BF16)
        place(dot(prods[...], group_sum[...]) * scale(j))

    def weight_gradient(j):
        sums[...] = dot(spec[1, j], tile[...]) * scale(j)
        for b in range(4):
            rep = dot(spec[0, j], repeat[:, b * 256 : (b + 1) * 256])
            for kx in range(KXL):
                re, im = mode_rows(kx)
                g_r = jnp.concatenate([sums[re, :]] * 2, axis=1)
                g_i = jnp.concatenate([sums[im, :]] * 2, axis=1)
                wgrad[j, kx, :, b * 256 : (b + 1) * 256] = (rep[re] * g_r + rep[im] * g_i).astype(BF16)
                wgrad[j, kx, :, 1024 + b * 256 : 1024 + (b + 1) * 256] = (
                    rep[re] * g_i - rep[im] * g_r
                ).astype(BF16)

    def y_inverse(a, j):
        first = dot(y_inv(), mix[0]).astype(BF16)
        ns[a, 1, j, :, : 2 * YL, :] = first.reshape(narrow, 2 * YL, 128)
        both = dot(y_inv_split(), mix[1])
        split = narrow * YL
        last = jnp.where(lane < 2, both[:split], shift(both[split:], 2)).astype(BF16)
        ns[a, 1, j, :, 2 * YL :, :] = last.reshape(narrow, YL, 128)
        send_narrow(a, 1, j, lambda to: lax.rem(to + half, narrow), n)

    def x_inverse(a, j):
        wait_narrow(nr, nr_sem, a, 1, j)
        t1[...] = nr[a, 1, j, :, : 2 * YL, :].reshape(narrow * 2 * YL, 128).astype(F32)
        t1_last[...] = nr[a, 1, j, :, 2 * YL :, :].reshape(narrow * YL, 128).astype(F32)
        for yb in range(4):
            lanes = slice(yb * 128, (yb + 1) * 128)
            ys = [4 * yb + g for g in range(4)]
            loaded = [
                [t1[pl.ds(ri * YL + y, narrow, stride=2 * YL), :] for y in ys] for ri in range(2)
            ]
            last = [t1_last[pl.ds(y, narrow, stride=YL), :] for y in ys]
            real, imag, last = [transpose_groups(p) for p in loaded + [last]]
            pairs = list(zip(real, imag)) + [(last[0], last[2]), (last[1], last[3])]
            for kx, pair in enumerate(pairs):
                t2[kx * 2 * narrow : (kx + 1) * 2 * narrow, lanes] = jnp.concatenate(
                    pair, axis=0
                ).astype(BF16)
        modes_cy = dot(t2[...], perm_t[...]).astype(BF16)
        out = dot(x_inv(), modes_cy).astype(BF16)
        ls[a, :, j] = out.reshape(wide, 2 * XL, cells)

    def store_gradient(j):
        return pltpu.make_async_copy(wgrad.at[j], wgrad_hbm.at[j], store_sem.at[4 + j])

    def make_gradient(j):
        weight_gradient(j)
        store_gradient(j).start()

    def each(step):
        @pl.loop(0, KL)
        def _(j):
            step(j)

    def through_modes(a):
        def mode_step(j):
            y_forward(a, j)
            mix_back(j) if a else mix_forward(j)
            y_inverse(a, j)

        for hb in range(2):
            wait_first(fr, fr_sem, a, hb)
        each(lambda j: x_forward(a, j))
        each(mode_step)

        @pl.loop(0, KL)
        def _(j):
            if a:

                @pl.when(j == KL - 1)
                def _():
                    make_gradient(0)

            x_inverse(a, j)

            for c, j_last in enumerate((KL - 2, KL - 1)):

                @pl.when(j == j_last)
                def _():
                    send_last(a, c)

        if a:
            pl.loop(1, KL)(make_gradient)

    def depth_in():
        for c in range(2):
            wait_last(lr, lr_sem, 0, c)
        for b in range(4):

            @pl.loop(0, KL)
            def _(j):
                block = lr[0, :, j, :, b * 128 : (b + 1) * 128].reshape(rows_j, 128)
                zi[b, part(j), :] = block.astype(F32)

    def pointwise(matrix, source):
        @pl.loop(0, XL // 2)
        def _(x):
            both = [source[:, 2 * x + i].reshape(cells, NZ) for i in range(2)]
            out = dot(matrix[...], jnp.concatenate(both, axis=1))
            for i in range(2):
                near[2 * x + i] = out[:, i * NZ : (i + 1) * NZ]

    loads[1].wait()
    for hb in range(2):
        loads[2 * hb].wait()
        for x in range(XL):
            depth(x, hb, field[hb * 16 : (hb + 1) * 16, x].reshape(256, NZ))
        if hb == 0:
            pl.semaphore_wait(barrier, wide + narrow - 1)
        depth_out(0, hb)

    for load in loads[5:]:
        load.start()
    loads[3].wait()
    loads[4].wait()
    perm[...] = ones_where(((row & 15) == (col >> 5)) & ((row >> 4) == (col & 31)))
    perm_t[...] = ones_where(((row >> 5) == (col & 15)) & ((row & 31) == (col >> 4)))
    spread_row = lax.broadcasted_iota(jnp.int32, (cells, C), 0)
    spread_col = lax.broadcasted_iota(jnp.int32, (cells, C), 1)
    spread = ones_where((spread_row >> 4) == spread_col)
    same_y = (row & 15) == (col & 15)
    behind = dot(dot(spread, pw[...]).astype(BF16), spread, ((1,), (1,)))
    pw_back[...] = jnp.where(same_y, behind, 0.0).astype(BF16)
    ahead = dot(dot(spread, pw[...], ((1,), (1,))).astype(BF16), spread, ((1,), (1,)))
    pw_fwd[...] = jnp.where(same_y, ahead, 0.0).astype(BF16)
    r_row = lax.broadcasted_iota(jnp.int32, (128, 1024), 0)
    r_col = lax.broadcasted_iota(jnp.int32, (128, 1024), 1)
    repeat[...] = ones_where(r_row == (r_col >> 5))
    t_row = lax.broadcasted_iota(jnp.int32, (128, 128), 0)
    t_col = lax.broadcasted_iota(jnp.int32, (128, 128), 1)
    tile[...] = ones_where(t_row == (t_col & 31))
    g_row = lax.broadcasted_iota(jnp.int32, (1024, 128), 0)
    g_col = lax.broadcasted_iota(jnp.int32, (1024, 128), 1)
    group_sum[...] = ones_where((g_row >> 5) == (g_col & 31))
    pointwise(pw_fwd, field)
    loads[5].wait()
    loads[6].wait()

    through_modes(0)
    depth_in()

    root = 0.7978845608028654

    @pl.loop(0, 2)
    def _(hb):
        rows = pl.ds(pl.multiple_of(hb * 256, 256), 256)
        group = pl.ds(hb * 16, 16)
        for x in range(XL):
            block = jnp.concatenate(
                [zi[2 * hb + i, pl.ds(x, kk, stride=XL), :].astype(BF16) for i in range(2)], axis=1
            )
            t = dot(block, z_fwd(), ((0,), (0,))) + near[x, rows, :]
            square = t * t
            gate = 0.5 + 0.5 * jnp.tanh(t * (root + (root * 0.044715) * square))
            out = t * gate
            act[group, x] = out.astype(BF16).reshape(16, YL, NZ)
            grad = gate + out * (1.0 - gate) * (2.0 * root + (6.0 * root * 0.044715) * square)
            up = cot[group, x].reshape(256, NZ).astype(F32)
            block = (up * grad).astype(BF16)
            slope[group, x] = block.reshape(16, YL, NZ)
            depth(x, hb, block)

        for i in range(2):

            @pl.when(hb == i)
            def _():
                depth_out(1, i)

    stores = [
        pltpu.make_async_copy(src, dst, store_sem.at[i])
        for i, (src, dst) in enumerate(
            (
                (act, act_hbm),
                (near, near_hbm),
                (lr.at[1, :, chunks[0]], back_hbm.at[:, chunks[0]]),
                (lr.at[1, :, chunks[1]], back_hbm.at[:, chunks[1]]),
            )
        )
    ]
    stores[0].start()
    pointwise(pw_back, slope)
    stores[1].start()
    through_modes(1)
    for c in range(2):
        wait_last(lr, lr_sem, 1, c)
        stores[2 + c].start()

    for a in range(2):
        for i in range(2):
            wait_first(fs, fs_sem, a, i)
            wait_last(ls, ls_sem, a, i)
            for j in range(KL):
                wait_narrow(ns, ns_sem, a, i, j)

    each(lambda j: store_gradient(j).wait())
    for store in stores:
        store.wait()


def finish(
    kk, act_in, wgrad_in, back_hbm, near_hbm, table_hbm,
    act_hbm, wgrad_hbm, fgrad_hbm,
    back, near, table, zi, fgrad, act, wgrad, sem,
):
    load_table = pltpu.make_async_copy(table_hbm.at[pl.ds(0, kk)], table, sem.at[0])
    load_table.start()
    loads, passed, stores = [], [], []
    for hb in range(2):
        part = pl.ds(hb * 256, 256)
        loads.append(
            (
                pltpu.make_async_copy(
                    back_hbm.at[:, :, :, part], back.at[:, :, :, part], sem.at[1 + hb]
                ),
                pltpu.make_async_copy(near_hbm.at[:, part], near.at[:, part], sem.at[5 + hb]),
            )
        )
        for load in loads[-1]:
            load.start()
    whole = [(act_in, act, act_hbm)] + [
        (wgrad_in.at[j], wgrad.at[j], wgrad_hbm.at[j]) for j in range(KL)
    ]
    for i, (src, held, dst) in enumerate(whole):
        passed.append(
            (
                pltpu.make_async_copy(src, held, sem.at[9 + i]),
                pltpu.make_async_copy(held, dst, sem.at[13 + i]),
            )
        )
        passed[-1][0].start()
    load_table.wait()
    for hb in range(2):
        for load in loads[hb]:
            load.wait()
        for b in (2 * hb, 2 * hb + 1):
            for j in range(KL):
                rows = back.shape[0] * 2 * XL
                block = back[:, j, :, b * 128 : (b + 1) * 128].reshape(rows, 128)
                zi[b, j * rows : (j + 1) * rows, :] = block.astype(F32)
        for x in range(XL):
            block = jnp.concatenate(
                [zi[2 * hb + i, pl.ds(x, kk, stride=XL), :].astype(BF16) for i in range(2)], axis=1
            )
            rows = slice(hb * 256, (hb + 1) * 256)
            t = dot(block, table[...], ((0,), (0,))) + near[x, rows, :]
            fgrad[hb * 16 : (hb + 1) * 16, x] = t.astype(BF16).reshape(16, YL, NZ)
        group = pl.ds(hb * 16, 16)
        stores.append(pltpu.make_async_copy(fgrad.at[group], fgrad_hbm.at[group], sem.at[17 + hb]))
        stores[-1].start()
        for i in (2 * hb, 2 * hb + 1):
            passed[i][0].wait()
            passed[i][1].start()
            stores.append(passed[i][1])
    for store in stores:
        store.wait()


def on_device(wide, narrow, field, weight, pw, cot):
    ky = weight.shape[2]
    total = float(XL * wide * YL * narrow * NZ)
    places, packed = tables(wide, narrow, ky)
    table = jnp.asarray(packed)
    cells = C * YL
    kk = KL * wide * 2
    modes = KXL * 2 * ky
    hbm = pl.BlockSpec(memory_space=pl.ANY)
    grid_like = jax.ShapeDtypeStruct(field.shape, BF16)
    weight_like = jax.ShapeDtypeStruct(weight.shape, BF16)
    parts = pl.pallas_call(
        functools.partial(kernel, wide, narrow, ky, total, places),
        out_shape=(
            grid_like,
            weight_like,
            jax.ShapeDtypeStruct((wide, KL, 2 * XL, cells), BF16),
            jax.ShapeDtypeStruct((XL, cells, NZ), F32),
        ),
        in_specs=[hbm] * 5,
        out_specs=(hbm,) * 4,
        scratch_shapes=[
            pltpu.VMEM(table.shape, BF16),
            pltpu.VMEM(field.shape, BF16),
            pltpu.VMEM(cot.shape, BF16),
            pltpu.VMEM(weight.shape, BF16),
            pltpu.VMEM(pw.shape, BF16),
            pltpu.VMEM(field.shape, BF16),
            pltpu.VMEM(weight.shape, BF16),
            pltpu.VMEM((4, kk * XL, 128), F32),
            pltpu.VMEM((XL, cells, NZ), F32),
            pltpu.VMEM((4, kk * XL, 128), F32),
            pltpu.VMEM(field.shape, BF16),
            pltpu.VMEM((2, KL, modes, 128), BF16),
            pltpu.VMEM((modes, 128), F32),
            pltpu.VMEM((modes, 1024), BF16),
            pltpu.VMEM((2, 2 * ky, 128), BF16),
            pltpu.VMEM((narrow * 2 * YL, 128), F32),
            pltpu.VMEM((narrow * YL, 128), F32),
            pltpu.VMEM((KXL * narrow * 2, cells), BF16),
            pltpu.VMEM((cells, cells), BF16),
            pltpu.VMEM((cells, cells), BF16),
            pltpu.VMEM((cells, cells), BF16),
            pltpu.VMEM((cells, cells), BF16),
            pltpu.VMEM((128, 1024), BF16),
            pltpu.VMEM((128, 128), BF16),
            pltpu.VMEM((1024, 128), BF16),
            pltpu.VMEM((2, wide, 2, KL, 2 * XL, 256), BF16),
            pltpu.VMEM((2, wide, 2, KL, 2 * XL, 256), BF16),
            pltpu.VMEM((2, wide, KL, 2 * XL, cells), BF16),
            pltpu.VMEM((2, wide, KL, 2 * XL, cells), BF16),
            pltpu.VMEM((2, 2, KL, narrow, 3 * YL, 128), BF16),
            pltpu.VMEM((2, 2, KL, narrow, 3 * YL, 128), BF16),
            pltpu.SemaphoreType.DMA((2, 2)),
            pltpu.SemaphoreType.DMA((2, 2)),
            pltpu.SemaphoreType.DMA((2, 2)),
            pltpu.SemaphoreType.DMA((2, 2)),
            pltpu.SemaphoreType.DMA((2, 2, KL)),
            pltpu.SemaphoreType.DMA((2, 2, KL)),
            pltpu.SemaphoreType.DMA((7,)),
            pltpu.SemaphoreType.DMA((4 + KL,)),
        ],
        compiler_params=pltpu.CompilerParams(
            collective_id=0, has_side_effects=True, vmem_limit_bytes=VMEM_BYTES
        ),
        name="spectral_layer",
    )(field, cot, weight, pw, table)
    act, wgrad, fgrad = pl.pallas_call(
        functools.partial(finish, kk),
        out_shape=(grid_like, weight_like, grid_like),
        in_specs=[hbm] * 5,
        out_specs=(hbm,) * 3,
        scratch_shapes=[
            pltpu.VMEM((wide, KL, 2 * XL, cells), BF16),
            pltpu.VMEM((XL, cells, NZ), F32),
            pltpu.VMEM((kk, NZ), BF16),
            pltpu.VMEM((4, kk * XL, 128), F32),
            pltpu.VMEM(field.shape, BF16),
            pltpu.VMEM(field.shape, BF16),
            pltpu.VMEM(weight.shape, BF16),
            pltpu.SemaphoreType.DMA((21,)),
        ],
        compiler_params=pltpu.CompilerParams(vmem_limit_bytes=VMEM_BYTES),
        name="field_gradient",
    )(*parts, table)
    return act, fgrad, wgrad


def solution(mesh):
    wide, narrow = mesh.shape["wide"], mesh.shape["narrow"]
    return jax.shard_map(
        functools.partial(on_device, wide, narrow),
        mesh=mesh,
        in_specs=(
            P(None, "wide", "narrow", None),
            P("wide", "narrow", None, None),
            P(),
            P(None, "wide", "narrow", None),
        ),
        out_specs=(
            P(None, "wide", "narrow", None),
            P(None, "wide", "narrow", None),
            P("wide", "narrow", None, None),
        ),
        check_vma=False,
    )
```

```python
import functools

import jax
import jax.numpy as jnp
import ml_dtypes
import numpy as np
from jax import lax
from jax.experimental import pallas as pl
from jax.experimental.pallas import tpu as pltpu
from jax.sharding import PartitionSpec as P

C = 32
XL = 8
YL = 16
KXL = 6
KL = 3
NZ = 128
VMEM_BYTES = 64 * 1024 * 1024
MESH = pl.DeviceIdType.MESH
F32 = jnp.float32
BF16 = jnp.bfloat16


def angles(extent, kept, two_sided):
    positions = np.arange(kept)
    frequency = (
        np.where(positions < kept // 2, positions, positions + extent - kept)
        if two_sided
        else positions
    )
    phases = np.arange(extent)[:, None] * frequency[None, :] % extent
    theta = 2.0 * np.pi * phases / extent
    rounded = lambda t: t.astype(np.float32).astype(ml_dtypes.bfloat16).astype(np.float32)
    return rounded(np.cos(theta)), rounded(np.sin(theta))


def tables(wide, narrow, ky):
    nx, ny, kx, kz = XL * wide, YL * narrow, KXL * narrow, KL * wide
    cx, sx = angles(nx, kx, True)
    cy, sy = angles(ny, ky, True)
    cz, sz = angles(NZ, kz, False)
    z_rows = np.stack([cz, -sz], axis=-1).reshape(NZ, wide, KL, 2)
    z_fwd = z_rows.transpose(2, 1, 3, 0).reshape(KL * wide * 2, NZ)
    fwd = lambda c, s: np.stack([np.stack([c, s]), np.stack([-s, c])])
    inv = lambda c, s: np.stack([np.stack([c, -s]), np.stack([s, c])])
    fx = fwd(cx, sx).reshape(2, 2, wide, XL, narrow, KXL)
    x_fwd = fx.transpose(5, 0, 4, 2, 1, 3).reshape(KXL * 2 * narrow, wide * 2 * XL)
    ix = inv(cx, sx).reshape(2, 2, wide, XL, narrow, KXL)
    x_inv = ix.transpose(2, 0, 3, 5, 1, 4).reshape(wide * 2 * XL, KXL * 2 * narrow)
    fy = fwd(cy, sy).reshape(2, 2, narrow, YL, ky)
    y_fwd = fy.transpose(0, 4, 2, 1, 3).reshape(2 * ky, narrow * 2 * YL)
    y_fwd_split = fy.transpose(1, 0, 4, 2, 3).reshape(4 * ky, narrow * YL)
    iy = inv(cy, sy).reshape(2, 2, narrow, YL, ky)
    y_inv = iy.transpose(2, 0, 3, 1, 4).reshape(narrow * 2 * YL, 2 * ky)
    y_inv_split = iy.transpose(0, 2, 3, 1, 4).reshape(2 * narrow * YL, 2 * ky)
    found = (z_fwd, x_fwd, x_inv, y_fwd, y_fwd_split, y_inv, y_inv_split)
    places, blocks, row = [], [], 0
    for t in found:
        rows, columns = t.shape
        places.append((row, rows, columns))
        for first in range(0, columns, 128):
            block = t[:, first : first + 128]
            blocks.append(np.pad(block, ((0, 0), (0, 128 - block.shape[1]))))
            row += rows
    return places, np.concatenate(blocks).astype(ml_dtypes.bfloat16)


def read_table(table, place):
    row, rows, columns = place
    blocks = [
        table[row + i * rows : row + (i + 1) * rows, : min(128, columns - first)]
        for i, first in enumerate(range(0, columns, 128))
    ]
    return jnp.concatenate(blocks, axis=1) if len(blocks) > 1 else blocks[0]


def dot(a, b, dims=((1,), (0,))):
    return lax.dot_general(a, b, (dims, ((), ())), preferred_element_type=F32)


def ones_where(condition):
    return jnp.where(condition, 1.0, 0.0).astype(BF16)


def kernel(
    wide, narrow, ky, total, places,
    field_hbm, cot_hbm, weight_hbm, pw_hbm, table_hbm,
    act_hbm, wgrad_hbm, back_hbm, near_hbm,
    *scratch,
):
    (
        table, field, cot, weight, pw, act, wgrad, zi, near, zs, slope, spec, sums, prods, mix, t1, t1_last, t2,
        perm, perm_t, pw_fwd, pw_back, repeat, tile, group_sum,
        fs, fr, ls, lr, ns, nr,
        fs_sem, fr_sem, ls_sem, lr_sem, ns_sem, nr_sem, load_sem, store_sem,
    ) = scratch
    w = lax.axis_index("wide")
    n = lax.axis_index("narrow")
    cells = C * YL
    kk = KL * wide * 2
    rows_j = wide * 2 * XL
    modes = KXL * 2 * ky

    z_fwd, x_fwd, x_inv, y_fwd, y_fwd_split, y_inv, y_inv_split = [
        functools.partial(read_table, table, place) for place in places
    ]
    z_part = pl.ds(0, kk)
    other = pl.ds(kk, table.shape[0] - kk)
    loads = [
        pltpu.make_async_copy(src, dst, load_sem.at[i])
        for i, (src, dst) in enumerate(
            (
                (field_hbm.at[pl.ds(0, C // 2)], field.at[pl.ds(0, C // 2)]),
                (table_hbm.at[z_part], table.at[z_part]),
                (field_hbm.at[pl.ds(C // 2, C // 2)], field.at[pl.ds(C // 2, C // 2)]),
                (pw_hbm, pw),
                (table_hbm.at[other], table.at[other]),
                (cot_hbm, cot),
                (weight_hbm, weight),
            )
        )
    ]
    for load in loads[:5]:
        load.start()

    barrier = pltpu.get_barrier_semaphore()

    half = narrow // 2
    flip = lax.rem(n + half, narrow)

    @pl.loop(0, wide)
    def _(d):
        pl.semaphore_signal(
            barrier, inc=1, device_id={"wide": d, "narrow": flip}, device_id_type=MESH
        )

    @pl.loop(1, narrow)
    def _(d):
        pl.semaphore_signal(
            barrier, inc=1, device_id={"narrow": lax.rem(n + d, narrow)}, device_id_type=MESH
        )

    row = lax.broadcasted_iota(jnp.int32, (cells, cells), 0)
    col = lax.broadcasted_iota(jnp.int32, (cells, cells), 1)
    lane = lax.broadcasted_iota(jnp.int32, (1, 128), 1) >> 5

    def shift(value, groups):
        amount = (groups * 32) % 128
        return value if amount == 0 else pltpu.roll(value, amount, 1)

    def pick(pieces):
        acc = pieces[0]
        for s, piece in enumerate(pieces[1:], 1):
            acc = jnp.where(lane == s, piece, acc)
        return acc

    def exchange(low, high, groups, first):
        return (
            jnp.where(first, low, shift(high, groups)),
            jnp.where(first, shift(low, -groups), high),
        )

    def transpose_groups(p):
        p0, p2 = exchange(p[0], p[2], 2, lane < 2)
        p1, p3 = exchange(p[1], p[3], 2, lane < 2)
        p0, p1 = exchange(p0, p1, 1, (lane & 1) == 0)
        p2, p3 = exchange(p2, p3, 1, (lane & 1) == 0)
        return [p0, p1, p2, p3]

    def depth(x, hb, block):
        out = dot(z_fwd(), block, ((1,), (1,)))
        for i in range(2):
            zs[2 * hb + i, pl.ds(x, kk, stride=XL), :] = out[:, i * 128 : (i + 1) * 128]

    def send_wide(src, dst, send_sem, recv_sem):
        @pl.loop(0, wide)
        def _(d):
            to = lax.rem(w + d, wide)
            pltpu.make_async_remote_copy(
                src_ref=src(to),
                dst_ref=dst(w),
                send_sem=send_sem,
                recv_sem=recv_sem,
                device_id={"wide": to, "narrow": flip},
                device_id_type=MESH,
            ).start()

    def wait(ref, sem):
        pltpu.make_async_copy(ref, ref, sem).wait()

    def send_first(a, hb):
        send_wide(
            lambda to: fs.at[a, to, hb], lambda me: fr.at[a, me, hb],
            fs_sem.at[a, hb], fr_sem.at[a, hb],
        )

    def wait_first(buffer, sem, a, hb):
        wait(buffer.at[a, pl.ds(0, wide), hb], sem.at[a, hb])

    chunks = (pl.ds(0, KL - 1), pl.ds(KL - 1, 1))

    def send_last(a, c):
        send_wide(
            lambda to: ls.at[a, to, chunks[c]], lambda me: lr.at[a, me, chunks[c]],
            ls_sem.at[a, c], lr_sem.at[a, c],
        )

    def wait_last(buffer, sem, a, c):
        wait(buffer.at[a, pl.ds(0, wide), chunks[c]], sem.at[a, c])

    def send_narrow(a, i, j, take, slot):
        nr[a, i, j, slot] = ns[a, i, j, take(n)]

        @pl.loop(1, narrow)
        def _(d):
            to = lax.rem(n + d, narrow)
            pltpu.make_async_remote_copy(
                src_ref=ns.at[a, i, j, take(to)],
                dst_ref=nr.at[a, i, j, slot],
                send_sem=ns_sem.at[a, i, j],
                recv_sem=nr_sem.at[a, i, j],
                device_id={"narrow": to},
                device_id_type=MESH,
            ).start()

    def wait_narrow(buffer, sem, a, i, j):
        wait(buffer.at[a, i, j, pl.ds(0, narrow - 1)], sem.at[a, i, j])

    def part(j):
        return pl.ds(pl.multiple_of(j * rows_j, rows_j), rows_j)

    def depth_out(a, hb):
        @pl.loop(0, KL)
        def _(j):
            for i in range(2):
                block = zs[2 * hb + i, part(j), :].astype(BF16).reshape(wide, 2 * XL, 128)
                fs[a, :, hb, j, :, i * 128 : (i + 1) * 128] = block

        send_first(a, hb)

    def x_forward(a, j):
        block = [fr[a, :, hb, j].reshape(rows_j, 256) for hb in range(2)]
        out = dot(x_fwd(), jnp.concatenate(block, axis=1))
        out = dot(out.astype(BF16), perm[...])
        for yb in range(4):

            def piece(kx, ri):
                first = (kx * 2 + ri) * narrow
                return out[first : first + narrow, yb * 128 : (yb + 1) * 128]

            for ri in range(2):
                for g, value in enumerate(transpose_groups([piece(s, ri) for s in range(4)])):
                    t1[pl.ds(ri * YL + 4 * yb + g, narrow, stride=2 * YL), :] = value
            last = transpose_groups([piece(4 + s % 2, s // 2) for s in range(4)])
            for g, value in enumerate(last):
                t1_last[pl.ds(4 * yb + g, narrow, stride=YL), :] = value
        ns[a, 0, j, :, : 2 * YL, :] = t1[...].astype(BF16).reshape(narrow, 2 * YL, 128)
        ns[a, 0, j, :, 2 * YL :, :] = t1_last[...].astype(BF16).reshape(narrow, YL, 128)
        send_narrow(a, 0, j, lambda to: to, flip)

    def y_forward(a, j):
        wait_narrow(nr, nr_sem, a, 0, j)
        first = dot(y_fwd(), nr[a, 0, j, :, : 2 * YL, :].reshape(narrow * 2 * YL, 128))
        both = dot(y_fwd_split(), nr[a, 0, j, :, 2 * YL :, :].reshape(narrow * YL, 128))
        last = both[: 2 * ky] + shift(both[2 * ky :], 2)
        for kx in range(KXL):
            source = first if kx < 4 else last
            spec[a, j, kx * 2 * ky : (kx + 1) * 2 * ky, :] = shift(source, -(kx % 4)).astype(BF16)

    def scale(j):
        return jnp.where(w * KL + j == 0, 1.0, 2.0).astype(F32) / total

    def weights(j, kx, b):
        return (
            weight[j, kx, :, b * 256 : (b + 1) * 256].astype(F32),
            weight[j, kx, :, 1024 + b * 256 : 1024 + (b + 1) * 256].astype(F32),
        )

    def mode_rows(kx):
        return slice(kx * 2 * ky, kx * 2 * ky + ky), slice(kx * 2 * ky + ky, (kx + 1) * 2 * ky)

    def place(summed):
        for lb in range(2):
            found = [
                summed[kx * 2 * ky : (kx + 1) * 2 * ky] for kx in range(4 * lb, min(4 * lb + 4, KXL))
            ]
            mix[lb] = pick(found).astype(BF16)

    def mix_forward(j):
        for b in range(4):
            rep = dot(spec[0, j], repeat[:, b * 256 : (b + 1) * 256])
            for kx in range(KXL):
                re, im = mode_rows(kx)
                w_r, w_i = weights(j, kx, b)
                p_r = rep[re] * w_r - rep[im] * w_i
                p_i = rep[re] * w_i + rep[im] * w_r
                p_r = p_r[:, :128] + p_r[:, 128:]
                p_i = p_i[:, :128] + p_i[:, 128:]
                sums[re, :] = p_r if b == 0 else sums[re, :] + p_r
                sums[im, :] = p_i if b == 0 else sums[im, :] + p_i
        acc = sums[...] * scale(j)
        acc = acc + shift(acc, 2)
        acc = acc + shift(acc, 1)
        place(acc)

    def mix_back(j):
        sums[...] = dot(spec[1, j], tile[...])
        for kx in range(KXL):
            re, im = mode_rows(kx)
            g_r = jnp.concatenate([sums[re, :]] * 2, axis=1)
            g_i = jnp.concatenate([sums[im, :]] * 2, axis=1)
            for b in range(4):
                w_r, w_i = weights(j, kx, b)
                lanes = slice(b * 256, (b + 1) * 256)
                prods[re, lanes] = (w_r * g_r + w_i * g_i).astype(BF16)
                prods[im, lanes] = (w_r * g_i - w_i * g_r).astype(BF16)
        place(dot(prods[...], group_sum[...]) * scale(j))

    def weight_gradient(j):
        sums[...] = dot(spec[1, j], tile[...]) * scale(j)
        for b in range(4):
            rep = dot(spec[0, j], repeat[:, b * 256 : (b + 1) * 256])
            for kx in range(KXL):
                re, im = mode_rows(kx)
                g_r = jnp.concatenate([sums[re, :]] * 2, axis=1)
                g_i = jnp.concatenate([sums[im, :]] * 2, axis=1)
                wgrad[j, kx, :, b * 256 : (b + 1) * 256] = (rep[re] * g_r + rep[im] * g_i).astype(BF16)
                wgrad[j, kx, :, 1024 + b * 256 : 1024 + (b + 1) * 256] = (
                    rep[re] * g_i - rep[im] * g_r
                ).astype(BF16)

    def y_inverse(a, j):
        first = dot(y_inv(), mix[0]).astype(BF16)
        ns[a, 1, j, :, : 2 * YL, :] = first.reshape(narrow, 2 * YL, 128)
        both = dot(y_inv_split(), mix[1])
        split = narrow * YL
        last = jnp.where(lane < 2, both[:split], shift(both[split:], 2)).astype(BF16)
        ns[a, 1, j, :, 2 * YL :, :] = last.reshape(narrow, YL, 128)
        send_narrow(a, 1, j, lambda to: lax.rem(to + half, narrow), n)

    def x_inverse(a, j):
        wait_narrow(nr, nr_sem, a, 1, j)
        t1[...] = nr[a, 1, j, :, : 2 * YL, :].reshape(narrow * 2 * YL, 128).astype(F32)
        t1_last[...] = nr[a, 1, j, :, 2 * YL :, :].reshape(narrow * YL, 128).astype(F32)
        for yb in range(4):
            lanes = slice(yb * 128, (yb + 1) * 128)
            ys = [4 * yb + g for g in range(4)]
            loaded = [
                [t1[pl.ds(ri * YL + y, narrow, stride=2 * YL), :] for y in ys] for ri in range(2)
            ]
            last = [t1_last[pl.ds(y, narrow, stride=YL), :] for y in ys]
            real, imag, last = [transpose_groups(p) for p in loaded + [last]]
            pairs = list(zip(real, imag)) + [(last[0], last[2]), (last[1], last[3])]
            for kx, pair in enumerate(pairs):
                t2[kx * 2 * narrow : (kx + 1) * 2 * narrow, lanes] = jnp.concatenate(
                    pair, axis=0
                ).astype(BF16)
        modes_cy = dot(t2[...], perm_t[...]).astype(BF16)
        out = dot(x_inv(), modes_cy).astype(BF16)
        ls[a, :, j] = out.reshape(wide, 2 * XL, cells)

    def store_gradient(j):
        return pltpu.make_async_copy(wgrad.at[j], wgrad_hbm.at[j], store_sem.at[4 + j])

    def make_gradient(j):
        weight_gradient(j)
        store_gradient(j).start()

    def each(step):
        @pl.loop(0, KL)
        def _(j):
            step(j)

    def through_modes(a):
        def mode_step(j):
            y_forward(a, j)
            mix_back(j) if a else mix_forward(j)
            y_inverse(a, j)

        for hb in range(2):
            wait_first(fr, fr_sem, a, hb)
        each(lambda j: x_forward(a, j))
        each(mode_step)

        @pl.loop(0, KL)
        def _(j):
            if a:

                @pl.when(j == KL - 1)
                def _():
                    make_gradient(0)

            x_inverse(a, j)

            for c, j_last in enumerate((KL - 2, KL - 1)):

                @pl.when(j == j_last)
                def _():
                    send_last(a, c)

        if a:
            pl.loop(1, KL)(make_gradient)

    def depth_in():
        for c in range(2):
            wait_last(lr, lr_sem, 0, c)
        for b in range(4):

            @pl.loop(0, KL)
            def _(j):
                block = lr[0, :, j, :, b * 128 : (b + 1) * 128].reshape(rows_j, 128)
                zi[b, part(j), :] = block.astype(F32)

    def pointwise(matrix, source):
        @pl.loop(0, XL // 2)
        def _(x):
            both = [source[:, 2 * x + i].reshape(cells, NZ) for i in range(2)]
            out = dot(matrix[...], jnp.concatenate(both, axis=1))
            for i in range(2):
                near[2 * x + i] = out[:, i * NZ : (i + 1) * NZ]

    loads[1].wait()
    for hb in range(2):
        loads[2 * hb].wait()
        @pl.loop(0, XL, unroll=2)
        def _(x):
            depth(x, hb, field[hb * 16 : (hb + 1) * 16, x].reshape(256, NZ))

        if hb == 0:
            pl.semaphore_wait(barrier, wide + narrow - 1)
        depth_out(0, hb)

    for load in loads[5:]:
        load.start()
    loads[3].wait()
    loads[4].wait()
    perm[...] = ones_where(((row & 15) == (col >> 5)) & ((row >> 4) == (col & 31)))
    perm_t[...] = ones_where(((row >> 5) == (col & 15)) & ((row & 31) == (col >> 4)))
    spread_row = lax.broadcasted_iota(jnp.int32, (cells, C), 0)
    spread_col = lax.broadcasted_iota(jnp.int32, (cells, C), 1)
    spread = ones_where((spread_row >> 4) == spread_col)
    same_y = (row & 15) == (col & 15)
    behind = dot(dot(spread, pw[...]).astype(BF16), spread, ((1,), (1,)))
    pw_back[...] = jnp.where(same_y, behind, 0.0).astype(BF16)
    ahead = dot(dot(spread, pw[...], ((1,), (1,))).astype(BF16), spread, ((1,), (1,)))
    pw_fwd[...] = jnp.where(same_y, ahead, 0.0).astype(BF16)
    r_row = lax.broadcasted_iota(jnp.int32, (128, 1024), 0)
    r_col = lax.broadcasted_iota(jnp.int32, (128, 1024), 1)
    repeat[...] = ones_where(r_row == (r_col >> 5))
    t_row = lax.broadcasted_iota(jnp.int32, (128, 128), 0)
    t_col = lax.broadcasted_iota(jnp.int32, (128, 128), 1)
    tile[...] = ones_where(t_row == (t_col & 31))
    g_row = lax.broadcasted_iota(jnp.int32, (1024, 128), 0)
    g_col = lax.broadcasted_iota(jnp.int32, (1024, 128), 1)
    group_sum[...] = ones_where((g_row >> 5) == (g_col & 31))
    pointwise(pw_fwd, field)
    loads[5].wait()
    loads[6].wait()

    through_modes(0)
    depth_in()

    root = 0.7978845608028654

    @pl.loop(0, 2)
    def _(hb):
        rows = pl.ds(pl.multiple_of(hb * 256, 256), 256)
        group = pl.ds(hb * 16, 16)

        @pl.loop(0, XL, unroll=2)
        def _(x):
            block = jnp.concatenate(
                [zi[2 * hb + i, pl.ds(x, kk, stride=XL), :].astype(BF16) for i in range(2)], axis=1
            )
            t = dot(block, z_fwd(), ((0,), (0,))) + near[x, rows, :]
            square = t * t
            gate = 0.5 + 0.5 * jnp.tanh(t * (root + (root * 0.044715) * square))
            out = t * gate
            act[group, x] = out.astype(BF16).reshape(16, YL, NZ)
            grad = gate + out * (1.0 - gate) * (2.0 * root + (6.0 * root * 0.044715) * square)
            up = cot[group, x].reshape(256, NZ).astype(F32)
            block = (up * grad).astype(BF16)
            slope[group, x] = block.reshape(16, YL, NZ)
            depth(x, hb, block)

        for i in range(2):

            @pl.when(hb == i)
            def _():
                depth_out(1, i)

    stores = [
        pltpu.make_async_copy(src, dst, store_sem.at[i])
        for i, (src, dst) in enumerate(
            (
                (act, act_hbm),
                (near, near_hbm),
                (lr.at[1, :, chunks[0]], back_hbm.at[:, chunks[0]]),
                (lr.at[1, :, chunks[1]], back_hbm.at[:, chunks[1]]),
            )
        )
    ]
    stores[0].start()
    pointwise(pw_back, slope)
    stores[1].start()
    through_modes(1)
    for c in range(2):
        wait_last(lr, lr_sem, 1, c)
        stores[2 + c].start()

    for a in range(2):
        for i in range(2):
            wait_first(fs, fs_sem, a, i)
            wait_last(ls, ls_sem, a, i)
            for j in range(KL):
                wait_narrow(ns, ns_sem, a, i, j)

    each(lambda j: store_gradient(j).wait())
    for store in stores:
        store.wait()


def finish(
    kk, act_in, wgrad_in, back_hbm, near_hbm, table_hbm,
    act_hbm, wgrad_hbm, fgrad_hbm,
    back, near, table, zi, fgrad, act, wgrad, sem,
):
    load_table = pltpu.make_async_copy(table_hbm.at[pl.ds(0, kk)], table, sem.at[0])
    load_table.start()
    loads, passed, stores = [], [], []
    for hb in range(2):
        part = pl.ds(hb * 256, 256)
        loads.append(
            (
                pltpu.make_async_copy(
                    back_hbm.at[:, :, :, part], back.at[:, :, :, part], sem.at[1 + hb]
                ),
                pltpu.make_async_copy(near_hbm.at[:, part], near.at[:, part], sem.at[5 + hb]),
            )
        )
        for load in loads[-1]:
            load.start()
    whole = [(act_in, act, act_hbm)] + [
        (wgrad_in.at[j], wgrad.at[j], wgrad_hbm.at[j]) for j in range(KL)
    ]
    for i, (src, held, dst) in enumerate(whole):
        passed.append(
            (
                pltpu.make_async_copy(src, held, sem.at[9 + i]),
                pltpu.make_async_copy(held, dst, sem.at[13 + i]),
            )
        )
        passed[-1][0].start()
    load_table.wait()
    for hb in range(2):
        for load in loads[hb]:
            load.wait()
        for b in (2 * hb, 2 * hb + 1):
            for j in range(KL):
                rows = back.shape[0] * 2 * XL
                block = back[:, j, :, b * 128 : (b + 1) * 128].reshape(rows, 128)
                zi[b, j * rows : (j + 1) * rows, :] = block.astype(F32)
        for x in range(XL):
            block = jnp.concatenate(
                [zi[2 * hb + i, pl.ds(x, kk, stride=XL), :].astype(BF16) for i in range(2)], axis=1
            )
            rows = slice(hb * 256, (hb + 1) * 256)
            t = dot(block, table[...], ((0,), (0,))) + near[x, rows, :]
            fgrad[hb * 16 : (hb + 1) * 16, x] = t.astype(BF16).reshape(16, YL, NZ)
        group = pl.ds(hb * 16, 16)
        stores.append(pltpu.make_async_copy(fgrad.at[group], fgrad_hbm.at[group], sem.at[17 + hb]))
        stores[-1].start()
        for i in (2 * hb, 2 * hb + 1):
            passed[i][0].wait()
            passed[i][1].start()
            stores.append(passed[i][1])
    for store in stores:
        store.wait()


def on_device(wide, narrow, field, weight, pw, cot):
    ky = weight.shape[2]
    total = float(XL * wide * YL * narrow * NZ)
    places, packed = tables(wide, narrow, ky)
    table = jnp.asarray(packed)
    cells = C * YL
    kk = KL * wide * 2
    modes = KXL * 2 * ky
    hbm = pl.BlockSpec(memory_space=pl.ANY)
    grid_like = jax.ShapeDtypeStruct(field.shape, BF16)
    weight_like = jax.ShapeDtypeStruct(weight.shape, BF16)
    parts = pl.pallas_call(
        functools.partial(kernel, wide, narrow, ky, total, places),
        out_shape=(
            grid_like,
            weight_like,
            jax.ShapeDtypeStruct((wide, KL, 2 * XL, cells), BF16),
            jax.ShapeDtypeStruct((XL, cells, NZ), F32),
        ),
        in_specs=[hbm] * 5,
        out_specs=(hbm,) * 4,
        scratch_shapes=[
            pltpu.VMEM(table.shape, BF16),
            pltpu.VMEM(field.shape, BF16),
            pltpu.VMEM(cot.shape, BF16),
            pltpu.VMEM(weight.shape, BF16),
            pltpu.VMEM(pw.shape, BF16),
            pltpu.VMEM(field.shape, BF16),
            pltpu.VMEM(weight.shape, BF16),
            pltpu.VMEM((4, kk * XL, 128), F32),
            pltpu.VMEM((XL, cells, NZ), F32),
            pltpu.VMEM((4, kk * XL, 128), F32),
            pltpu.VMEM(field.shape, BF16),
            pltpu.VMEM((2, KL, modes, 128), BF16),
            pltpu.VMEM((modes, 128), F32),
            pltpu.VMEM((modes, 1024), BF16),
            pltpu.VMEM((2, 2 * ky, 128), BF16),
            pltpu.VMEM((narrow * 2 * YL, 128), F32),
            pltpu.VMEM((narrow * YL, 128), F32),
            pltpu.VMEM((KXL * narrow * 2, cells), BF16),
            pltpu.VMEM((cells, cells), BF16),
            pltpu.VMEM((cells, cells), BF16),
            pltpu.VMEM((cells, cells), BF16),
            pltpu.VMEM((cells, cells), BF16),
            pltpu.VMEM((128, 1024), BF16),
            pltpu.VMEM((128, 128), BF16),
            pltpu.VMEM((1024, 128), BF16),
            pltpu.VMEM((2, wide, 2, KL, 2 * XL, 256), BF16),
            pltpu.VMEM((2, wide, 2, KL, 2 * XL, 256), BF16),
            pltpu.VMEM((2, wide, KL, 2 * XL, cells), BF16),
            pltpu.VMEM((2, wide, KL, 2 * XL, cells), BF16),
            pltpu.VMEM((2, 2, KL, narrow, 3 * YL, 128), BF16),
            pltpu.VMEM((2, 2, KL, narrow, 3 * YL, 128), BF16),
            pltpu.SemaphoreType.DMA((2, 2)),
            pltpu.SemaphoreType.DMA((2, 2)),
            pltpu.SemaphoreType.DMA((2, 2)),
            pltpu.SemaphoreType.DMA((2, 2)),
            pltpu.SemaphoreType.DMA((2, 2, KL)),
            pltpu.SemaphoreType.DMA((2, 2, KL)),
            pltpu.SemaphoreType.DMA((7,)),
            pltpu.SemaphoreType.DMA((4 + KL,)),
        ],
        compiler_params=pltpu.CompilerParams(
            collective_id=0, has_side_effects=True, vmem_limit_bytes=VMEM_BYTES
        ),
        name="spectral_layer",
    )(field, cot, weight, pw, table)
    act, wgrad, fgrad = pl.pallas_call(
        functools.partial(finish, kk),
        out_shape=(grid_like, weight_like, grid_like),
        in_specs=[hbm] * 5,
        out_specs=(hbm,) * 3,
        scratch_shapes=[
            pltpu.VMEM((wide, KL, 2 * XL, cells), BF16),
            pltpu.VMEM((XL, cells, NZ), F32),
            pltpu.VMEM((kk, NZ), BF16),
            pltpu.VMEM((4, kk * XL, 128), F32),
            pltpu.VMEM(field.shape, BF16),
            pltpu.VMEM(field.shape, BF16),
            pltpu.VMEM(weight.shape, BF16),
            pltpu.SemaphoreType.DMA((21,)),
        ],
        compiler_params=pltpu.CompilerParams(vmem_limit_bytes=VMEM_BYTES),
        name="field_gradient",
    )(*parts, table)
    return act, fgrad, wgrad


def solution(mesh):
    wide, narrow = mesh.shape["wide"], mesh.shape["narrow"]
    return jax.shard_map(
        functools.partial(on_device, wide, narrow),
        mesh=mesh,
        in_specs=(
            P(None, "wide", "narrow", None),
            P("wide", "narrow", None, None),
            P(),
            P(None, "wide", "narrow", None),
        ),
        out_specs=(
            P(None, "wide", "narrow", None),
            P(None, "wide", "narrow", None),
            P("wide", "narrow", None, None),
        ),
        check_vma=False,
    )
```
